32 devices in a mesh: fsdp: 16 (over z, y, x), rep: 2 (over core).
Axes of the slice: x: 2, y: 2, z: 4, core: 2. Of those that a mesh axis runs over, the one named last changes fastest.
Arguments:
- tokens: bfloat16 [16, 256, 2048], P('fsdp', 'rep'), may hold values from -6 to 6
- segments: int32 [16, 256], P('fsdp'), may hold values from 0 to 1, never falling along the last dimension, each value on 1 to 192 neighbouring positions
- cotangent: bfloat16 [16, 256, 2048], P('fsdp', 'rep'), may hold values from -6 to 6
- w_query: bfloat16 [1, 2048, 2048], P(None, 'fsdp'), may hold values from -0.125 to 0.125
- w_key: bfloat16 [1, 2048, 1024], P(None, 'fsdp'), may hold values from -0.125 to 0.125
- w_value: bfloat16 [1, 2048, 1024], P(None, 'fsdp'), may hold values from -0.125 to 0.125
- w_output: bfloat16 [1, 2048, 2048], P(None, 'fsdp'), may hold values from -0.375 to 0.375
- w_gate: bfloat16 [1, 2048, 6144], P(None, 'fsdp'), may hold values from -0.125 to 0.125
- w_up: bfloat16 [1, 2048, 6144], P(None, 'fsdp'), may hold values from -0.125 to 0.125
- w_down: bfloat16 [1, 6144, 2048], P(None, 'fsdp'), may hold values from -0.078125 to 0.078125
- gain_in: float32 [1, 2048], replicated, may hold values from 0.25 to 1.75
- gain_query: float32 [1, 128], replicated, may hold values from 0.25 to 1.75
- gain_key: float32 [1, 128], replicated, may hold values from 0.25 to 1.75
- gain_post: float32 [1, 2048], replicated, may hold values from 0.25 to 1.75
Outputs:
- activations: bfloat16 [16, 256, 2048], P('fsdp', 'rep')
- d_tokens: bfloat16 [16, 256, 2048], P('fsdp', 'rep')
- grad_query: float32 [1, 2048, 2048], P(None, 'fsdp')
- grad_key: float32 [1, 2048, 1024], P(None, 'fsdp')
- grad_value: float32 [1, 2048, 1024], P(None, 'fsdp')
- grad_output: float32 [1, 2048, 2048], P(None, 'fsdp')
- grad_gate: float32 [1, 2048, 6144], P(None, 'fsdp')
- grad_up: float32 [1, 2048, 6144], P(None, 'fsdp')
- grad_down: float32 [1, 6144, 2048], P(None, 'fsdp')
- grad_gain_in: float32 [1, 2048], replicated
- grad_gain_query: float32 [1, 128], replicated
- grad_gain_key: float32 [1, 128], replicated
- grad_gain_post: float32 [1, 2048], replicated
The draws below stay inside these ranges and needn't reach their ends.
Inputs may be any that keep to these rules, and one draw needn't show every extreme that they name: `segments`: segment numbers never fall along a sequence; each sequence holds 2 documents of 1 to 192 tokens.
All inputs are finite; a program needn't handle non-finite values.
Results may differ from the reference program's by a relative error of at most 0.015.
Values may be sent and summed in bfloat16 or wider, within the bound.
No kernel may reach another device: no remote copies, remote signals or barrier semaphores. Data moves between devices by JAX's collectives and lax.ppermute only.
A program may use at most 512 MiB of HBM per device.

```python
import functools
import math
import jax
import jax.numpy as jnp
import numpy as np
from jax import lax

D = 2048
FF = 6144
HD = 128
LAYERS = 1
LEN = 256
DOCS = 2
DOC_MOST = 192
NSEQ = 16
QW = 2048
KVW = 1024


def levels(stream_key, dims, split, smallest, largest):
    loudness, own = 1.0, jax.random.fold_in(stream_key, 6)
    for dim, parts in split:
        steps = jnp.exp(jax.random.uniform(jax.random.fold_in(own, dim), (parts,), jnp.float32, smallest / len(split), largest / len(split)))
        loudness = loudness * jnp.repeat(steps, dims[dim] // parts).reshape([-1 if axis == dim else 1 for axis in range(len(dims))])
    return loudness


def length_profile(count, total, bound, slope):
    portions = [(1 << 20) // math.isqrt(grade ** slope) + 1 for grade in range(2, count + 1)]
    surplus, holding = total - bound - (count - 1), [1] * (count - 1)
    while surplus > 0:
        free = [i for i in range(count - 1) if holding[i] < bound]
        whole, remaining = sum([portions[i] for i in free]), surplus
        for i in free:
            extra = min(bound - holding[i], max(1, remaining * portions[i] // whole), surplus)
            holding[i] = holding[i] + extra
            surplus = surplus - extra
    return np.array([bound] + holding)


def ragged(key, amount, total, most, lean):
    if amount == 2:
        one = jax.random.randint(key, (), max(1, total - most), min(most, total - 1) + 1)
        return jnp.stack([one, total - one])
    sizes = jnp.asarray(length_profile(amount, total, most, lean), jnp.int32)
    pairs = (amount - 1) // 2
    source_of, taker = sizes[1:1 + 2 * pairs:2], sizes[2:2 + 2 * pairs:2]
    margin = jnp.minimum(source_of - 1, most - taker)
    passed = jax.random.randint(jax.random.fold_in(key, 1), (pairs,), 0, 1 << 20) % (margin + 1)
    sizes = sizes.at[1:1 + 2 * pairs:2].set(source_of - passed).at[2:2 + 2 * pairs:2].set(taker + passed)
    return sizes[jax.random.permutation(jax.random.fold_in(key, 2), amount)]


def centred(stream_key, extent, scale, reach, split=(), kind=jnp.bfloat16):
    entries = jax.random.normal(stream_key, extent, jnp.float32) * scale
    if len(split) > 0:
        entries = levels(stream_key, extent, split, -0.22, 0.18) * entries
    return jnp.clip(entries, min=-reach, max=reach).astype(kind)


def setup_inputs(seed: int = 0) -> dict:
    key_of = jax.random.split(jax.random.key(seed), 15)
    tokens = centred(key_of[0], (NSEQ, LEN, D), 1.0, 6.0, ((0, 16), (1, 2)))
    segments = jax.vmap(lambda own: jnp.searchsorted(jnp.cumsum(ragged(own, DOCS, LEN, DOC_MOST, 0)), jnp.arange(LEN), side="right"))(jax.random.split(key_of[1], NSEQ)).reshape((NSEQ, LEN)).astype(jnp.int32)
    cotangent = centred(key_of[2], (NSEQ, LEN, D), 1.0, 6.0, ((0, 16), (1, 2)))
    w_query = centred(key_of[3], (LAYERS, D, QW), D ** -0.5, 0.125, ((1, 16),))
    w_key = centred(key_of[4], (LAYERS, D, KVW), D ** -0.5, 0.125, ((1, 16),))
    w_value = centred(key_of[5], (LAYERS, D, KVW), D ** -0.5, 0.125, ((1, 16),))
    w_output = centred(key_of[6], (LAYERS, QW, D), (QW // 8) ** -0.5, 0.375, ((1, 16),))
    w_gate = centred(key_of[7], (LAYERS, D, FF), D ** -0.5, 0.125, ((1, 16),))
    w_up = centred(key_of[8], (LAYERS, D, FF), D ** -0.5, 0.125, ((1, 16),))
    w_down = centred(key_of[9], (LAYERS, FF, D), FF ** -0.5, 0.078125, ((1, 16),))
    gain_in = jnp.clip(1.0 + 0.15 * jax.random.normal(key_of[10], (LAYERS, D), jnp.float32), 0.25, 1.75)
    gain_query = jnp.clip(1.0 + 0.15 * jax.random.normal(key_of[11], (LAYERS, HD), jnp.float32), 0.25, 1.75)
    gain_key = jnp.clip(1.0 + 0.15 * jax.random.normal(key_of[12], (LAYERS, HD), jnp.float32), 0.25, 1.75)
    gain_post = jnp.clip(1.0 + 0.15 * jax.random.normal(key_of[13], (LAYERS, D), jnp.float32), 0.25, 1.75)
    return dict(tokens=tokens, segments=segments, cotangent=cotangent, w_query=w_query, w_key=w_key, w_value=w_value, w_output=w_output, w_gate=w_gate, w_up=w_up, w_down=w_down, gain_in=gain_in, gain_query=gain_query, gain_key=gain_key, gain_post=gain_post)


NORM_EPS = 1e-06
NEG_FILL = -1e+30
ROPE_BASE = 1000000.0

def contract(form, left_arr, right_arr):
    return jnp.einsum(form, left_arr.astype(jnp.float32), right_arr.astype(jnp.float32))

def rms_scale(in_value, gain_vec):
    return in_value * lax.rsqrt(lax.optimization_barrier(jnp.mean(in_value * in_value, axis=-1, keepdims=True)) + NORM_EPS) * gain_vec

def head_prep(raw_heads, gain_vec, cosines, sines):
    normed = rms_scale(raw_heads, gain_vec)
    half_width = normed.shape[-1] // 2
    turned = jnp.concatenate([-normed[..., half_width:], normed[..., :half_width]], axis=-1)
    return normed * cosines + turned * sines

def layout(segments):
    seq_count, seq_len = segments.shape
    position_index = lax.broadcasted_iota(jnp.int32, (seq_count, seq_len), 1)
    prev_segment = jnp.concatenate([segments[:, :1] - 1, segments[:, :-1]], axis=1)
    doc_start = lax.cummax(jnp.where(segments != prev_segment, position_index, 0), axis=1)
    position = (position_index - doc_start).astype(jnp.float32)
    inv_freq = jnp.exp(jnp.arange(HD // 2, dtype=jnp.float32) * (-2.0 * math.log(ROPE_BASE) / HD))
    rotation = position[:, :, None] * inv_freq
    rotation = jnp.concatenate([rotation, rotation], axis=-1)[:, :, None, :]
    causal = position_index[:, None, :] <= position_index[:, :, None]
    doc_match = segments[:, :, None] == segments[:, None, :]
    same_doc = (causal & doc_match)[:, None, None, :, :]
    return (same_doc, jnp.cos(rotation), jnp.sin(rotation))

def attention_scores(queries, key_heads, same_doc):
    seq_count, seq_len, head_count, head_width = queries.shape
    kv_groups = key_heads.shape[2]
    grouped = queries.reshape(seq_count, seq_len, kv_groups, head_count // kv_groups, head_width)
    raw_scores = contract('sqgrd,skgd->sgrqk', grouped, key_heads) * (1.0 / math.sqrt(head_width))
    return jnp.where(same_doc, raw_scores, NEG_FILL)

def layer_forward(resid_in, attn_w, mlp_w, gain_set, same_doc, cosines, sines):
    w_q, w_k, w_v, w_o = attn_w
    w_g, w_u, w_d = mlp_w
    g_in, g_q, g_k, g_post = gain_set
    seq_count, seq_len, model_width = resid_in.shape
    row_count = seq_count * seq_len
    head_count = w_q.shape[1] // HD
    kv_heads = w_k.shape[1] // HD
    normed = rms_scale(resid_in, g_in).astype(jnp.bfloat16).reshape(row_count, model_width)
    q_raw = jnp.dot(normed, w_q, preferred_element_type=jnp.float32).reshape(seq_count, seq_len, head_count, HD)
    k_raw = jnp.dot(normed, w_k, preferred_element_type=jnp.float32).reshape(seq_count, seq_len, kv_heads, HD)
    values = jnp.dot(normed, w_v, preferred_element_type=jnp.float32).astype(jnp.bfloat16).reshape(seq_count, seq_len, kv_heads, HD)
    queries = head_prep(q_raw, g_q, cosines, sines).astype(jnp.bfloat16)
    key_heads = head_prep(k_raw, g_k, cosines, sines).astype(jnp.bfloat16)
    scores = attention_scores(queries, key_heads, same_doc)
    row_top = lax.optimization_barrier(jnp.max(scores, axis=-1, keepdims=True))
    expo_terms = jnp.exp(scores - row_top)
    row_total = lax.optimization_barrier(jnp.sum(expo_terms, axis=-1, keepdims=True))
    log_total = row_top + jnp.log(row_total)
    prob_rows = (expo_terms / row_total).astype(jnp.bfloat16)
    mixed_heads = contract('sgrqk,skgd->sqgrd', prob_rows, values).astype(jnp.bfloat16).reshape(row_count, head_count * HD)
    middle = resid_in + jnp.dot(mixed_heads, w_o, preferred_element_type=jnp.float32).reshape(seq_count, seq_len, model_width)
    normed_two = rms_scale(middle, g_post).astype(jnp.bfloat16).reshape(row_count, model_width)
    gate_proj = jnp.dot(normed_two, w_g, preferred_element_type=jnp.float32)
    up_proj = jnp.dot(normed_two, w_u, preferred_element_type=jnp.float32)
    hidden = (jax.nn.silu(gate_proj) * up_proj).astype(jnp.bfloat16)
    layer_out = middle + jnp.dot(hidden, w_d, preferred_element_type=jnp.float32).reshape(seq_count, seq_len, model_width)
    saved_state = (resid_in, normed, q_raw, k_raw, queries, key_heads, values, log_total, mixed_heads, middle, normed_two, gate_proj, up_proj, hidden)
    return (layer_out, saved_state)

def layer_backward(d_out, saved_state, attn_w, mlp_w, gain_set, same_doc, cosines, sines):
    w_q, w_k, w_v, w_o = attn_w
    w_g, w_u, w_d = mlp_w
    g_in, g_q, g_k, g_post = gain_set
    resid_in, normed, q_raw, k_raw, queries, key_heads, values, log_total, mixed_heads, middle, normed_two, gate_proj, up_proj, hidden = saved_state
    seq_count, seq_len, model_width = resid_in.shape
    row_count = seq_count * seq_len
    head_count = w_q.shape[1] // HD
    kv_heads = w_k.shape[1] // HD
    d_rows = d_out.astype(jnp.bfloat16).reshape(row_count, model_width)
    grad_down = jnp.dot(hidden.T, d_rows, preferred_element_type=jnp.float32)
    d_hidden = jnp.dot(d_rows, w_d.T, preferred_element_type=jnp.float32)
    gate_sigmoid = jax.nn.sigmoid(gate_proj)
    d_upper = (d_hidden * gate_proj * gate_sigmoid).astype(jnp.bfloat16)
    d_gate = (d_hidden * up_proj * gate_sigmoid * (1.0 + gate_proj * (1.0 - gate_sigmoid))).astype(jnp.bfloat16)
    grad_gate = jnp.dot(normed_two.T, d_gate, preferred_element_type=jnp.float32)
    grad_up = jnp.dot(normed_two.T, d_upper, preferred_element_type=jnp.float32)
    d_normed_two = jnp.dot(d_gate, w_g.T, preferred_element_type=jnp.float32) + jnp.dot(d_upper, w_u.T, preferred_element_type=jnp.float32)
    _, post_back = jax.vjp(rms_scale, middle, g_post)
    d_post, grad_post = post_back(d_normed_two.reshape(seq_count, seq_len, model_width))
    d_middle = d_out + d_post
    d_mid_rows = d_middle.astype(jnp.bfloat16).reshape(row_count, model_width)
    grad_out = jnp.dot(mixed_heads.T, d_mid_rows, preferred_element_type=jnp.float32)
    d_mixed = jnp.dot(d_mid_rows, w_o.T, preferred_element_type=jnp.float32).astype(jnp.bfloat16)
    d_mixed = d_mixed.reshape(seq_count, seq_len, kv_heads, head_count // kv_heads, HD)
    probs_full = jnp.exp(attention_scores(queries, key_heads, same_doc) - log_total)
    prob_rows = probs_full.astype(jnp.bfloat16)
    d_values = contract('sgrqk,sqgrd->skgd', prob_rows, d_mixed)
    d_probs = contract('sqgrd,skgd->sgrqk', d_mixed, values)
    d_scores = (probs_full * (d_probs - lax.optimization_barrier(jnp.sum(probs_full * d_probs, axis=-1, keepdims=True))) * (1.0 / math.sqrt(HD))).astype(jnp.bfloat16)
    d_queries = contract('sgrqk,skgd->sqgrd', d_scores, key_heads).reshape(seq_count, seq_len, head_count, HD)
    grouped = queries.reshape(seq_count, seq_len, kv_heads, head_count // kv_heads, HD)
    d_keys = contract('sgrqk,sqgrd->skgd', d_scores, grouped)
    _, q_back = jax.vjp(functools.partial(head_prep, cosines=cosines, sines=sines), q_raw, g_q)
    d_q_raw, grad_qgain = q_back(d_queries)
    _, k_back = jax.vjp(functools.partial(head_prep, cosines=cosines, sines=sines), k_raw, g_k)
    d_k_raw, grad_kgain = k_back(d_keys)
    d_query_rows = d_q_raw.astype(jnp.bfloat16).reshape(row_count, head_count * HD)
    d_key_rows = d_k_raw.astype(jnp.bfloat16).reshape(row_count, kv_heads * HD)
    d_value_rows = d_values.astype(jnp.bfloat16).reshape(row_count, kv_heads * HD)
    grad_query = jnp.dot(normed.T, d_query_rows, preferred_element_type=jnp.float32)
    grad_key = jnp.dot(normed.T, d_key_rows, preferred_element_type=jnp.float32)
    grad_value = jnp.dot(normed.T, d_value_rows, preferred_element_type=jnp.float32)
    d_normed = jnp.dot(d_query_rows, w_q.T, preferred_element_type=jnp.float32) + jnp.dot(d_key_rows, w_k.T, preferred_element_type=jnp.float32) + jnp.dot(d_value_rows, w_v.T, preferred_element_type=jnp.float32)
    _, in_back = jax.vjp(rms_scale, resid_in, g_in)
    d_resid, grad_in = in_back(d_normed.reshape(seq_count, seq_len, model_width))
    return (d_middle + d_resid, (grad_query, grad_key, grad_value, grad_out), (grad_gate, grad_up, grad_down), (grad_in, grad_qgain, grad_kgain, grad_post))

def reference(tokens, segments, cotangent, w_query, w_key, w_value, w_output, w_gate, w_up, w_down, gain_in, gain_query, gain_key, gain_post):
    block_seqs = min(16, NSEQ)
    block_count = NSEQ // block_seqs
    tok_blocks = tokens.reshape(block_count, block_seqs, LEN, D)
    seg_blocks = segments.reshape(block_count, block_seqs, LEN)
    cot_blocks = cotangent.reshape(block_count, block_seqs, LEN, D)
    weight_list = (w_query, w_key, w_value, w_output, w_gate, w_up, w_down, gain_in, gain_query, gain_key, gain_post)
    start_sums = tuple((jnp.zeros(wt.shape, jnp.float32) for wt in weight_list))

    def block_step(grad_sums, block_item):
        tok_block, seg_block, cot_block = block_item
        same_doc, cosines, sines = layout(seg_block)
        resid = tok_block.astype(jnp.float32)
        saved_list = []
        for layer_idx in range(LAYERS):
            resid, saved_state = layer_forward(resid, (w_query[layer_idx], w_key[layer_idx], w_value[layer_idx], w_output[layer_idx]), (w_gate[layer_idx], w_up[layer_idx], w_down[layer_idx]), (gain_in[layer_idx], gain_query[layer_idx], gain_key[layer_idx], gain_post[layer_idx]), same_doc, cosines, sines)
            saved_list.append(saved_state)
        d_resid = cot_block.astype(jnp.float32)
        layer_grads = [None] * LAYERS
        for layer_idx in reversed(range(LAYERS)):
            d_resid, attn_grads, mlp_grads, gain_grads = layer_backward(d_resid, saved_list[layer_idx], (w_query[layer_idx], w_key[layer_idx], w_value[layer_idx], w_output[layer_idx]), (w_gate[layer_idx], w_up[layer_idx], w_down[layer_idx]), (gain_in[layer_idx], gain_query[layer_idx], gain_key[layer_idx], gain_post[layer_idx]), same_doc, cosines, sines)
            layer_grads[layer_idx] = attn_grads + mlp_grads + gain_grads
        stacked = tuple((jnp.stack([layer_grads[layer_idx][entry] for layer_idx in range(LAYERS)]) for entry in range(11)))
        new_sums = tuple((prior_sum + block_sum for prior_sum, block_sum in zip(grad_sums, stacked)))
        return (new_sums, (resid.astype(jnp.bfloat16), d_resid.astype(jnp.bfloat16)))
    grad_sums, (out_blocks, d_blocks) = lax.scan(block_step, start_sums, (tok_blocks, seg_blocks, cot_blocks))
    activations = out_blocks.reshape(NSEQ, LEN, D)
    d_tokens = d_blocks.reshape(NSEQ, LEN, D)
    return (activations, d_tokens, grad_sums[0], grad_sums[1], grad_sums[2], grad_sums[3], grad_sums[4], grad_sums[5], grad_sums[6], grad_sums[7], grad_sums[8], grad_sums[9], grad_sums[10])
```

```python
import functools
import math

import jax
import jax.numpy as jnp
from jax import lax
from jax.sharding import PartitionSpec as P

HD = 128
NORM_EPS = 1e-06
NEG_FILL = -1e30
ROPE_BASE = 1000000.0
BF16 = jnp.bfloat16
F32 = jnp.float32


def dot(x, y):
    return jnp.dot(x, y, preferred_element_type=F32)


def dot_tn(x, y):
    return lax.dot_general(x, y, (((0,), (0,)), ((), ())), preferred_element_type=F32)


def dot_nt(x, y):
    return lax.dot_general(x, y, (((1,), (1,)), ((), ())), preferred_element_type=F32)


def contract(form, x, y):
    return jnp.einsum(form, x, y, preferred_element_type=F32)


def rms_scale(v, gain):
    return v * lax.rsqrt(jnp.mean(v * v, axis=-1, keepdims=True) + NORM_EPS) * gain


def head_prep(raw, gain, cosines, sines):
    normed = rms_scale(raw, gain)
    half = normed.shape[-1] // 2
    turned = jnp.concatenate([-normed[..., half:], normed[..., :half]], axis=-1)
    return normed * cosines + turned * sines


class Grid:
    def __init__(self, mesh):
        n = mesh.shape["fsdp"]
        assert mesh.shape["rep"] == 2 and n % 16 == 0 and n & (n - 1) == 0
        self.n = n
        self.F = n // 4
        self.B = 2 ** (int(math.log2(self.F)) // 2)
        self.A = self.F // self.B
        self.Q = self.F // 4
        self.tmask, self.umask = 2 * self.B, 1

    def place(self):
        i = lax.axis_index("fsdp")
        self.u = i % 2
        self.b = (i // 2) % self.B
        self.t = (i // (2 * self.B)) % 2
        self.a = i // (4 * self.B)
        self.c = lax.axis_index("rep")

    def px(self, x, mask):
        return lax.ppermute(x, "fsdp", [(i, i ^ mask) for i in range(self.n)])

    def pc(self, x):
        return lax.ppermute(x, "rep", [(0, 1), (1, 0)])

    def pa(self, x, delta):
        return self.px(x, 4 * self.B * delta)

    def pb(self, x, delta):
        return self.px(x, 2 * delta)

    def pt(self, x, dt, du):
        return self.px(x, dt * self.tmask + du * self.umask)

    def kv_head(self, t, u, c, rows):
        first = (u * 2 + c) * self.Q
        block = ((first // self.B * 2 + t) * self.B + first % self.B) * 2
        return block * rows // (2 * HD)

    def hidden_blocks(self, t, u, c):
        half = self.B // 2
        return [
            ((a * 2 + t) * self.B + c * half + b) * 2 + u
            for a in range(self.A)
            for b in range(half)
        ]


SHIFTS = ((1, 1), (0, 1), (1, 0))


def pick(x, *index):
    lead = len(index)
    starts = list(index) + [0] * (x.ndim - lead)
    sizes = [1] * lead + list(x.shape[lead:])
    return lax.dynamic_slice(x, starts, sizes).reshape(x.shape[lead:])


def put(x, piece, *index):
    lead = len(index)
    starts = list(index) + [0] * (x.ndim - lead)
    return lax.dynamic_update_slice(x, piece.reshape((1,) * lead + x.shape[lead:]), starts)


def swap_halves(g, own, other):
    return jnp.where(g.c == 0, jnp.stack([own, other]), jnp.stack([other, own]))


def tokens_gather(g, x):
    out = jnp.zeros((2, 2, 2) + x.shape, x.dtype)
    near = {(0, 0): x}
    for dt, du in SHIFTS:
        near[dt, du] = g.pt(x, dt, du)
    for (dt, du), mine in near.items():
        theirs = g.pc(mine)
        out = put(out, mine, g.t ^ dt, g.u ^ du, g.c)
        out = put(out, theirs, g.t ^ dt, g.u ^ du, 1 - g.c)
    return out


def tokens_scatter(g, partial):
    total = None
    got = []
    for dt, du in SHIFTS + ((0, 0),):
        tt, uu = g.t ^ dt, g.u ^ du
        theirs = g.pc(pick(partial, tt, uu, 1 - g.c).astype(BF16))
        both = pick(partial, tt, uu, g.c) + theirs.astype(F32)
        if (dt, du) == (0, 0):
            total = both
        else:
            got.append(g.pt(both.astype(BF16), dt, du))
    for piece in got:
        total = total + piece.astype(F32)
    return total


def shards_gather(g, x):
    out = jnp.zeros((g.A, g.B) + x.shape, x.dtype)
    held = {0: x}
    for d in range(1, g.A):
        held[d] = g.pa(x, d)
    for d, block in held.items():
        out = put(out, block, g.a ^ d, g.b)
        for e in range(1, g.B):
            out = put(out, g.pb(block, e), g.a ^ d, g.b ^ e)
    return out


def shards_scatter(g, x):
    over_b = [pick(x, d, g.b).astype(F32) for d in range(g.A)]
    rows = jnp.stack(over_b)
    for e in range(1, g.B):
        sent = jnp.stack([pick(x, d, g.b ^ e) for d in range(g.A)]).astype(BF16)
        rows = rows + g.pb(sent, e).astype(F32)
    total = pick(rows, g.a)
    for d in range(1, g.A):
        total = total + g.pa(pick(rows, g.a ^ d).astype(BF16), d).astype(F32)
    return total


def columns_fetch(g, slices):
    own = slices(g.t, g.u)
    block = put(jnp.zeros((2, 2) + own.shape, own.dtype), own, g.t, g.u)
    for dt, du in SHIFTS:
        block = put(block, g.pt(slices(g.t ^ dt, g.u ^ du), dt, du), g.t ^ dt, g.u ^ du)
    whole = shards_gather(g, block)
    return whole.transpose(0, 2, 1, 3, 4, 5).reshape(-1, own.shape[1])


def columns_return(g, grad, rows):
    parts = grad.reshape(g.A, 2, g.B, 2, rows, -1).transpose(0, 2, 1, 3, 4, 5)
    mine = shards_scatter(g, parts).astype(BF16)
    out = {}
    for dt, du in SHIFTS + ((0, 0),):
        piece = pick(mine, g.t ^ dt, g.u ^ du)
        if (dt, du) != (0, 0):
            piece = g.pt(piece, dt, du)
        out[dt, du] = (piece, g.pc(piece))
    return out


def per_device(
    g,
    tokens,
    segments,
    cotangent,
    w_query,
    w_key,
    w_value,
    w_output,
    w_gate,
    w_up,
    w_down,
    gain_in,
    gain_query,
    gain_key,
    gain_post,
):
    g.place()
    A, B, Q = g.A, g.B, g.Q
    _, span, width = tokens.shape
    seq_len = segments.shape[1]
    w_q, w_k, w_v, w_o, w_g, w_u, w_d = (
        w[0] for w in (w_query, w_key, w_value, w_output, w_gate, w_up, w_down)
    )
    rows_in, rows_o, rows_d = w_q.shape[0], w_o.shape[0], w_d.shape[0]
    q_width, kv_width, hidden_width = w_q.shape[1], w_k.shape[1], w_g.shape[1]
    g_in, g_q, g_k, g_post = gain_in[0], gain_query[0], gain_key[0], gain_post[0]

    x_own = tokens[0].astype(F32)
    d_out = cotangent[0].astype(F32)

    def attn_slice(t, u):
        kv = g.kv_head(t, u, g.c, rows_o)
        return jnp.concatenate(
            [
                lax.dynamic_slice(w_q, (0, kv * 2 * HD), (rows_in, 2 * HD)),
                lax.dynamic_slice(w_k, (0, kv * HD), (rows_in, HD)),
                lax.dynamic_slice(w_v, (0, kv * HD), (rows_in, HD)),
            ],
            axis=1,
        )

    w_qkv = columns_fetch(g, attn_slice)

    xn_own = rms_scale(x_own, g_in).astype(BF16)
    xn = tokens_gather(g, xn_own).reshape(4 * seq_len, width)

    seg_all = put(jnp.zeros((2, 2, seq_len), segments.dtype), segments[0], g.t, g.u)
    for dt, du in SHIFTS:
        seg_all = put(seg_all, g.pt(segments[0], dt, du), g.t ^ dt, g.u ^ du)
    seg_all = seg_all.reshape(4, seq_len)
    index = lax.broadcasted_iota(jnp.int32, (4, seq_len), 1)
    earlier = seg_all[:, None, :] < seg_all[:, :, None]
    doc_start = jnp.sum(earlier.astype(jnp.int32), axis=-1)
    pos = (index - doc_start).astype(F32)
    inv_freq = jnp.exp(jnp.arange(HD // 2, dtype=F32) * (-2.0 * math.log(ROPE_BASE) / HD))
    rotation = pos[:, :, None] * inv_freq
    rotation = jnp.concatenate([rotation, rotation], axis=-1)[:, :, None, :]
    cosines, sines = jnp.cos(rotation), jnp.sin(rotation)
    same_doc = (index[:, None, :] <= index[:, :, None]) & (
        seg_all[:, :, None] == seg_all[:, None, :]
    )
    same_doc = same_doc[:, None]

    half_o = lax.dynamic_slice(w_o, (g.c * (rows_o // 2), 0), (rows_o // 2, width))
    o_blocks = shards_gather(g, half_o).reshape(2, 2, Q, rows_o // 2, width)
    o_mine = pick(o_blocks, g.u)
    o_next = g.px(pick(o_blocks, 1 - g.u), g.umask)
    o_pair = jnp.where(g.u == 0, jnp.stack([o_mine, o_next]), jnp.stack([o_next, o_mine]))
    o_pair = o_pair.transpose(1, 2, 0, 3, 4)
    o_other = g.pc(pick(o_pair, 1 - g.c))
    w_o_all = swap_halves(g, pick(o_pair, g.c), o_other)
    w_o_all = w_o_all.transpose(1, 2, 0, 3, 4).reshape(-1, width)

    qkv = dot(xn, w_qkv)
    q_raw = qkv[:, : 2 * HD].reshape(4, seq_len, 2, HD)
    k_raw = qkv[:, 2 * HD : 3 * HD].reshape(4, seq_len, 1, HD)
    vals = qkv[:, 3 * HD :].astype(BF16).reshape(4, seq_len, HD)
    queries, q_back = jax.vjp(
        functools.partial(head_prep, cosines=cosines, sines=sines), q_raw, g_q
    )
    keys, k_back = jax.vjp(functools.partial(head_prep, cosines=cosines, sines=sines), k_raw, g_k)
    queries = queries.astype(BF16)
    keys = keys.astype(BF16).reshape(4, seq_len, HD)
    scale = 1.0 / math.sqrt(HD)
    scores = jnp.where(same_doc, contract("sqrd,skd->srqk", queries, keys) * scale, NEG_FILL)
    top = jnp.max(scores, axis=-1, keepdims=True)
    expo = jnp.exp(scores - top)
    probs = expo / jnp.sum(expo, axis=-1, keepdims=True)
    probs_low = probs.astype(BF16)
    att = contract("srqk,skd->sqrd", probs_low, vals).astype(BF16).reshape(4 * seq_len, 2 * HD)
    att_part = dot(att, w_o_all).reshape(2, 2, 2, span, width)
    mid = x_own + tokens_scatter(g, att_part)
    xn2_own, post_back = jax.vjp(rms_scale, mid, g_post)
    xn2_own = xn2_own.astype(BF16)
    xn2 = tokens_gather(g, xn2_own).reshape(4 * seq_len, width)

    def hidden_slice(w):
        def take(t, u):
            return jnp.concatenate(
                [
                    lax.dynamic_slice(w, (0, i * rows_d), (rows_in, rows_d))
                    for i in g.hidden_blocks(t, u, g.c)
                ],
                axis=1,
            )

        return take

    half_d = lax.dynamic_slice(w_d, (g.c * (rows_d // 2), 0), (rows_d // 2, width))
    d_blocks = shards_gather(g, half_d).reshape(A, 2, B // 2, rows_d // 2, width)
    d_blocks = d_blocks.transpose(1, 0, 2, 3, 4)
    d_other = g.pc(pick(d_blocks, 1 - g.c))
    w_d_all = swap_halves(g, pick(d_blocks, g.c), d_other)
    w_d_all = w_d_all.transpose(1, 2, 0, 3, 4).reshape(-1, width)
    w_g_all = columns_fetch(g, hidden_slice(w_g))
    w_u_all = columns_fetch(g, hidden_slice(w_u))

    dob = tokens_gather(g, cotangent[0]).reshape(4 * seq_len, width)

    d_hidden = dot_nt(dob, w_d_all)
    gate = dot(xn2, w_g_all)
    up = dot(xn2, w_u_all)
    sig = jax.nn.sigmoid(gate)
    hidden = (gate * sig * up).astype(BF16)
    d_up = (d_hidden * gate * sig).astype(BF16)
    d_gate = (d_hidden * up * sig * (1.0 + gate * (1.0 - sig))).astype(BF16)
    d_xn2 = dot_nt(d_gate, w_g_all) + dot_nt(d_up, w_u_all)
    d_xn2 = tokens_scatter(g, d_xn2.reshape(2, 2, 2, span, width))
    d_post, grad_post = post_back(d_xn2)
    d_mid = d_out + d_post
    dmb = tokens_gather(g, d_mid.astype(BF16)).reshape(4 * seq_len, width)
    out_part = dot(hidden, w_d_all).reshape(2, 2, 2, span, width)
    activations = (mid + tokens_scatter(g, out_part)).astype(BF16)

    grad_g = columns_return(g, dot_tn(xn2, d_gate), rows_in)
    grad_u = columns_return(g, dot_tn(xn2, d_up), rows_in)

    def down_return(grad):
        grad = grad.reshape(A, B // 2, 2, rows_d // 2, width)
        mine = pick(grad.transpose(2, 0, 1, 3, 4), g.c).astype(BF16)
        other = g.pc(pick(grad.transpose(2, 0, 1, 3, 4), 1 - g.c).astype(BF16))
        both = swap_halves(g, mine, other)
        both = both.transpose(1, 0, 2, 3, 4).reshape(A, B, rows_d // 2, width)
        half = shards_scatter(g, both).astype(BF16)
        return swap_halves(g, half, g.pc(half)).reshape(1, rows_d, width).astype(F32)

    grad_down = down_return(dot_tn(hidden, dob))

    d_att = dot_nt(dmb, w_o_all).astype(BF16).reshape(4, seq_len, 2, HD)
    d_vals = contract("srqk,sqrd->skd", probs_low, d_att)
    d_probs = contract("sqrd,skd->srqk", d_att, vals)
    d_scores = (
        probs * (d_probs - jnp.sum(probs * d_probs, axis=-1, keepdims=True)) * scale
    ).astype(BF16)
    d_queries = contract("srqk,skd->sqrd", d_scores, keys)
    d_keys = contract("srqk,sqrd->skd", d_scores, queries)
    d_q_raw, grad_qgain = q_back(d_queries)
    d_k_raw, grad_kgain = k_back(d_keys.reshape(4, seq_len, 1, HD))
    d_qkv = jnp.concatenate(
        [
            d_q_raw.astype(BF16).reshape(4 * seq_len, 2 * HD),
            d_k_raw.astype(BF16).reshape(4 * seq_len, HD),
            d_vals.astype(BF16).reshape(4 * seq_len, HD),
        ],
        axis=1,
    )
    d_xn = tokens_scatter(g, dot_nt(d_qkv, w_qkv).reshape(2, 2, 2, span, width))
    _, in_back = jax.vjp(rms_scale, x_own, g_in)
    d_x, grad_in = in_back(d_xn)
    d_tokens = (d_mid + d_x).astype(BF16)

    def output_return(grad):
        grad = grad.reshape(Q, 2, rows_o, width).transpose(1, 0, 2, 3)
        mine = pick(grad, g.u).astype(BF16)
        other = g.px(pick(grad, 1 - g.u).astype(BF16), g.umask)
        both = jnp.where(g.u == 0, jnp.stack([mine, other]), jnp.stack([other, mine]))
        both = both.reshape(2, Q, 2, rows_o // 2, width).transpose(2, 0, 1, 3, 4)
        swapped = swap_halves(g, pick(both, g.c), g.pc(pick(both, 1 - g.c)))
        swapped = swapped.transpose(1, 0, 2, 3, 4).reshape(A, B, rows_o // 2, width)
        half = shards_scatter(g, swapped).astype(BF16)
        return swap_halves(g, half, g.pc(half)).reshape(1, rows_o, width).astype(F32)

    grad_output = output_return(dot_tn(att, dmb))
    grad_qkv = columns_return(g, dot_tn(xn, d_qkv), rows_in)

    grad_query = jnp.zeros((rows_in, q_width), F32)
    grad_key = jnp.zeros((rows_in, kv_width), F32)
    grad_value = jnp.zeros((rows_in, kv_width), F32)
    for (dt, du), pair in grad_qkv.items():
        for k, piece in enumerate(pair):
            kv = g.kv_head(g.t ^ dt, g.u ^ du, g.c ^ k, rows_o)
            piece = piece.astype(F32)
            grad_query = lax.dynamic_update_slice(grad_query, piece[:, : 2 * HD], (0, kv * 2 * HD))
            grad_key = lax.dynamic_update_slice(
                grad_key, piece[:, 2 * HD : 3 * HD], (0, kv * HD)
            )
            grad_value = lax.dynamic_update_slice(grad_value, piece[:, 3 * HD :], (0, kv * HD))

    def hidden_place(grads):
        out = jnp.zeros((rows_in, hidden_width), F32)
        for (dt, du), pair in grads.items():
            for k, piece in enumerate(pair):
                blocks = g.hidden_blocks(g.t ^ dt, g.u ^ du, g.c ^ k)
                for j, i in enumerate(blocks):
                    part = piece[:, j * rows_d : (j + 1) * rows_d].astype(F32)
                    out = lax.dynamic_update_slice(out, part, (0, i * rows_d))
        return out[None]

    gains = jnp.concatenate([grad_in, grad_post, grad_qgain, grad_kgain])
    for bit in range(int(math.log2(g.n))):
        gains = gains + g.px(gains, 1 << bit)
    gains = (gains + g.pc(gains))[None]
    return (
        activations[None],
        d_tokens[None],
        grad_query[None],
        grad_key[None],
        grad_value[None],
        grad_output,
        hidden_place(grad_g),
        hidden_place(grad_u),
        grad_down,
        gains[:, :width],
        gains[:, 2 * width : 2 * width + HD],
        gains[:, 2 * width + HD :],
        gains[:, width : 2 * width],
    )


def solution(mesh):
    rows = P("fsdp", "rep", None)
    cut_rows = P(None, "fsdp", None)
    return jax.shard_map(
        functools.partial(per_device, Grid(mesh)),
        mesh=mesh,
        in_specs=(rows, P("fsdp", None), rows) + (cut_rows,) * 7 + (P(),) * 4,
        out_specs=(rows, rows) + (cut_rows,) * 7 + (P(),) * 4,
        check_vma=False,
    )
```

```python
import functools
import math

import jax
import jax.numpy as jnp
from jax import lax
from jax.experimental import pallas as pl
from jax.experimental.pallas import tpu as pltpu
from jax.sharding import PartitionSpec as P

HD = 128
NORM_EPS = 1e-06
NEG_FILL = -1e30
ROPE_BASE = 1000000.0
BF16 = jnp.bfloat16
F32 = jnp.float32


def dot(x, y):
    return jnp.dot(x, y, preferred_element_type=F32)


def dot_tn(x, y):
    return lax.dot_general(x, y, (((0,), (0,)), ((), ())), preferred_element_type=F32)


def dot_nt(x, y):
    return lax.dot_general(x, y, (((1,), (1,)), ((), ())), preferred_element_type=F32)


def rms_scale(v, gain):
    return v * lax.rsqrt(jnp.mean(v * v, axis=-1, keepdims=True) + NORM_EPS) * gain


class Grid:
    def __init__(self, mesh):
        n = mesh.shape["fsdp"]
        assert mesh.shape["rep"] == 2 and n % 16 == 0 and n & (n - 1) == 0
        self.n = n
        self.F = n // 4
        self.B = 2 ** (int(math.log2(self.F)) // 2)
        self.A = self.F // self.B
        self.Q = self.F // 4
        self.tmask, self.umask = 2 * self.B, 1

    def place(self):
        i = lax.axis_index("fsdp")
        self.u = i % 2
        self.b = (i // 2) % self.B
        self.t = (i // (2 * self.B)) % 2
        self.a = i // (4 * self.B)
        self.c = lax.axis_index("rep")

    def px(self, x, mask):
        return lax.ppermute(x, "fsdp", [(i, i ^ mask) for i in range(self.n)])

    def pc(self, x):
        return lax.ppermute(x, "rep", [(0, 1), (1, 0)])

    def pa(self, x, delta):
        return self.px(x, 4 * self.B * delta)

    def pb(self, x, delta):
        return self.px(x, 2 * delta)

    def pt(self, x, dt, du):
        return self.px(x, dt * self.tmask + du * self.umask)

    def kv_head(self, t, u, c, rows):
        first = (u * 2 + c) * self.Q
        block = ((first // self.B * 2 + t) * self.B + first % self.B) * 2
        return block * rows // (2 * HD)

    def hidden_blocks(self, t, u, c):
        half = self.B // 2
        return [
            ((a * 2 + t) * self.B + c * half + b) * 2 + u
            for a in range(self.A)
            for b in range(half)
        ]


SHIFTS = ((1, 1), (0, 1), (1, 0))


def pick(x, *index):
    lead = len(index)
    starts = list(index) + [0] * (x.ndim - lead)
    sizes = [1] * lead + list(x.shape[lead:])
    return lax.dynamic_slice(x, starts, sizes).reshape(x.shape[lead:])


def put(x, piece, *index):
    lead = len(index)
    starts = list(index) + [0] * (x.ndim - lead)
    return lax.dynamic_update_slice(x, piece.reshape((1,) * lead + x.shape[lead:]), starts)


def swap_halves(g, own, other):
    return jnp.where(g.c == 0, jnp.stack([own, other]), jnp.stack([other, own]))


class Live(dict):
    __getattr__ = dict.__getitem__
    __setattr__ = dict.__setitem__


ORDER = ((0, 0),) + SHIFTS
LANES = 128


def cut_columns(sources, pieces):
    rows = sources[0].shape[0]
    cuts = [cut for piece in pieces for cut in piece]
    if any(c[2] % LANES for c in cuts) or rows % 16:
        return [
            jnp.concatenate(
                [lax.dynamic_slice(sources[k], (0, at), (rows, w)) for k, at, w in piece], axis=1
            )
            for piece in pieces
        ]

    def kernel(at_ref, *refs):
        ins, outs = refs[: len(sources)], refs[len(sources) :]
        j = 0
        for out, piece in zip(outs, pieces):
            to = 0
            for k, _, w in piece:
                start = pl.multiple_of(at_ref[j] * LANES, LANES)
                out[:, to : to + w] = ins[k][:, pl.ds(start, w)]
                to += w
                j += 1

    vmem = pl.BlockSpec(memory_space=pltpu.VMEM)
    return pl.pallas_call(
        kernel,
        in_specs=[pl.BlockSpec(memory_space=pltpu.SMEM)] + [vmem] * len(sources),
        out_specs=[vmem] * len(pieces),
        out_shape=[
            jax.ShapeDtypeStruct((rows, sum(w for _, _, w in piece)), sources[0].dtype)
            for piece in pieces
        ],
        compiler_params=pltpu.CompilerParams(vmem_limit_bytes=24 << 20),
        name="cut_columns",
    )(jnp.stack([jnp.asarray(at // LANES, jnp.int32) for _, at, _ in cuts]), *sources)


def place_columns(pieces, widths, places):
    rows = pieces[0].shape[0]
    if any(p[2] % LANES or p[1] % LANES for p in places) or rows % 16:
        outs = [jnp.zeros((rows, w), F32) for w in widths]
        for k, at, w, o, to in places:
            part = pieces[k][:, at : at + w].astype(F32)
            outs[o] = lax.dynamic_update_slice(outs[o], part, (0, to))
        return outs

    def kernel(to_ref, *refs):
        ins, outs = refs[: len(pieces)], refs[len(pieces) :]
        for j, (k, at, w, o, _) in enumerate(places):
            start = pl.multiple_of(to_ref[j] * LANES, LANES)
            outs[o][:, pl.ds(start, w)] = ins[k][:, at : at + w].astype(F32)

    vmem = pl.BlockSpec(memory_space=pltpu.VMEM)
    return pl.pallas_call(
        kernel,
        in_specs=[pl.BlockSpec(memory_space=pltpu.SMEM)] + [vmem] * len(pieces),
        out_specs=[vmem] * len(widths),
        out_shape=[jax.ShapeDtypeStruct((rows, w), F32) for w in widths],
        compiler_params=pltpu.CompilerParams(vmem_limit_bytes=24 << 20),
        name="place_columns",
    )(jnp.stack([jnp.asarray(to // LANES, jnp.int32) for *_, to in places]), *pieces)


def chips_swap(g, pieces):
    return [pieces[0]] + [g.pt(x, dt, du) for x, (dt, du) in zip(pieces[1:], SHIFTS)]


def gather_one(g, x):
    return x, g.pt(x, 0, 1), g.pt(x, 1, 0)


def gather_two(g, near):
    own, along_u, along_t = near
    return [own, g.pt(along_t, 0, 1), along_u, along_t]


def scatter_one(g, blocks):
    own, far, to_u, to_t = blocks
    return own, to_u, to_t, g.pt(far.astype(BF16), 0, 1)


def scatter_two(g, state):
    own, to_u, to_t, relayed = state
    return (
        own,
        g.pt(to_u.astype(BF16), 0, 1),
        g.pt((to_t + relayed.astype(F32)).astype(BF16), 1, 0),
    )


def add_all(pieces):
    total = pieces[0]
    for x in pieces[1:]:
        total = total + x.astype(F32)
    return total


def permute_joined(permute, arrays):
    out = [None] * len(arrays)
    for n in sorted({x.shape[-1] for x in arrays}):
        which = [k for k, x in enumerate(arrays) if x.shape[-1] == n]
        flat = [arrays[k].reshape(-1, n) for k in which]
        got = permute(jnp.concatenate(flat) if len(flat) > 1 else flat[0])
        at = 0
        for k, x in zip(which, flat):
            out[k] = got[at : at + x.shape[0]].reshape(arrays[k].shape)
            at += x.shape[0]
    return out


class Shards:
    def __init__(self, g, live):
        self.g, self.live = g, live

    def fetch(self, name, parts):
        self.live[name] = {(p, 0, 0): x for p, x in enumerate(parts)}

    def fetch_a(self, *jobs):
        for d in range(1, self.g.A):
            got = permute_joined(
                lambda x, d=d: self.g.pa(x, d), [self.live[n][p, 0, 0] for n, p in jobs]
            )
            for (n, p), x in zip(jobs, got):
                self.live[n] = {**self.live[n], (p, d, 0): x}

    def fetch_b(self, *jobs):
        jobs = [
            (n, p, d) for n, p, rest in jobs for d in (range(1, self.g.A) if rest else (0,))
        ]
        for e in range(1, self.g.B):
            got = permute_joined(
                lambda x, e=e: self.g.pb(x, e), [self.live[n][p, d, 0] for n, p, d in jobs]
            )
            for (n, p, d), x in zip(jobs, got):
                self.live[n] = {**self.live[n], (p, d, e): x}

    def total(self, name, parts):
        g = self.g
        self.live[name] = {}
        for p, x in enumerate(parts):
            by_b = x.swapaxes(0, 1)
            sent = [pick(by_b, g.b ^ e).astype(BF16) for e in range(1, g.B)]
            self.live[name][p] = (pick(by_b, g.b), sent)

    def total_b(self, *jobs):
        g = self.g
        got = [
            permute_joined(lambda x, e=e: g.pb(x, e), [self.live[n][p][1][e - 1] for n, p in jobs])
            for e in range(1, g.B)
        ]
        for k, (n, p) in enumerate(jobs):
            self.live[n] = {**self.live[n], p: (self.live[n][p][0], [x[k] for x in got])}

    def prepare_a(self, *jobs):
        g = self.g
        for n, p in jobs:
            kept, got = self.live[n][p]
            rows = add_all([kept.astype(F32)] + got)
            sent = [pick(rows, g.a ^ d).astype(BF16) for d in range(1, g.A)]
            self.live[n] = {**self.live[n], p: (pick(rows, g.a), sent)}

    def total_a(self, *jobs):
        g = self.g
        got = [
            permute_joined(lambda x, d=d: g.pa(x, d), [self.live[n][p][1][d - 1] for n, p in jobs])
            for d in range(1, g.A)
        ]
        for k, (n, p) in enumerate(jobs):
            self.live[n] = {**self.live[n], p: (self.live[n][p][0], [x[k] for x in got])}

    def finish(self, *names):
        for n in names:
            self.live[n] = {
                p: add_all([kept] + got).astype(BF16) for p, (kept, got) in self.live[n].items()
            }

    def rows(self, name):
        g, state = self.g, self.live[name]
        parts = 1 + max(p for p, _, _ in state)
        height = [state[p, 0, 0].shape[0] for p in range(parts)]
        out = jnp.zeros((g.A, g.B, sum(height)) + state[0, 0, 0].shape[1:], BF16)
        for (p, d, e), x in state.items():
            starts = [g.a ^ d, g.b ^ e, sum(height[:p])] + [0] * (x.ndim - 1)
            out = lax.dynamic_update_slice(out, x[None, None], starts)
        return out

    def columns(self, name):
        g, state = self.g, self.live[name]
        pieces, rows = [], []
        for (p, d, e), x in state.items():
            pieces.append(x)
            for k in range(2):
                dt, du = ORDER[2 * p + k]
                rows.append(
                    (((g.a ^ d) * 2 + (g.t ^ dt)) * g.B + (g.b ^ e)) * 2 + (g.u ^ du)
                )
        return jnp.stack(rows).astype(jnp.int32), pieces

    def total_rows(self):
        g = self.g
        return jnp.stack(
            [
                (a * 2 + t) * g.B + (g.b ^ e)
                for t in range(2)
                for e in range(g.B)
                for a in range(g.A)
            ]
        ).astype(jnp.int32)

    def total_split(self, name, arrays):
        n = self.g.B
        self.live[name] = {p: (arrays[p * n], arrays[p * n + 1 : (p + 1) * n]) for p in range(2)}


def columns_pieces(g, state):
    both = jnp.stack([state[0], state[1]])
    return [pick(both, g.t ^ dt, g.u ^ du) for dt, du in ORDER]


def kernel_call(kernel, ins, outs, scratch, name):
    vmem = pl.BlockSpec(memory_space=pltpu.VMEM)
    smem = pl.BlockSpec(memory_space=pltpu.SMEM)
    return pl.pallas_call(
        kernel,
        in_specs=[smem if x.dtype == jnp.int32 else vmem for x in ins],
        out_specs=[vmem] * len(outs),
        out_shape=[jax.ShapeDtypeStruct(shape, dtype) for shape, dtype in outs],
        scratch_shapes=[pltpu.VMEM(shape, dtype) for shape, dtype in scratch],
        compiler_params=pltpu.CompilerParams(vmem_limit_bytes=20 << 20),
        cost_estimate=pl.CostEstimate(flops=1 << 20, bytes_accessed=1 << 16, transcendentals=0),
        name=name,
    )(*ins)


def join_rows(rows_ref, pieces, whole):
    height = pieces[0].shape[1]
    for j, piece in enumerate(pieces):
        for k in range(2):
            at = pl.multiple_of(rows_ref[2 * j + k] * height, height)
            whole[pl.ds(at, height), :] = piece[k]


def split_rows(rows_ref, whole, outs):
    j = 0
    for out in outs:
        count, height = out.shape[0], out.shape[1] * out.shape[2]
        for k in range(count):
            at = pl.multiple_of(rows_ref[j] * height, height)
            out[k] = whole[pl.ds(at, height), :].reshape(out.shape[1:])
            j += 1


BLOCK = 512


def over_rows(near, far, body):
    for part, ref in enumerate((near, far)):

        @pl.loop(0, ref.shape[0] // BLOCK)
        def _(j, part=part, ref=ref):
            at = pl.multiple_of(j * BLOCK, BLOCK)
            body(part, at, pl.multiple_of(part * ref.shape[0] + at, BLOCK), ref[pl.ds(at, BLOCK), :])


def grad_rows(near, far, right, whole):
    half = near.shape[0]

    @pl.loop(0, near.shape[1] // BLOCK)
    def _(j):
        at = pl.multiple_of(j * BLOCK, BLOCK)
        cols = pl.ds(at, BLOCK)
        whole[cols, :] = (
            dot_tn(near[:, cols], right[:half, :]) + dot_tn(far[:, cols], right[half:, :])
        ).astype(BF16)


def turn_half(x):
    return pltpu.roll(x, HD // 2, 1)


SCALE = 1.0 / math.sqrt(HD)


def attend(rows, pieces, near, far, cosines, sines, mask, g_q, g_k):
    many, span = 2 * near.shape[0], near.shape[0] // 4
    width = near.shape[1]

    def kernel(rows_ref, *refs):
        ws, refs = refs[: len(pieces)], refs[len(pieces) :]
        near, far, cos_ref, sin_ref, mask_ref, gq_ref, gk_ref = refs[:7]
        w_ref, raw_ref, q_ref, k_ref, v_ref, p_ref, att_ref, qkv_ref = refs[7:]
        join_rows(rows_ref, ws, w_ref)

        def project(part, at, row, x):
            qkv_ref[pl.ds(row, BLOCK), :] = dot(x, w_ref[...])

        over_rows(near, far, project)
        raw_ref[...] = qkv_ref[:, : 3 * HD]

        @pl.loop(0, 4)
        def _(k):
            own = pl.ds(pl.multiple_of(k * span, span), span)
            other = pl.ds(pl.multiple_of(4 * span + k * span, span), span)
            x = jnp.concatenate([qkv_ref[own, :], qkv_ref[other, :]])
            cos, sin = cos_ref[k], sin_ref[k]

            def head(u, gain):
                u = u * lax.rsqrt(jnp.mean(u * u, axis=-1, keepdims=True) + NORM_EPS) * gain
                return (u * cos + turn_half(u) * sin).astype(BF16)

            key = head(x[:, 2 * HD : 3 * HD], gk_ref[...])
            val = x[:, 3 * HD :].astype(BF16)
            k_ref[k] = key
            v_ref[k] = val
            for h in range(2):
                cols = slice(h * HD, (h + 1) * HD)
                query = head(x[:, cols], gq_ref[...])
                q_ref[k, :, cols] = query
                scores = jnp.where(mask_ref[k] > 0, dot_nt(query, key) * SCALE, NEG_FILL)
                expo = jnp.exp(scores - jnp.max(scores, axis=-1, keepdims=True))
                probs = expo / jnp.sum(expo, axis=-1, keepdims=True)
                p_ref[k, h] = probs
                att = dot(probs.astype(BF16), val).astype(BF16)
                att_ref[own, cols] = att[:span]
                att_ref[other, cols] = att[span:]

    seq = 2 * span
    outs = [
        ((width, 4 * HD), BF16), ((many, 3 * HD), F32), ((4, seq, 2 * HD), BF16),
        ((4, seq, HD), BF16), ((4, seq, HD), BF16), ((4, 2, seq, seq), F32), ((many, 2 * HD), BF16),
    ]
    ins = [rows, *pieces, near, far, cosines, sines, mask, g_q, g_k]
    return kernel_call(kernel, ins, outs, [((many, 4 * HD), F32)], "attend")


def attend_back(g, rows_out, near_d, far_d, w_o, att, saved, cosines, sines, g_q, g_k, near, far, rows_in):
    w_qkv, raw, q, k, v, probs = saved
    many, span = 2 * near.shape[0], near.shape[0] // 4
    width = near.shape[1]
    parts = 2 * g.B

    def kernel(rows_ref, *refs):
        near_d, far_d, wo_ref, att_ref, w_ref, raw_ref, q_ref, k_ref, v_ref, p_ref = refs[:10]
        cos_ref, sin_ref, gq_ref, gk_ref, near, far = refs[10:16]
        own_ref, sent_ref, go_ref, gain_ref, in_ref = refs[16:21]
        outs, (datt_ref, dqkv_ref, whole_ref) = refs[21 : 21 + parts], refs[21 + parts :]

        def project(part, at, row, x):
            datt_ref[pl.ds(row, BLOCK), :] = dot_nt(x, wo_ref[...]).astype(BF16)

        over_rows(near_d, far_d, project)
        gain_ref[...] = jnp.zeros_like(gain_ref)

        @pl.loop(0, 4)
        def _(s):
            own = pl.ds(pl.multiple_of(s * span, span), span)
            other = pl.ds(pl.multiple_of(4 * span + s * span, span), span)
            cos, sin = cos_ref[s], sin_ref[s]
            key, val = k_ref[s], v_ref[s]
            d_val = d_key = None

            def put_back(cols, x):
                x = x.astype(BF16)
                dqkv_ref[own, cols] = x[:span]
                dqkv_ref[other, cols] = x[span:]

            def head_back(cot, cols, gain, which):
                x = jnp.concatenate([raw_ref[own, cols], raw_ref[other, cols]])
                r = lax.rsqrt(jnp.mean(x * x, axis=-1, keepdims=True) + NORM_EPS)
                d_norm = cot * cos + turn_half(cot * sin)
                x = x * r
                gain_ref[which : which + 1, :] += jnp.sum(d_norm * x, axis=0, keepdims=True)
                d_norm = d_norm * gain
                put_back(cols, r * (d_norm - x * jnp.mean(d_norm * x, axis=-1, keepdims=True)))

            for h in range(2):
                cols = slice(h * HD, (h + 1) * HD)
                d_att = jnp.concatenate([datt_ref[own, cols], datt_ref[other, cols]])
                probs = p_ref[s, h]
                query = q_ref[s, :, cols]
                dv = dot_tn(probs.astype(BF16), d_att)
                dp = dot_nt(d_att, val)
                ds = probs * (dp - jnp.sum(probs * dp, axis=-1, keepdims=True)) * SCALE
                ds = ds.astype(BF16)
                dk = dot_tn(ds, query)
                d_val = dv if d_val is None else d_val + dv
                d_key = dk if d_key is None else d_key + dk
                head_back(dot(ds, key), cols, gq_ref[...], 0)
            head_back(d_key, slice(2 * HD, 3 * HD), gk_ref[...], 1)
            put_back(slice(3 * HD, 4 * HD), d_val)

        half = many // 2

        in_ref[...] = jnp.zeros_like(in_ref)

        def inward(part, at, row, x):
            d_xn = dot_nt(dqkv_ref[pl.ds(row, BLOCK), :], w_ref[...])
            in_ref[...] += jnp.sum(d_xn * x.astype(F32), axis=0, keepdims=True)
            out = sent_ref if part else own_ref
            out[pl.ds(at, BLOCK), :] = d_xn.astype(out.dtype)

        over_rows(near, far, inward)
        grad_rows(near, far, dqkv_ref, whole_ref)
        split_rows(rows_ref, whole_ref, outs)

        @pl.loop(0, width // BLOCK)
        def _(j):
            cols = pl.ds(pl.multiple_of(j * BLOCK, BLOCK), BLOCK)
            go_ref[:, cols] = (
                dot_tn(att_ref[:half, :], near_d[:, cols])
                + dot_tn(att_ref[half:, :], far_d[:, cols])
            ).astype(BF16)

    outs = [
        ((many // 2, width), F32), ((many // 2, width), BF16), ((2 * HD, width), BF16), ((2, HD), F32),
        ((1, width), F32),
    ]
    outs += [((g.A, 2, rows_in, 4 * HD), BF16)] * parts
    scratch = [((many, 2 * HD), BF16), ((many, 4 * HD), BF16), ((width, 4 * HD), BF16)]
    ins = [rows_out, near_d, far_d, w_o, att, w_qkv, raw, q, k, v, probs]
    ins += [cosines, sines, g_q, g_k, near, far]
    return kernel_call(kernel, ins, outs, scratch, "attend_back")


def feed(g, rows, rows_out, pieces, near, far, near_d, far_d, w_d, before, last):
    many, width = 2 * near.shape[0], near.shape[1]
    pw, rows_in = w_d.shape[0], pieces[0].shape[1]
    parts = 2 * g.B
    half = many // 2

    def kernel(rows_ref, rows_out_ref, *refs):
        ws, refs = refs[: len(pieces)], refs[len(pieces) :]
        near, far, near_d, far_d, wd_ref = refs[:5]
        given, refs = refs[5 : 5 + len(before)], refs[5 + len(before) :]
        hid_ref, gd_ref = refs[:2]
        outs, refs = refs[2 : 2 + parts], refs[2 + parts :]
        if len(before) == 0:
            (dgu_ref, w_ref), refs = refs[:2], refs[2:]
            dx = None
        else:
            dx, refs = refs[:2], refs[2:]
            (dgu_ref, w_ref), refs = refs[-2:], refs[:-2]
        (whole_ref,) = refs
        join_rows(rows_ref, ws, w_ref)

        def one(part, at, row, x):
            both = dot(x, w_ref[...])
            gate, up = both[:, :pw], both[:, pw:]
            d_ref = far_d if part else near_d
            dh = dot_nt(d_ref[pl.ds(at, BLOCK), :], wd_ref[...])
            sig = jax.nn.sigmoid(gate)
            lit = gate * sig
            rows = pl.ds(row, BLOCK)
            hid_ref[rows, :] = (lit * up).astype(BF16)
            dgu_ref[rows, pw:] = (dh * lit).astype(BF16)
            dgu_ref[rows, :pw] = (dh * up * sig * (1.0 + gate * (1.0 - sig))).astype(BF16)
            if dx is not None:
                total = dot_nt(dgu_ref[rows, :], w_ref[...])
                if last:
                    total = total + given[part][pl.ds(at, BLOCK), :]
                else:
                    total = total + dot_nt(given[0][rows, :], given[1][...])
                dx[part][pl.ds(at, BLOCK), :] = total.astype(dx[part].dtype)

        over_rows(near, far, one)
        grad_rows(near, far, dgu_ref, whole_ref)
        split_rows(rows_out_ref, whole_ref, outs)

        @pl.loop(0, width // BLOCK)
        def _(j):
            cols = pl.ds(pl.multiple_of(j * BLOCK, BLOCK), BLOCK)
            gd_ref[:, cols] = (
                dot_tn(hid_ref[:half, :], near_d[:, cols])
                + dot_tn(hid_ref[half:, :], far_d[:, cols])
            ).astype(BF16)

    outs = [((many, pw), BF16), ((pw, width), BF16)]
    outs += [((g.A, 2, rows_in, 2 * pw), BF16)] * parts
    local = [((many, 2 * pw), BF16), ((width, 2 * pw), BF16)]
    whole = [((width, 2 * pw), BF16)]
    if len(before) == 0:
        outs, scratch = outs + local, whole
    else:
        outs += [((half, width), F32), ((half, width), BF16 if last else F32)]
        scratch = whole + local
    ins = [rows, rows_out, *pieces, near, far, near_d, far_d, w_d, *before]
    got = kernel_call(kernel, ins, outs, scratch, "feed")
    return got[0], got[1], got[2 : 2 + parts], got[2 + parts :]


def project_out(x, w):
    half, width = x.shape[0] // 2, w.shape[1]

    def kernel(x_ref, w_ref, own_ref, sent_ref):
        @pl.loop(0, half // BLOCK)
        def _(j):
            at = pl.ds(pl.multiple_of(j * BLOCK, BLOCK), BLOCK)
            own_ref[at, :] = dot(x_ref[at, :], w_ref[...])
            low = pl.ds(pl.multiple_of(half + j * BLOCK, BLOCK), BLOCK)
            sent_ref[at, :] = dot(x_ref[low, :], w_ref[...]).astype(BF16)

    outs = [((half, width), F32), ((half, width), BF16)]
    return kernel_call(kernel, [x, w], outs, [], "project_out")


PARTS = 3


def per_device(
    g,
    tokens,
    segments,
    cotangent,
    w_query,
    w_key,
    w_value,
    w_output,
    w_gate,
    w_up,
    w_down,
    gain_in,
    gain_query,
    gain_key,
    gain_post,
):
    g.place()
    A, B, Q = g.A, g.B, g.Q
    _, span, width = tokens.shape
    seq_len = segments.shape[1]
    w_q, w_k, w_v, w_o, w_g, w_u, w_d = (
        w[0] for w in (w_query, w_key, w_value, w_output, w_gate, w_up, w_down)
    )
    rows_in, rows_o, rows_d = w_q.shape[0], w_o.shape[0], w_d.shape[0]
    q_width, kv_width, hidden_width = w_q.shape[1], w_k.shape[1], w_g.shape[1]
    g_in, g_q, g_k, g_post = gain_in[0], gain_query[0], gain_key[0], gain_post[0]
    many = 8 * span
    units = hidden_width // 8
    pw = units // PARTS
    hd2 = 2 * HD

    def hidden_cuts(t, u, c, part):
        out = []
        for j, i in enumerate(g.hidden_blocks(t, u, c)):
            lo, hi = max(j * rows_d, part * pw), min((j + 1) * rows_d, (part + 1) * pw)
            if lo < hi:
                out.append((i * rows_d + lo - j * rows_d, hi - lo))
        return out

    x_own = tokens[0].astype(F32)
    xn_own = rms_scale(x_own, g_in).astype(BF16)
    half_o = lax.dynamic_slice(w_o, (g.c * (rows_o // 2), 0), (rows_o // 2, width))
    half_d = lax.dynamic_slice(w_d, (g.c * (rows_d // 2), 0), (rows_d // 2, width))
    third = rows_d // 6
    seg_low = segments[0].astype(BF16)[None]
    seg_low = jnp.pad(seg_low, ((0, 15), (0, width - seq_len)))
    first, later = [], []
    for dt, du in ORDER:
        t, u = g.t ^ dt, g.u ^ du
        kv = g.kv_head(t, u, g.c, rows_o)
        first.append([(0, kv * hd2, hd2), (1, kv * HD, HD), (2, kv * HD, HD)])
        later.append(
            [
                (k, at, w)
                for part in range(PARTS)
                for k in (0, 1)
                for at, w in hidden_cuts(t, u, g.c, part)
            ]
        )
    first = cut_columns([w_q, w_k, w_v], first)
    later = cut_columns([w_g, w_u], later)
    L = Live(qkv=first)
    S = Shards(g, L)
    S.fetch("o", [half_o])
    S.fetch("d", [half_d[k * third : (k + 1) * third] for k in range(3)])

    def done(*floating):
        new = lax.optimization_barrier({k: v for k, v in L.items() if k not in floating})
        L.update(new)

    def pairs(x):
        return [jnp.stack(x[:2]), jnp.stack(x[2:])]

    done()

    L.qkv = chips_swap(g, L.qkv)
    S.fetch_a(("o", 0))
    S.fetch_b(("o", 0, False))
    L.xn, L.cot = jnp.concatenate([xn_own, seg_low]), cotangent[0]
    L.gu = (later[0], later[2], jnp.concatenate([later[1], later[3]], axis=1))
    done()

    L.xn = gather_one(g, L.xn)
    S.fetch("qkv", pairs(L.qkv))
    S.fetch_a(("qkv", 0))
    S.fetch_b(("qkv", 0, False), ("qkv", 1, False))
    done()
    L.xn = gather_two(g, L.xn)
    S.fetch_a(("qkv", 1))
    S.fetch_b(("qkv", 0, True), ("o", 0, True))
    L.gu_t = g.pt(L.gu[2], 1, 0)
    done("gu_t")

    near = jnp.concatenate([x[:span] for x in L.xn])
    L.seg = [x[span, :seq_len] for x in L.xn]
    L.xn = (near, g.pc(near))
    S.fetch_a(("d", 0))
    S.fetch_b(("qkv", 1, True))
    o_blocks = S.rows("o").reshape(2, 2, Q, rows_o // 2, width)
    o_mine = pick(o_blocks, g.u)
    o_next = g.px(pick(o_blocks, 1 - g.u), g.umask)
    L.gu_u = g.pt(L.gu[1], 0, 1)
    seg_all = jnp.stack(L.seg)
    index = lax.broadcasted_iota(jnp.int32, (4, seq_len), 1)
    earlier = seg_all[:, None, :] < seg_all[:, :, None]
    pos = index - jnp.sum(earlier.astype(jnp.int32), axis=-1)
    turn = lambda v: lax.dynamic_slice(
        jnp.concatenate([v, v], axis=1), (0, g.c * span), (4, seq_len)
    )
    index, pos, seg_own = turn(index), turn(pos).astype(F32), turn(seg_all)
    inv_freq = jnp.exp(jnp.arange(HD // 2, dtype=F32) * (-2.0 * math.log(ROPE_BASE) / HD))
    rotation = pos[:, :, None] * inv_freq
    cosines, sines = jnp.cos(rotation), jnp.sin(rotation)
    L.cosines = jnp.concatenate([cosines, cosines], axis=-1)
    L.sines = jnp.concatenate([-sines, sines], axis=-1)
    same_doc = (index[:, None, :] <= index[:, :, None]) & (
        seg_own[:, :, None] == seg_own[:, None, :]
    )
    L.mask = same_doc.astype(F32)
    L.o = (o_mine, o_next)
    done("gu_u", "o")

    def core_sum(own, sent):
        return own + g.pc(sent).astype(F32)

    def chip_blocks(x):
        return [x[k * span : (k + 1) * span] for k in range(4)]

    L.cot = gather_one(g, L.cot)
    pass_on, along_t = L.gu_t[:, : 2 * units], L.gu_t[:, 2 * units :]
    L.gu = [L.gu[0], g.pt(pass_on, 0, 1), L.gu_u, along_t]
    del L["gu_t"], L["gu_u"]
    S.fetch_a(("d", 1), ("d", 2))
    S.fetch_b(("d", 0, False), ("d", 1, False), ("d", 2, False))
    o_mine, o_next = L.o
    o_pair = jnp.where(g.u == 0, jnp.stack([o_mine, o_next]), jnp.stack([o_next, o_mine]))
    o_pair = o_pair.transpose(1, 2, 0, 3, 4)
    w_o_all = swap_halves(g, pick(o_pair, g.c), g.pc(pick(o_pair, 1 - g.c)))
    w_o_all = w_o_all.transpose(1, 2, 0, 3, 4).reshape(-1, width)
    rows, pieces = S.columns("qkv")
    *saved, att = attend(rows, pieces, *L.xn, L.cosines, L.sines, L.mask, gain_query, gain_key)
    L.part = project_out(att, w_o_all)
    done()

    L.part = core_sum(*L.part)
    L.cot = gather_two(g, L.cot)
    for k in range(PARTS):
        S.fetch(f"gu{k + 1}", pairs([x[:, 2 * pw * k : 2 * pw * (k + 1)] for x in L.gu]))
    del L["gu"]
    S.fetch_a(("gu1", 0))
    S.fetch_b(("d", 0, True), ("d", 1, True))
    done()

    L.part = scatter_one(g, chip_blocks(L.part))
    S.fetch_a(("gu1", 1))
    S.fetch_b(("d", 2, True), ("gu1", 0, False), ("gu1", 1, False))
    cot_near = jnp.concatenate(L.cot)
    L.cot = (cot_near, g.pc(cot_near))
    done()
    L.part = scatter_two(g, L.part)
    S.fetch_a(("gu2", 0))
    S.fetch_b(("gu1", 0, True), ("gu1", 1, True))
    d_blocks = S.rows("d").reshape(A, 2, B // 2, rows_d // 2, width).transpose(1, 0, 2, 3, 4)
    L.d = (pick(d_blocks, g.c), g.pc(pick(d_blocks, 1 - g.c)))
    done()

    mid = x_own + add_all(L.part)
    xn2_own, post_back = jax.vjp(rms_scale, mid, g_post)
    L.xn2 = gather_one(g, xn2_own.astype(BF16))
    S.fetch_a(("gu2", 1))
    S.fetch_b(("gu2", 0, False), ("gu2", 1, False))
    done()
    L.xn2 = gather_two(g, L.xn2)
    S.fetch_a(("gu3", 0))
    S.fetch_b(("gu2", 0, True), ("gu2", 1, True))
    w_d_all = swap_halves(g, *L.d)
    L.w_d_all = w_d_all.transpose(1, 2, 0, 3, 4).reshape(-1, width)
    done()

    near = jnp.concatenate(L.xn2)
    L.xn2 = (near, g.pc(near))
    S.fetch_a(("gu3", 1))
    S.fetch_b(("gu3", 0, False), ("gu3", 1, False))
    done()
    w_d_all = L.w_d_all

    rows_out = S.total_rows()

    def feed_part(part, before):
        name = f"gu{part + 1}"
        rows, pieces = S.columns(name)
        w_d_part = w_d_all[part * pw : (part + 1) * pw]
        hid, grad_d, grads, rest = feed(
            g, rows, rows_out, pieces, *L.xn2, *L.cot, w_d_part, before, part == PARTS - 1
        )
        S.total_split(name, grads)
        return (hid, grad_d), rest

    S.fetch_b(("gu3", 0, True), ("gu3", 1, True))
    L.one, L.rest = feed_part(0, ())
    done()

    S.total_b(("gu1", 0))
    S.prepare_a(("gu1", 0))
    L.two, L.rest = feed_part(1, L.rest)
    done()

    S.total_b(("gu1", 1))
    S.prepare_a(("gu1", 1))
    S.total_a(("gu1", 0))
    L.three, L.part = feed_part(2, L.rest)
    done()

    L.part = core_sum(*L.part)
    S.total_b(("gu2", 0))
    S.prepare_a(("gu2", 0))
    S.total_a(("gu1", 1))
    grad_d = jnp.concatenate([L.one[1], L.two[1], L.three[1]])
    grad_d = grad_d.reshape(A, B // 2, 2, rows_d // 2, width)
    grad_d = grad_d.transpose(2, 0, 1, 3, 4)
    L.d = (pick(grad_d, g.c), pick(grad_d, 1 - g.c))
    done()

    L.part = scatter_one(g, chip_blocks(L.part))
    S.total_b(("gu2", 1))
    S.prepare_a(("gu2", 1))
    S.total_a(("gu2", 0))
    S.finish("gu1")
    L.d = (L.d[0], g.pc(L.d[1]))
    L.hidden = jnp.concatenate([L.one[0], L.two[0], L.three[0]], axis=1)
    done()
    L.part = scatter_two(g, L.part)
    S.total_b(("gu3", 0))
    S.prepare_a(("gu3", 0))
    S.total_a(("gu2", 1))
    grad_d = swap_halves(g, *L.d).transpose(1, 0, 2, 3, 4).reshape(A, B, rows_d // 2, width)
    S.total("d", [grad_d[:, :, k * third : (k + 1) * third] for k in range(3)])
    L.out = project_out(L.hidden, w_d_all)
    done()

    d_post, grad_post = post_back(add_all(L.part))
    d_mid = cotangent[0].astype(F32) + d_post
    L.dmb = gather_one(g, d_mid.astype(BF16))
    S.total_b(("gu3", 1))
    S.prepare_a(("gu3", 1))
    S.total_a(("gu3", 0))
    S.finish("gu2")
    done()
    L.dmb = gather_two(g, L.dmb)
    S.total_b(("d", 0))
    S.prepare_a(("d", 0))
    S.total_a(("gu3", 1))
    L.out = core_sum(*L.out)
    done()

    near = jnp.concatenate(L.dmb)
    L.dmb = (near, g.pc(near))
    S.total_b(("d", 1))
    S.prepare_a(("d", 1))
    S.total_a(("d", 0))
    S.finish("gu3")
    L.out = scatter_one(g, chip_blocks(L.out))
    grads = [columns_pieces(g, L[f"gu{k + 1}"]) for k in range(PARTS)]
    L.gu = [jnp.concatenate(x, axis=1) for x in zip(*grads)]
    done()

    S.total_b(("d", 2))
    S.prepare_a(("d", 2))
    S.total_a(("d", 1))
    L.gu = chips_swap(g, L.gu)
    own, sent, grad_o, head_gains, grad_in, *grads = attend_back(
        g, rows_out, *L.dmb, w_o_all, att, saved, L.cosines, L.sines, gain_query, gain_key, *L.xn,
        rows_in,
    )
    L.part = (own, sent)
    L.gains = jnp.concatenate([grad_in[0] / g_in, grad_post, head_gains.reshape(-1)])
    grad_o = grad_o.reshape(Q, 2, rows_o, width).transpose(1, 0, 2, 3)
    L.o = (pick(grad_o, g.u), pick(grad_o, 1 - g.u))
    S.total_split("qkv", grads)
    done()

    L.part = core_sum(*L.part)
    S.total_b(("qkv", 0))
    S.prepare_a(("qkv", 0))
    S.total_a(("d", 2))
    L.o = (L.o[0], g.px(L.o[1], g.umask))
    L.gu = (L.gu, g.pc(jnp.stack(L.gu)))
    L.gains = L.gains + g.pc(L.gains)
    done()

    L.part = scatter_one(g, chip_blocks(L.part))
    S.total_b(("qkv", 1))
    S.total_a(("qkv", 0))
    S.finish("d")
    mine, other = L.o
    grad_o = jnp.where(g.u == 0, jnp.stack([mine, other]), jnp.stack([other, mine]))
    grad_o = grad_o.reshape(2, Q, 2, rows_o // 2, width).transpose(2, 0, 1, 3, 4)
    grad_o = swap_halves(g, pick(grad_o, g.c), g.pc(pick(grad_o, 1 - g.c)))
    grad_o = grad_o.transpose(1, 0, 2, 3, 4).reshape(A, B, rows_o // 2, width)
    S.total("o", [grad_o])
    S.prepare_a(("qkv", 1))
    bits = int(math.log2(g.n))
    for bit in range(bits // 2):
        L.gains = L.gains + g.px(L.gains, 1 << bit)
    done()
    L.part = scatter_two(g, L.part)
    for bit in range(bits // 2, bits):
        L.gains = L.gains + g.px(L.gains, 1 << bit)
    S.total_b(("o", 0))
    S.total_a(("qkv", 1))
    S.prepare_a(("o", 0))
    S.finish("qkv")
    d_sum = jnp.concatenate([L.d[k] for k in range(3)])
    L.d = (d_sum, g.pc(d_sum))
    done()

    S.total_a(("o", 0))
    L.qkv = chips_swap(g, columns_pieces(g, L.qkv))
    _, in_back = jax.vjp(lambda x: rms_scale(x, g_in), x_own)
    L.d_tokens = (d_mid + in_back(add_all(L.part))[0]).astype(BF16)
    grad_down = swap_halves(g, *L.d).reshape(1, rows_d, width).astype(F32)
    done()

    gains = L.gains[None]
    S.finish("o")
    L.out = scatter_two(g, L.out)
    L.qkv = (L.qkv, g.pc(jnp.stack(L.qkv)))
    grad_output = swap_halves(g, L.o[0], g.pc(L.o[0])).reshape(1, rows_o, width).astype(F32)
    activations = (mid + add_all(L.out)).astype(BF16)
    d_tokens = L.d_tokens

    def both_cores(pair):
        near, far = pair
        return list(near) + [far[k] for k in range(4)]

    pieces = both_cores(L.qkv)
    places = []
    for j, piece in enumerate(pieces):
        dt, du = ORDER[j % 4]
        kv = g.kv_head(g.t ^ dt, g.u ^ du, g.c ^ (j // 4), rows_o)
        places += [
            (j, 0, hd2, 0, kv * hd2),
            (j, hd2, HD, 1, kv * HD),
            (j, hd2 + HD, HD, 2, kv * HD),
        ]
    grad_query, grad_key, grad_value = place_columns(pieces, [q_width, kv_width, kv_width], places)

    pieces, places = both_cores(L.gu), []
    for part in range(PARTS):
        for j, piece in enumerate(pieces):
            dt, du = ORDER[j % 4]
            at = 2 * pw * part
            for to, w in hidden_cuts(g.t ^ dt, g.u ^ du, g.c ^ (j // 4), part):
                places += [
                    (j, at, w, 0, to),
                    (j, pw + at, w, 1, to),
                ]
                at += w
    grad_gate, grad_up = place_columns(pieces, [hidden_width, hidden_width], places)

    return (
        activations[None],
        d_tokens[None],
        grad_query[None],
        grad_key[None],
        grad_value[None],
        grad_output,
        grad_gate[None],
        grad_up[None],
        grad_down,
        gains[:, :width],
        gains[:, 2 * width : 2 * width + HD],
        gains[:, 2 * width + HD :],
        gains[:, width : 2 * width],
    )


def solution(mesh):
    rows = P("fsdp", "rep", None)
    cut_rows = P(None, "fsdp", None)
    return jax.shard_map(
        functools.partial(per_device, Grid(mesh)),
        mesh=mesh,
        in_specs=(rows, P("fsdp", None), rows) + (cut_rows,) * 7 + (P(),) * 4,
        out_specs=(rows, rows) + (cut_rows,) * 7 + (P(),) * 4,
        check_vma=False,
    )
```

```python
import functools
import math

import jax
import jax.numpy as jnp
from jax import lax
from jax.experimental import pallas as pl
from jax.experimental.pallas import tpu as pltpu
from jax.sharding import PartitionSpec as P

HD = 128
NORM_EPS = 1e-06
NEG_FILL = -1e30
ROPE_BASE = 1000000.0
BF16 = jnp.bfloat16
F32 = jnp.float32


def dot(x, y):
    return jnp.dot(x, y, preferred_element_type=F32)


def dot_tn(x, y):
    return lax.dot_general(x, y, (((0,), (0,)), ((), ())), preferred_element_type=F32)


def dot_nt(x, y):
    return lax.dot_general(x, y, (((1,), (1,)), ((), ())), preferred_element_type=F32)


def rms_scale(v, gain):
    return v * lax.rsqrt(jnp.mean(v * v, axis=-1, keepdims=True) + NORM_EPS) * gain


class Grid:
    def __init__(self, mesh):
        n = mesh.shape["fsdp"]
        assert mesh.shape["rep"] == 2 and n % 16 == 0 and n & (n - 1) == 0
        self.n = n
        self.F = n // 4
        self.B = 2 ** (int(math.log2(self.F)) // 2)
        self.A = self.F // self.B
        self.Q = self.F // 4
        self.tmask, self.umask = 2 * self.B, 1

    def place(self):
        i = lax.axis_index("fsdp")
        self.u = i % 2
        self.b = (i // 2) % self.B
        self.t = (i // (2 * self.B)) % 2
        self.a = i // (4 * self.B)
        self.c = lax.axis_index("rep")

    def px(self, x, mask):
        return lax.ppermute(x, "fsdp", [(i, i ^ mask) for i in range(self.n)])

    def pc(self, x):
        return lax.ppermute(x, "rep", [(0, 1), (1, 0)])

    def pa(self, x, delta):
        return self.px(x, 4 * self.B * delta)

    def pb(self, x, delta):
        return self.px(x, 2 * delta)

    def pt(self, x, dt, du):
        return self.px(x, dt * self.tmask + du * self.umask)

    def kv_head(self, t, u, c, rows):
        first = (u * 2 + c) * self.Q
        block = ((first // self.B * 2 + t) * self.B + first % self.B) * 2
        return block * rows // (2 * HD)

    def hidden_blocks(self, t, u, c):
        half = self.B // 2
        return [
            ((a * 2 + t) * self.B + c * half + b) * 2 + u
            for a in range(self.A)
            for b in range(half)
        ]


SHIFTS = ((1, 1), (0, 1), (1, 0))


def pick(x, *index):
    lead = len(index)
    starts = list(index) + [0] * (x.ndim - lead)
    sizes = [1] * lead + list(x.shape[lead:])
    return lax.dynamic_slice(x, starts, sizes).reshape(x.shape[lead:])


def put(x, piece, *index):
    lead = len(index)
    starts = list(index) + [0] * (x.ndim - lead)
    return lax.dynamic_update_slice(x, piece.reshape((1,) * lead + x.shape[lead:]), starts)


def swap_halves(g, own, other):
    return jnp.where(g.c == 0, jnp.stack([own, other]), jnp.stack([other, own]))


class Live(dict):
    __getattr__ = dict.__getitem__
    __setattr__ = dict.__setitem__


ORDER = ((0, 0),) + SHIFTS
LANES = 128


def cut_columns(sources, pieces):
    rows = sources[0].shape[0]
    cuts = [cut for piece in pieces for cut in piece]
    if any(c[2] % LANES for c in cuts) or rows % 16:
        return [
            jnp.concatenate(
                [lax.dynamic_slice(sources[k], (0, at), (rows, w)) for k, at, w in piece], axis=1
            )
            for piece in pieces
        ]

    def kernel(at_ref, *refs):
        ins, outs = refs[: len(sources)], refs[len(sources) :]
        j = 0
        for out, piece in zip(outs, pieces):
            to = 0
            for k, _, w in piece:
                start = pl.multiple_of(at_ref[j] * LANES, LANES)
                out[:, to : to + w] = ins[k][:, pl.ds(start, w)]
                to += w
                j += 1

    vmem = pl.BlockSpec(memory_space=pltpu.VMEM)
    return pl.pallas_call(
        kernel,
        in_specs=[pl.BlockSpec(memory_space=pltpu.SMEM)] + [vmem] * len(sources),
        out_specs=[vmem] * len(pieces),
        out_shape=[
            jax.ShapeDtypeStruct((rows, sum(w for _, _, w in piece)), sources[0].dtype)
            for piece in pieces
        ],
        compiler_params=pltpu.CompilerParams(vmem_limit_bytes=24 << 20),
        name="cut_columns",
    )(jnp.stack([jnp.asarray(at // LANES, jnp.int32) for _, at, _ in cuts]), *sources)


def place_columns(pieces, widths, places):
    rows = pieces[0].shape[0]
    if any(p[2] % LANES or p[1] % LANES for p in places) or rows % 16:
        outs = [jnp.zeros((rows, w), F32) for w in widths]
        for k, at, w, o, to in places:
            part = pieces[k][:, at : at + w].astype(F32)
            outs[o] = lax.dynamic_update_slice(outs[o], part, (0, to))
        return outs

    def kernel(to_ref, *refs):
        ins, outs = refs[: len(pieces)], refs[len(pieces) :]
        for j, (k, at, w, o, _) in enumerate(places):
            start = pl.multiple_of(to_ref[j] * LANES, LANES)
            outs[o][:, pl.ds(start, w)] = ins[k][:, at : at + w].astype(F32)

    vmem = pl.BlockSpec(memory_space=pltpu.VMEM)
    return pl.pallas_call(
        kernel,
        in_specs=[pl.BlockSpec(memory_space=pltpu.SMEM)] + [vmem] * len(pieces),
        out_specs=[vmem] * len(widths),
        out_shape=[jax.ShapeDtypeStruct((rows, w), F32) for w in widths],
        compiler_params=pltpu.CompilerParams(vmem_limit_bytes=24 << 20),
        name="place_columns",
    )(jnp.stack([jnp.asarray(to // LANES, jnp.int32) for *_, to in places]), *pieces)


def chips_swap(g, pieces):
    return [pieces[0]] + [g.pt(x, dt, du) for x, (dt, du) in zip(pieces[1:], SHIFTS)]


def gather_one(g, x):
    return x, g.pt(x, 0, 1), g.pt(x, 1, 0)


def gather_two(g, near):
    own, along_u, along_t = near
    return [own, g.pt(along_t, 0, 1), along_u, along_t]


def gather_two_along_t(g, near):
    own, along_u, along_t = near
    return [own, g.pt(along_u, 1, 0), along_u, along_t]


def scatter_one(g, blocks):
    own, far, to_u, to_t = blocks
    return own, to_u, to_t, g.pt(far.astype(BF16), 0, 1)


def scatter_two(g, state):
    own, to_u, to_t, relayed = state
    return (
        own,
        g.pt(to_u.astype(BF16), 0, 1),
        g.pt((to_t + relayed.astype(F32)).astype(BF16), 1, 0),
    )


def add_all(pieces):
    total = pieces[0]
    for x in pieces[1:]:
        total = total + x.astype(F32)
    return total


def permute_joined(permute, arrays):
    out = [None] * len(arrays)
    for n in sorted({x.shape[-1] for x in arrays}):
        which = [k for k, x in enumerate(arrays) if x.shape[-1] == n]
        flat = [arrays[k].reshape(-1, n) for k in which]
        got = permute(jnp.concatenate(flat) if len(flat) > 1 else flat[0])
        at = 0
        for k, x in zip(which, flat):
            out[k] = got[at : at + x.shape[0]].reshape(arrays[k].shape)
            at += x.shape[0]
    return out


class Shards:
    def __init__(self, g, live):
        self.g, self.live = g, live

    def fetch(self, name, parts):
        self.live[name] = {(p, 0, 0): x for p, x in enumerate(parts)}

    def fetch_a(self, *jobs):
        for d in range(1, self.g.A):
            got = permute_joined(
                lambda x, d=d: self.g.pa(x, d), [self.live[n][p, 0, 0] for n, p in jobs]
            )
            for (n, p), x in zip(jobs, got):
                self.live[n] = {**self.live[n], (p, d, 0): x}

    def fetch_b(self, *jobs):
        jobs = [
            (n, p, d) for n, p, rest in jobs for d in (range(1, self.g.A) if rest else (0,))
        ]
        for e in range(1, self.g.B):
            got = permute_joined(
                lambda x, e=e: self.g.pb(x, e), [self.live[n][p, d, 0] for n, p, d in jobs]
            )
            for (n, p, d), x in zip(jobs, got):
                self.live[n] = {**self.live[n], (p, d, e): x}

    def total(self, name, parts):
        g = self.g
        self.live[name] = {}
        for p, x in enumerate(parts):
            by_b = x.swapaxes(0, 1)
            sent = [pick(by_b, g.b ^ e).astype(BF16) for e in range(1, g.B)]
            self.live[name][p] = (pick(by_b, g.b), sent)

    def total_b(self, *jobs):
        g = self.g
        got = [
            permute_joined(lambda x, e=e: g.pb(x, e), [self.live[n][p][1][e - 1] for n, p in jobs])
            for e in range(1, g.B)
        ]
        for k, (n, p) in enumerate(jobs):
            self.live[n] = {**self.live[n], p: (self.live[n][p][0], [x[k] for x in got])}

    def prepare_a(self, *jobs):
        g = self.g
        for n, p in jobs:
            kept, got = self.live[n][p]
            rows = add_all([kept.astype(F32)] + got)
            sent = [pick(rows, g.a ^ d).astype(BF16) for d in range(1, g.A)]
            self.live[n] = {**self.live[n], p: (pick(rows, g.a), sent)}

    def total_a(self, *jobs):
        g = self.g
        got = [
            permute_joined(lambda x, d=d: g.pa(x, d), [self.live[n][p][1][d - 1] for n, p in jobs])
            for d in range(1, g.A)
        ]
        for k, (n, p) in enumerate(jobs):
            self.live[n] = {**self.live[n], p: (self.live[n][p][0], [x[k] for x in got])}

    def finish(self, *names):
        for n in names:
            self.live[n] = {
                p: add_all([kept] + got).astype(BF16) for p, (kept, got) in self.live[n].items()
            }

    def rows(self, name):
        g, state = self.g, self.live[name]
        parts = 1 + max(p for p, _, _ in state)
        height = [state[p, 0, 0].shape[0] for p in range(parts)]
        out = jnp.zeros((g.A, g.B, sum(height)) + state[0, 0, 0].shape[1:], BF16)
        for (p, d, e), x in state.items():
            starts = [g.a ^ d, g.b ^ e, sum(height[:p])] + [0] * (x.ndim - 1)
            out = lax.dynamic_update_slice(out, x[None, None], starts)
        return out

    def columns(self, name):
        g, state = self.g, self.live[name]
        pieces, rows = [], []
        for (p, d, e), x in state.items():
            pieces.append(x)
            for k in range(2):
                dt, du = ORDER[2 * p + k]
                rows.append(
                    (((g.a ^ d) * 2 + (g.t ^ dt)) * g.B + (g.b ^ e)) * 2 + (g.u ^ du)
                )
        return jnp.stack(rows).astype(jnp.int32), pieces

    def total_rows(self):
        g = self.g
        return jnp.stack(
            [
                (a * 2 + t) * g.B + (g.b ^ e)
                for t in range(2)
                for e in range(g.B)
                for a in range(g.A)
            ]
        ).astype(jnp.int32)

    def total_split(self, name, arrays):
        n = self.g.B
        self.live[name] = {p: (arrays[p * n], arrays[p * n + 1 : (p + 1) * n]) for p in range(2)}


def columns_pieces(g, state):
    both = jnp.stack([state[0], state[1]])
    return [pick(both, g.t ^ dt, g.u ^ du) for dt, du in ORDER]


def kernel_call(kernel, ins, outs, scratch, name):
    vmem = pl.BlockSpec(memory_space=pltpu.VMEM)
    smem = pl.BlockSpec(memory_space=pltpu.SMEM)
    return pl.pallas_call(
        kernel,
        in_specs=[smem if x.dtype == jnp.int32 else vmem for x in ins],
        out_specs=[vmem] * len(outs),
        out_shape=[jax.ShapeDtypeStruct(shape, dtype) for shape, dtype in outs],
        scratch_shapes=[pltpu.VMEM(shape, dtype) for shape, dtype in scratch],
        compiler_params=pltpu.CompilerParams(vmem_limit_bytes=16 << 20),
        cost_estimate=pl.CostEstimate(flops=1 << 20, bytes_accessed=1 << 16, transcendentals=0),
        name=name,
    )(*ins)


def join_rows(rows_ref, pieces, whole):
    height = pieces[0].shape[1]
    for j, piece in enumerate(pieces):
        for k in range(2):
            at = pl.multiple_of(rows_ref[2 * j + k] * height, height)
            whole[pl.ds(at, height), :] = piece[k]


def split_rows(rows_ref, whole, outs):
    j = 0
    for out in outs:
        count, height = out.shape[0], out.shape[1] * out.shape[2]
        for k in range(count):
            at = pl.multiple_of(rows_ref[j] * height, height)
            out[k] = whole[pl.ds(at, height), :].reshape(out.shape[1:])
            j += 1


BLOCK = 512


def over_rows(near, far, body):
    for part, ref in enumerate((near, far)):

        @pl.loop(0, ref.shape[0] // BLOCK)
        def _(j, part=part, ref=ref):
            at = pl.multiple_of(j * BLOCK, BLOCK)
            body(part, at, pl.multiple_of(part * ref.shape[0] + at, BLOCK), ref[pl.ds(at, BLOCK), :])


def grad_rows(near, far, right, whole):
    half = near.shape[0]

    @pl.loop(0, near.shape[1] // BLOCK)
    def _(j):
        at = pl.multiple_of(j * BLOCK, BLOCK)
        cols = pl.ds(at, BLOCK)
        whole[cols, :] = (
            dot_tn(near[:, cols], right[:half, :]) + dot_tn(far[:, cols], right[half:, :])
        ).astype(BF16)


def turn_half(x):
    return pltpu.roll(x, HD // 2, 1)


SCALE = 1.0 / math.sqrt(HD)


def attend(rows, pieces, near, far, cosines, sines, mask, g_q, g_k):
    many, span = 2 * near.shape[0], near.shape[0] // 4
    width = near.shape[1]

    def kernel(rows_ref, *refs):
        ws, refs = refs[: len(pieces)], refs[len(pieces) :]
        near, far, cos_ref, sin_ref, mask_ref, gq_ref, gk_ref = refs[:7]
        w_ref, raw_ref, q_ref, k_ref, v_ref, p_ref, att_ref, qkv_ref = refs[7:]
        join_rows(rows_ref, ws, w_ref)

        def project(part, at, row, x):
            qkv_ref[pl.ds(row, BLOCK), :] = dot(x, w_ref[...])

        over_rows(near, far, project)
        raw_ref[...] = qkv_ref[:, : 3 * HD]

        @pl.loop(0, 4)
        def _(k):
            own = pl.ds(pl.multiple_of(k * span, span), span)
            other = pl.ds(pl.multiple_of(4 * span + k * span, span), span)
            x = jnp.concatenate([qkv_ref[own, :], qkv_ref[other, :]])
            cos, sin = cos_ref[k], sin_ref[k]

            def head(u, gain):
                u = u * lax.rsqrt(jnp.mean(u * u, axis=-1, keepdims=True) + NORM_EPS) * gain
                return (u * cos + turn_half(u) * sin).astype(BF16)

            key = head(x[:, 2 * HD : 3 * HD], gk_ref[...])
            val = x[:, 3 * HD :].astype(BF16)
            k_ref[k] = key
            v_ref[k] = val
            for h in range(2):
                cols = slice(h * HD, (h + 1) * HD)
                query = head(x[:, cols], gq_ref[...])
                q_ref[k, :, cols] = query
                scores = jnp.where(mask_ref[k] > 0, dot_nt(query, key) * SCALE, NEG_FILL)
                expo = jnp.exp(scores - jnp.max(scores, axis=-1, keepdims=True))
                probs = expo / jnp.sum(expo, axis=-1, keepdims=True)
                p_ref[k, h] = probs
                att = dot(probs.astype(BF16), val).astype(BF16)
                att_ref[own, cols] = att[:span]
                att_ref[other, cols] = att[span:]

    seq = 2 * span
    outs = [
        ((width, 4 * HD), BF16), ((many, 3 * HD), F32), ((4, seq, 2 * HD), BF16),
        ((4, seq, HD), BF16), ((4, seq, HD), BF16), ((4, 2, seq, seq), F32), ((many, 2 * HD), BF16),
    ]
    ins = [rows, *pieces, near, far, cosines, sines, mask, g_q, g_k]
    return kernel_call(kernel, ins, outs, [((many, 4 * HD), F32)], "attend")


def attend_back(g, rows_out, near_d, far_d, w_o, att, saved, cosines, sines, g_q, g_k, near, far, rows_in):
    w_qkv, raw, q, k, v, probs = saved
    many, span = 2 * near.shape[0], near.shape[0] // 4
    width = near.shape[1]
    parts = 2 * g.B

    def kernel(rows_ref, *refs):
        near_d, far_d, wo_ref, att_ref, w_ref, raw_ref, q_ref, k_ref, v_ref, p_ref = refs[:10]
        cos_ref, sin_ref, gq_ref, gk_ref, near, far = refs[10:16]
        own_ref, sent_ref, go_ref, gain_ref, in_ref = refs[16:21]
        outs, (datt_ref, dqkv_ref, whole_ref) = refs[21 : 21 + parts], refs[21 + parts :]

        def project(part, at, row, x):
            datt_ref[pl.ds(row, BLOCK), :] = dot_nt(x, wo_ref[...]).astype(BF16)

        over_rows(near_d, far_d, project)
        gain_ref[...] = jnp.zeros_like(gain_ref)

        @pl.loop(0, 4)
        def _(s):
            own = pl.ds(pl.multiple_of(s * span, span), span)
            other = pl.ds(pl.multiple_of(4 * span + s * span, span), span)
            cos, sin = cos_ref[s], sin_ref[s]
            key, val = k_ref[s], v_ref[s]
            d_val = d_key = None

            def put_back(cols, x):
                x = x.astype(BF16)
                dqkv_ref[own, cols] = x[:span]
                dqkv_ref[other, cols] = x[span:]

            def head_back(cot, cols, gain, which):
                x = jnp.concatenate([raw_ref[own, cols], raw_ref[other, cols]])
                r = lax.rsqrt(jnp.mean(x * x, axis=-1, keepdims=True) + NORM_EPS)
                d_norm = cot * cos + turn_half(cot * sin)
                x = x * r
                gain_ref[which : which + 1, :] += jnp.sum(d_norm * x, axis=0, keepdims=True)
                d_norm = d_norm * gain
                put_back(cols, r * (d_norm - x * jnp.mean(d_norm * x, axis=-1, keepdims=True)))

            for h in range(2):
                cols = slice(h * HD, (h + 1) * HD)
                d_att = jnp.concatenate([datt_ref[own, cols], datt_ref[other, cols]])
                probs = p_ref[s, h]
                query = q_ref[s, :, cols]
                dv = dot_tn(probs.astype(BF16), d_att)
                dp = dot_nt(d_att, val)
                ds = probs * (dp - jnp.sum(probs * dp, axis=-1, keepdims=True)) * SCALE
                ds = ds.astype(BF16)
                dk = dot_tn(ds, query)
                d_val = dv if d_val is None else d_val + dv
                d_key = dk if d_key is None else d_key + dk
                head_back(dot(ds, key), cols, gq_ref[...], 0)
            head_back(d_key, slice(2 * HD, 3 * HD), gk_ref[...], 1)
            put_back(slice(3 * HD, 4 * HD), d_val)

        half = many // 2

        in_ref[...] = jnp.zeros_like(in_ref)

        def inward(part, at, row, x):
            d_xn = dot_nt(dqkv_ref[pl.ds(row, BLOCK), :], w_ref[...])
            in_ref[...] += jnp.sum(d_xn * x.astype(F32), axis=0, keepdims=True)
            out = sent_ref if part else own_ref
            out[pl.ds(at, BLOCK), :] = d_xn.astype(out.dtype)

        over_rows(near, far, inward)
        grad_rows(near, far, dqkv_ref, whole_ref)
        split_rows(rows_ref, whole_ref, outs)

        @pl.loop(0, width // BLOCK)
        def _(j):
            cols = pl.ds(pl.multiple_of(j * BLOCK, BLOCK), BLOCK)
            go_ref[:, cols] = (
                dot_tn(att_ref[:half, :], near_d[:, cols])
                + dot_tn(att_ref[half:, :], far_d[:, cols])
            ).astype(BF16)

    outs = [
        ((many // 2, width), F32), ((many // 2, width), BF16), ((2 * HD, width), BF16), ((2, HD), F32),
        ((1, width), F32),
    ]
    outs += [((g.A, 2, rows_in, 4 * HD), BF16)] * parts
    scratch = [((many, 2 * HD), BF16), ((many, 4 * HD), BF16), ((width, 4 * HD), BF16)]
    ins = [rows_out, near_d, far_d, w_o, att, w_qkv, raw, q, k, v, probs]
    ins += [cosines, sines, g_q, g_k, near, far]
    return kernel_call(kernel, ins, outs, scratch, "attend_back")


def feed(g, rows, rows_out, pieces, near, far, near_d, far_d, w_d, before, last):
    many, width = 2 * near.shape[0], near.shape[1]
    pw, rows_in = w_d.shape[0], pieces[0].shape[1]
    parts = 2 * g.B
    half = many // 2

    def kernel(rows_ref, rows_out_ref, *refs):
        ws, refs = refs[: len(pieces)], refs[len(pieces) :]
        near, far, near_d, far_d, wd_ref = refs[:5]
        given, refs = refs[5 : 5 + len(before)], refs[5 + len(before) :]
        hid_ref, gd_ref = refs[:2]
        outs, refs = refs[2 : 2 + parts], refs[2 + parts :]
        if len(before) == 0:
            (dgu_ref, w_ref), refs = refs[:2], refs[2:]
            dx = None
        else:
            dx, refs = refs[:2], refs[2:]
            (dgu_ref, w_ref), refs = refs[-2:], refs[:-2]
        (whole_ref,) = refs
        join_rows(rows_ref, ws, w_ref)

        def one(part, at, row, x):
            both = dot(x, w_ref[...])
            gate, up = both[:, :pw], both[:, pw:]
            d_ref = far_d if part else near_d
            dh = dot_nt(d_ref[pl.ds(at, BLOCK), :], wd_ref[...])
            sig = jax.nn.sigmoid(gate)
            lit = gate * sig
            rows = pl.ds(row, BLOCK)
            hid_ref[rows, :] = (lit * up).astype(BF16)
            dgu_ref[rows, pw:] = (dh * lit).astype(BF16)
            dgu_ref[rows, :pw] = (dh * up * sig * (1.0 + gate * (1.0 - sig))).astype(BF16)
            if dx is not None:
                total = dot_nt(dgu_ref[rows, :], w_ref[...])
                if last:
                    total = total + given[part][pl.ds(at, BLOCK), :]
                else:
                    total = total + dot_nt(given[0][rows, :], given[1][...])
                dx[part][pl.ds(at, BLOCK), :] = total.astype(dx[part].dtype)

        over_rows(near, far, one)
        grad_rows(near, far, dgu_ref, whole_ref)
        split_rows(rows_out_ref, whole_ref, outs)

        @pl.loop(0, width // BLOCK)
        def _(j):
            cols = pl.ds(pl.multiple_of(j * BLOCK, BLOCK), BLOCK)
            gd_ref[:, cols] = (
                dot_tn(hid_ref[:half, :], near_d[:, cols])
                + dot_tn(hid_ref[half:, :], far_d[:, cols])
            ).astype(BF16)

    outs = [((many, pw), BF16), ((pw, width), BF16)]
    outs += [((g.A, 2, rows_in, 2 * pw), BF16)] * parts
    local = [((many, 2 * pw), BF16), ((width, 2 * pw), BF16)]
    whole = [((width, 2 * pw), BF16)]
    if len(before) == 0:
        outs, scratch = outs + local, whole
    else:
        outs += [((half, width), F32), ((half, width), BF16 if last else F32)]
        scratch = whole + local
    ins = [rows, rows_out, *pieces, near, far, near_d, far_d, w_d, *before]
    got = kernel_call(kernel, ins, outs, scratch, "feed")
    return got[0], got[1], got[2 : 2 + parts], got[2 + parts :]


def project_out(x, w):
    half, width = x.shape[0] // 2, w.shape[1]

    def kernel(x_ref, w_ref, own_ref, sent_ref):
        @pl.loop(0, half // BLOCK)
        def _(j):
            at = pl.ds(pl.multiple_of(j * BLOCK, BLOCK), BLOCK)
            own_ref[at, :] = dot(x_ref[at, :], w_ref[...])
            low = pl.ds(pl.multiple_of(half + j * BLOCK, BLOCK), BLOCK)
            sent_ref[at, :] = dot(x_ref[low, :], w_ref[...]).astype(BF16)

    outs = [((half, width), F32), ((half, width), BF16)]
    return kernel_call(kernel, [x, w], outs, [], "project_out")


PARTS = 3


def per_device(
    g,
    tokens,
    segments,
    cotangent,
    w_query,
    w_key,
    w_value,
    w_output,
    w_gate,
    w_up,
    w_down,
    gain_in,
    gain_query,
    gain_key,
    gain_post,
):
    g.place()
    A, B, Q = g.A, g.B, g.Q
    _, span, width = tokens.shape
    seq_len = segments.shape[1]
    w_q, w_k, w_v, w_o, w_g, w_u, w_d = (
        w[0] for w in (w_query, w_key, w_value, w_output, w_gate, w_up, w_down)
    )
    rows_in, rows_o, rows_d = w_q.shape[0], w_o.shape[0], w_d.shape[0]
    q_width, kv_width, hidden_width = w_q.shape[1], w_k.shape[1], w_g.shape[1]
    g_in, g_q, g_k, g_post = gain_in[0], gain_query[0], gain_key[0], gain_post[0]
    many = 8 * span
    units = hidden_width // 8
    pw = units // PARTS
    hd2 = 2 * HD

    def hidden_cuts(t, u, c, part):
        out = []
        for j, i in enumerate(g.hidden_blocks(t, u, c)):
            lo, hi = max(j * rows_d, part * pw), min((j + 1) * rows_d, (part + 1) * pw)
            if lo < hi:
                out.append((i * rows_d + lo - j * rows_d, hi - lo))
        return out

    x_own = tokens[0].astype(F32)
    xn_own = rms_scale(x_own, g_in).astype(BF16)
    half_o = lax.dynamic_slice(w_o, (g.c * (rows_o // 2), 0), (rows_o // 2, width))
    half_d = lax.dynamic_slice(w_d, (g.c * (rows_d // 2), 0), (rows_d // 2, width))
    third = rows_d // 6
    seg_low = segments[0].astype(BF16)[None]
    seg_low = jnp.pad(seg_low, ((0, 15), (0, width - seq_len)))
    qkv_cuts, gu_cuts = [], []
    for dt, du in ORDER:
        t, u = g.t ^ dt, g.u ^ du
        kv = g.kv_head(t, u, g.c, rows_o)
        qkv_cuts.append([(2, kv * hd2, hd2), (3, kv * HD, HD), (4, kv * HD, HD)])
        gu_cuts.append(
            [
                (k, at, w)
                for part in range(PARTS)
                for k in (0, 1)
                for at, w in hidden_cuts(t, u, g.c, part)
            ]
        )
    cuts = [qkv_cuts[0], qkv_cuts[1], qkv_cuts[2] + gu_cuts[2], qkv_cuts[3]]
    cuts += [gu_cuts[0], gu_cuts[3] + gu_cuts[1]]
    cut = cut_columns([w_g, w_u, w_q, w_k, w_v], cuts)
    L = Live(qkv=cut[:4])
    S = Shards(g, L)
    S.fetch("o", [half_o])
    S.fetch("d", [half_d[k * third : (k + 1) * third] for k in range(3)])

    def done(*floating):
        new = lax.optimization_barrier({k: v for k, v in L.items() if k not in floating})
        L.update(new)

    def pairs(x):
        return [jnp.stack(x[:2]), jnp.stack(x[2:])]

    done()

    L.qkv = chips_swap(g, L.qkv)
    S.fetch_a(("o", 0))
    S.fetch_b(("o", 0, False))
    L.xn, L.cot = jnp.concatenate([xn_own, seg_low]), cotangent[0]
    L.gu, L.gu_t, L.gu_f = cut[4], cut[5][:, : 2 * units], cut[5][:, 2 * units :]
    done()

    L.xn = gather_one(g, L.xn)
    L.gu_u = L.qkv[2][:, 4 * HD :]
    L.qkv[2] = L.qkv[2][:, : 4 * HD]
    S.fetch("qkv", pairs(L.qkv))
    S.fetch_a(("qkv", 0))
    S.fetch_b(("qkv", 0, False), ("qkv", 1, False), ("o", 0, True))
    done()
    L.xn = gather_two(g, L.xn)
    S.fetch_a(("qkv", 1))
    S.fetch_b(("qkv", 0, True))
    L.gu_f = g.pt(L.gu_f, 1, 0)
    o_blocks = S.rows("o").reshape(2, 2, Q, rows_o // 2, width)
    L.o = (pick(o_blocks, g.u), pick(o_blocks, 1 - g.u))
    done()

    near = jnp.concatenate([x[:span] for x in L.xn])
    L.seg = [x[span, :seq_len] for x in L.xn]
    L.xn = (near, g.pc(near))
    L.gu_t = g.pt(L.gu_t, 1, 0)
    joined = rows_in == span
    if joined:
        L.gu_f = jnp.concatenate([L.cot, L.gu_f], axis=1)
    S.fetch_a(("d", 0))
    S.fetch_b(("qkv", 1, True))
    L.o = (L.o[0], g.px(L.o[1], g.umask))
    seg_all = jnp.stack(L.seg)
    index = lax.broadcasted_iota(jnp.int32, (4, seq_len), 1)
    earlier = seg_all[:, None, :] < seg_all[:, :, None]
    pos = index - jnp.sum(earlier.astype(jnp.int32), axis=-1)
    turn = lambda v: lax.dynamic_slice(
        jnp.concatenate([v, v], axis=1), (0, g.c * span), (4, seq_len)
    )
    index, pos, seg_own = turn(index), turn(pos).astype(F32), turn(seg_all)
    inv_freq = jnp.exp(jnp.arange(HD // 2, dtype=F32) * (-2.0 * math.log(ROPE_BASE) / HD))
    rotation = pos[:, :, None] * inv_freq
    cosines, sines = jnp.cos(rotation), jnp.sin(rotation)
    L.cosines = jnp.concatenate([cosines, cosines], axis=-1)
    L.sines = jnp.concatenate([-sines, sines], axis=-1)
    same_doc = (index[:, None, :] <= index[:, :, None]) & (
        seg_own[:, :, None] == seg_own[:, None, :]
    )
    L.mask = same_doc.astype(F32)
    done()

    def core_sum(own, sent):
        return own + g.pc(sent).astype(F32)

    def chip_blocks(x):
        return [x[k * span : (k + 1) * span] for k in range(4)]

    if joined:
        both = g.pt(L.gu_f, 0, 1)
        L.cot = (L.cot, both[:, :width], g.pt(L.cot, 1, 0))
        L.gu_f = both[:, width:]
    else:
        L.cot, L.gu_f = gather_one(g, L.cot), g.pt(L.gu_f, 0, 1)
    L.gu = [L.gu, L.gu_f, L.gu_u, L.gu_t]
    del L["gu_t"], L["gu_u"], L["gu_f"]
    S.fetch_a(("d", 1), ("d", 2))
    S.fetch_b(("d", 0, False), ("d", 1, False), ("d", 2, False))
    o_mine, o_next = L.o
    o_pair = jnp.where(g.u == 0, jnp.stack([o_mine, o_next]), jnp.stack([o_next, o_mine]))
    o_pair = o_pair.transpose(1, 2, 0, 3, 4)
    w_o_all = swap_halves(g, pick(o_pair, g.c), g.pc(pick(o_pair, 1 - g.c)))
    w_o_all = w_o_all.transpose(1, 2, 0, 3, 4).reshape(-1, width)
    rows, pieces = S.columns("qkv")
    *saved, att = attend(rows, pieces, *L.xn, L.cosines, L.sines, L.mask, gain_query, gain_key)
    L.part = project_out(att, w_o_all)
    done()

    L.part = core_sum(*L.part)
    for k in range(PARTS):
        S.fetch(f"gu{k + 1}", pairs([x[:, 2 * pw * k : 2 * pw * (k + 1)] for x in L.gu]))
    del L["gu"]
    S.fetch_a(("gu1", 0))
    S.fetch_b(("d", 0, True), ("d", 1, True))
    done()

    L.part = scatter_one(g, chip_blocks(L.part))
    S.fetch_a(("gu1", 1))
    S.fetch_b(("d", 2, True), ("gu1", 0, False), ("gu1", 1, False))
    L.cot = gather_two_along_t(g, L.cot)
    done()
    L.part = scatter_two(g, L.part)
    S.fetch_a(("gu2", 0))
    S.fetch_b(("gu1", 0, True), ("gu1", 1, True))
    cot_near = jnp.concatenate(L.cot)
    L.cot = (cot_near, g.pc(cot_near))
    d_blocks = S.rows("d").reshape(A, 2, B // 2, rows_d // 2, width).transpose(1, 0, 2, 3, 4)
    L.d = (pick(d_blocks, g.c), pick(d_blocks, 1 - g.c))
    done()

    mid = x_own + add_all(L.part)
    xn2_own, post_back = jax.vjp(rms_scale, mid, g_post)
    L.xn2 = gather_one(g, xn2_own.astype(BF16))
    S.fetch_a(("gu2", 1))
    S.fetch_b(("gu2", 0, False), ("gu2", 1, False))
    L.d = (L.d[0], g.pc(L.d[1]))
    done()
    L.xn2 = gather_two(g, L.xn2)
    S.fetch_a(("gu3", 0))
    S.fetch_b(("gu2", 0, True), ("gu2", 1, True))
    w_d_all = swap_halves(g, *L.d)
    L.w_d_all = w_d_all.transpose(1, 2, 0, 3, 4).reshape(-1, width)
    done()

    near = jnp.concatenate(L.xn2)
    L.xn2 = (near, g.pc(near))
    S.fetch_a(("gu3", 1))
    S.fetch_b(("gu3", 0, False), ("gu3", 1, False))
    done()
    w_d_all = L.w_d_all

    rows_out = S.total_rows()

    def feed_part(part, before):
        name = f"gu{part + 1}"
        rows, pieces = S.columns(name)
        w_d_part = w_d_all[part * pw : (part + 1) * pw]
        hid, grad_d, grads, rest = feed(
            g, rows, rows_out, pieces, *L.xn2, *L.cot, w_d_part, before, part == PARTS - 1
        )
        S.total_split(name, grads)
        return (hid, grad_d), rest

    S.fetch_b(("gu3", 0, True), ("gu3", 1, True))
    L.one, L.rest = feed_part(0, ())
    done()

    S.total_b(("gu1", 0))
    S.prepare_a(("gu1", 0))
    L.two, L.rest = feed_part(1, L.rest)
    done()

    S.total_b(("gu1", 1))
    S.prepare_a(("gu1", 1))
    S.total_a(("gu1", 0))
    L.three, L.part = feed_part(2, L.rest)
    done()

    L.part = core_sum(*L.part)
    S.total_b(("gu2", 0))
    S.prepare_a(("gu2", 0))
    S.total_a(("gu1", 1))
    grad_d = jnp.concatenate([L.one[1], L.two[1], L.three[1]])
    grad_d = grad_d.reshape(A, B // 2, 2, rows_d // 2, width)
    grad_d = grad_d.transpose(2, 0, 1, 3, 4)
    L.d = (pick(grad_d, g.c), pick(grad_d, 1 - g.c))
    done()

    L.part = scatter_one(g, chip_blocks(L.part))
    S.total_b(("gu2", 1))
    S.prepare_a(("gu2", 1))
    S.total_a(("gu2", 0))
    S.finish("gu1")
    L.d = (L.d[0], g.pc(L.d[1]))
    L.hidden = jnp.concatenate([L.one[0], L.two[0], L.three[0]], axis=1)
    done()
    L.part = scatter_two(g, L.part)
    S.total_b(("gu3", 0))
    S.prepare_a(("gu3", 0))
    S.total_a(("gu2", 1))
    grad_d = swap_halves(g, *L.d).transpose(1, 0, 2, 3, 4).reshape(A, B, rows_d // 2, width)
    S.total("d", [grad_d[:, :, k * third : (k + 1) * third] for k in range(3)])
    L.out = project_out(L.hidden, w_d_all)
    done()

    d_post, grad_post = post_back(add_all(L.part))
    d_mid = cotangent[0].astype(F32) + d_post
    L.dmb = gather_one(g, d_mid.astype(BF16))
    S.total_b(("gu3", 1))
    S.prepare_a(("gu3", 1))
    S.total_a(("gu3", 0))
    S.finish("gu2")
    done()
    L.dmb = gather_two(g, L.dmb)
    S.total_b(("d", 0))
    S.prepare_a(("d", 0))
    S.total_a(("gu3", 1))
    L.out = core_sum(*L.out)
    done()

    near = jnp.concatenate(L.dmb)
    L.dmb = (near, g.pc(near))
    S.total_b(("d", 1))
    S.prepare_a(("d", 1))
    S.total_a(("d", 0))
    S.finish("gu3")
    out = chip_blocks(L.out)
    L.out = scatter_one(g, out)
    grads = [columns_pieces(g, L[f"gu{k + 1}"]) for k in range(PARTS)]
    L.gu = [jnp.concatenate(x, axis=1) for x in zip(*grads)]
    done()

    S.total_b(("d", 2))
    S.prepare_a(("d", 2))
    S.total_a(("d", 1))
    L.gu = chips_swap(g, L.gu)
    own, sent, grad_o, head_gains, grad_in, *grads = attend_back(
        g, rows_out, *L.dmb, w_o_all, att, saved, L.cosines, L.sines, gain_query, gain_key, *L.xn,
        rows_in,
    )
    L.part = (own, sent)
    L.gains = jnp.concatenate([grad_in[0] / g_in, grad_post, head_gains.reshape(-1)])
    grad_o = grad_o.reshape(Q, 2, rows_o, width).transpose(1, 0, 2, 3)
    L.o = (pick(grad_o, g.u), pick(grad_o, 1 - g.u))
    S.total_split("qkv", grads)
    done()

    L.part = core_sum(*L.part)
    S.total_b(("qkv", 0))
    S.prepare_a(("qkv", 0))
    S.total_a(("d", 2))
    L.o = (L.o[0], g.px(L.o[1], g.umask))
    own, to_u, to_t, relayed = L.out
    L.out = (own, to_u, g.pt((to_t + relayed.astype(F32)).astype(BF16), 1, 0))
    L.gains = L.gains + g.pc(L.gains)
    done()

    L.part = scatter_one(g, chip_blocks(L.part))
    S.total_b(("qkv", 1))
    S.total_a(("qkv", 0))
    S.finish("d")
    mine, other = L.o
    grad_o = jnp.where(g.u == 0, jnp.stack([mine, other]), jnp.stack([other, mine]))
    grad_o = grad_o.reshape(2, Q, 2, rows_o // 2, width).transpose(2, 0, 1, 3, 4)
    grad_o = swap_halves(g, pick(grad_o, g.c), g.pc(pick(grad_o, 1 - g.c)))
    grad_o = grad_o.transpose(1, 0, 2, 3, 4).reshape(A, B, rows_o // 2, width)
    S.total("o", [grad_o])
    S.prepare_a(("qkv", 1))
    bits = int(math.log2(g.n))
    for bit in range(bits // 2):
        L.gains = L.gains + g.px(L.gains, 1 << bit)
    done()
    L.part = scatter_two(g, L.part)
    for bit in range(bits // 2, bits - 1):
        L.gains = L.gains + g.px(L.gains, 1 << bit)
    S.total_b(("o", 0))
    S.total_a(("qkv", 1))
    S.prepare_a(("o", 0))
    S.finish("qkv")
    L.gu = (L.gu, g.pc(jnp.stack(L.gu)))
    d_sum = jnp.concatenate([L.d[k] for k in range(3)])
    L.d = d_sum
    done()

    def both_cores(pair):
        near, far = pair
        return list(near) + [far[k] for k in range(4)]

    pieces, places = both_cores(L.gu), []
    for part in range(PARTS):
        for j, piece in enumerate(pieces):
            dt, du = ORDER[j % 4]
            at = 2 * pw * part
            for to, w in hidden_cuts(g.t ^ dt, g.u ^ du, g.c ^ (j // 4), part):
                places += [
                    (j, at, w, 0, to),
                    (j, pw + at, w, 1, to),
                ]
                at += w
    L.gate, L.up = place_columns(pieces, [hidden_width, hidden_width], places)
    S.total_a(("o", 0))
    L.qkv = chips_swap(g, columns_pieces(g, L.qkv))
    own, to_u, from_t = L.out
    L.out = (own, g.pt(to_u.astype(BF16), 0, 1), from_t)
    _, in_back = jax.vjp(lambda x: rms_scale(x, g_in), x_own)
    L.d_tokens = (d_mid + in_back(add_all(L.part))[0]).astype(BF16)
    done("out")

    L.d = swap_halves(g, L.d, g.pc(L.d)).reshape(1, rows_d, width).astype(F32)
    gains = (L.gains + g.px(L.gains, 1 << (bits - 1)))[None]
    S.finish("o")
    L.qkv = (L.qkv, g.pc(jnp.stack(L.qkv)))
    grad_output = swap_halves(g, L.o[0], g.pc(L.o[0])).reshape(1, rows_o, width).astype(F32)
    activations = (mid + add_all(L.out)).astype(BF16)
    d_tokens = L.d_tokens

    pieces = both_cores(L.qkv)
    places = []
    for j, piece in enumerate(pieces):
        dt, du = ORDER[j % 4]
        kv = g.kv_head(g.t ^ dt, g.u ^ du, g.c ^ (j // 4), rows_o)
        places += [
            (j, 0, hd2, 0, kv * hd2),
            (j, hd2, HD, 1, kv * HD),
            (j, hd2 + HD, HD, 2, kv * HD),
        ]
    grad_query, grad_key, grad_value = place_columns(pieces, [q_width, kv_width, kv_width], places)

    return (
        activations[None],
        d_tokens[None],
        grad_query[None],
        grad_key[None],
        grad_value[None],
        grad_output,
        L.gate[None],
        L.up[None],
        L.d,
        gains[:, :width],
        gains[:, 2 * width : 2 * width + HD],
        gains[:, 2 * width + HD :],
        gains[:, width : 2 * width],
    )


def solution(mesh):
    rows = P("fsdp", "rep", None)
    cut_rows = P(None, "fsdp", None)
    return jax.shard_map(
        functools.partial(per_device, Grid(mesh)),
        mesh=mesh,
        in_specs=(rows, P("fsdp", None), rows) + (cut_rows,) * 7 + (P(),) * 4,
        out_specs=(rows, rows) + (cut_rows,) * 7 + (P(),) * 4,
        check_vma=False,
    )
```

```python
import functools
import math

import jax
import jax.numpy as jnp
from jax import lax
from jax.experimental import pallas as pl
from jax.experimental.pallas import tpu as pltpu
from jax.sharding import PartitionSpec as P

HD = 128
NORM_EPS = 1e-06
NEG_FILL = -1e30
ROPE_BASE = 1000000.0
BF16 = jnp.bfloat16
F32 = jnp.float32


def dot(x, y):
    return jnp.dot(x, y, preferred_element_type=F32)


def dot_tn(x, y):
    return lax.dot_general(x, y, (((0,), (0,)), ((), ())), preferred_element_type=F32)


def dot_nt(x, y):
    return lax.dot_general(x, y, (((1,), (1,)), ((), ())), preferred_element_type=F32)


def rms_scale(v, gain):
    return v * lax.rsqrt(jnp.mean(v * v, axis=-1, keepdims=True) + NORM_EPS) * gain


class Grid:
    def __init__(self, mesh):
        n = mesh.shape["fsdp"]
        assert mesh.shape["rep"] == 2 and n % 16 == 0 and n & (n - 1) == 0
        self.n = n
        self.F = n // 4
        self.B = 2 ** (int(math.log2(self.F)) // 2)
        self.A = self.F // self.B
        self.Q = self.F // 4
        self.tmask, self.umask = 2 * self.B, 1

    def place(self):
        i = lax.axis_index("fsdp")
        self.u = i % 2
        self.b = (i // 2) % self.B
        self.t = (i // (2 * self.B)) % 2
        self.a = i // (4 * self.B)
        self.c = lax.axis_index("rep")

    def px(self, x, mask):
        return lax.ppermute(x, "fsdp", [(i, i ^ mask) for i in range(self.n)])

    def pc(self, x):
        return lax.ppermute(x, "rep", [(0, 1), (1, 0)])

    def pa(self, x, delta):
        return self.px(x, 4 * self.B * delta)

    def pb(self, x, delta):
        return self.px(x, 2 * delta)

    def pt(self, x, dt, du):
        return self.px(x, dt * self.tmask + du * self.umask)

    def kv_head(self, t, u, c, rows):
        first = (u * 2 + c) * self.Q
        block = ((first // self.B * 2 + t) * self.B + first % self.B) * 2
        return block * rows // (2 * HD)

    def hidden_blocks(self, t, u, c):
        half = self.B // 2
        return [
            ((a * 2 + t) * self.B + c * half + b) * 2 + u
            for a in range(self.A)
            for b in range(half)
        ]


SHIFTS = ((1, 1), (0, 1), (1, 0))


def pick(x, *index):
    lead = len(index)
    starts = list(index) + [0] * (x.ndim - lead)
    sizes = [1] * lead + list(x.shape[lead:])
    return lax.dynamic_slice(x, starts, sizes).reshape(x.shape[lead:])


def put(x, piece, *index):
    lead = len(index)
    starts = list(index) + [0] * (x.ndim - lead)
    return lax.dynamic_update_slice(x, piece.reshape((1,) * lead + x.shape[lead:]), starts)


def swap_halves(g, own, other):
    return jnp.where(g.c == 0, jnp.stack([own, other]), jnp.stack([other, own]))


class Live(dict):
    __getattr__ = dict.__getitem__
    __setattr__ = dict.__setitem__


ORDER = ((0, 0),) + SHIFTS
LANES = 128


def cut_columns(sources, pieces, tail):
    rows = sources[0].shape[0]
    cuts = [cut for piece in pieces for cut in piece]
    widths = [sum(w for _, _, w in piece) for piece in pieces]
    heights = [rows if rest is None else rows + rest.shape[0] for rest in tail]
    if any(c[2] % LANES for c in cuts) or rows % 16:
        out = [
            jnp.concatenate(
                [lax.dynamic_slice(sources[k], (0, at), (rows, w)) for k, at, w in piece], axis=1
            )
            for piece in pieces
        ]
        return [
            x if rest is None else jnp.concatenate([x, jnp.pad(rest, ((0, 0), (0, w - rest.shape[1])))])
            for x, rest, w in zip(out, tail, widths)
        ]
    (rest,) = {id(x): x for x in tail if x is not None}.values()

    def kernel(at_ref, *refs):
        ins, rest_ref, outs = refs[: len(sources)], refs[len(sources)], refs[len(sources) + 1 :]
        j = 0
        for out, piece, height in zip(outs, pieces, heights):
            to = 0
            for k, _, w in piece:
                start = pl.multiple_of(at_ref[j] * LANES, LANES)
                out[:rows, to : to + w] = ins[k][:, pl.ds(start, w)]
                to += w
                j += 1
            if height > rows:
                out[rows:, :] = jnp.zeros((height - rows, to), out.dtype)
                out[rows:, : rest.shape[1]] = rest_ref[...]

    vmem = pl.BlockSpec(memory_space=pltpu.VMEM)
    return pl.pallas_call(
        kernel,
        in_specs=[pl.BlockSpec(memory_space=pltpu.SMEM)] + [vmem] * (len(sources) + 1),
        out_specs=[vmem] * len(pieces),
        out_shape=[
            jax.ShapeDtypeStruct(shape, sources[0].dtype) for shape in zip(heights, widths)
        ],
        compiler_params=pltpu.CompilerParams(vmem_limit_bytes=24 << 20),
        name="cut_columns",
    )(jnp.stack([jnp.asarray(at // LANES, jnp.int32) for _, at, _ in cuts]), *sources, rest)


def place_columns(pieces, widths, places):
    rows = pieces[0].shape[0]
    if any(p[2] % LANES or p[1] % LANES for p in places) or rows % 16:
        outs = [jnp.zeros((rows, w), F32) for w in widths]
        for k, at, w, o, to in places:
            part = pieces[k][:, at : at + w].astype(F32)
            outs[o] = lax.dynamic_update_slice(outs[o], part, (0, to))
        return outs

    def kernel(to_ref, *refs):
        ins, outs = refs[: len(pieces)], refs[len(pieces) :]
        for j, (k, at, w, o, _) in enumerate(places):
            start = pl.multiple_of(to_ref[j] * LANES, LANES)
            outs[o][:, pl.ds(start, w)] = ins[k][:, at : at + w].astype(F32)

    vmem = pl.BlockSpec(memory_space=pltpu.VMEM)
    return pl.pallas_call(
        kernel,
        in_specs=[pl.BlockSpec(memory_space=pltpu.SMEM)] + [vmem] * len(pieces),
        out_specs=[vmem] * len(widths),
        out_shape=[jax.ShapeDtypeStruct((rows, w), F32) for w in widths],
        compiler_params=pltpu.CompilerParams(vmem_limit_bytes=24 << 20),
        name="place_columns",
    )(jnp.stack([jnp.asarray(to // LANES, jnp.int32) for *_, to in places]), *pieces)


def chips_swap(g, pieces):
    return [pieces[0]] + [g.pt(x, dt, du) for x, (dt, du) in zip(pieces[1:], SHIFTS)]


def gather_one(g, x):
    return x, g.pt(x, 0, 1), g.pt(x, 1, 0)


def gather_two(g, near):
    own, along_u, along_t = near
    return [own, g.pt(along_t, 0, 1), along_u, along_t]


def gather_two_along_t(g, near):
    own, along_u, along_t = near
    return [own, g.pt(along_u, 1, 0), along_u, along_t]


def scatter_one(g, blocks):
    own, far, to_u, to_t = blocks
    return own, to_u, to_t, g.pt(far.astype(BF16), 0, 1)


def scatter_two(g, state):
    own, to_u, to_t, relayed = state
    return (
        own,
        g.pt(to_u.astype(BF16), 0, 1),
        g.pt((to_t + relayed.astype(F32)).astype(BF16), 1, 0),
    )


def add_all(pieces):
    total = pieces[0]
    for x in pieces[1:]:
        total = total + x.astype(F32)
    return total


def permute_joined(permute, arrays):
    out = [None] * len(arrays)
    for n in sorted({x.shape[-1] for x in arrays}):
        which = [k for k, x in enumerate(arrays) if x.shape[-1] == n]
        flat = [arrays[k].reshape(-1, n) for k in which]
        got = permute(jnp.concatenate(flat) if len(flat) > 1 else flat[0])
        at = 0
        for k, x in zip(which, flat):
            out[k] = got[at : at + x.shape[0]].reshape(arrays[k].shape)
            at += x.shape[0]
    return out


class Shards:
    def __init__(self, g, live):
        self.g, self.live = g, live

    def fetch(self, name, parts, whole=None):
        self.live[name] = {(p, 0, 0): x for p, x in enumerate(parts)}
        if whole is not None:
            self.live[name + "_whole"] = whole

    def fetch_b_own(self, name):
        whole = self.live.pop(name + "_whole")
        own = {p: x for (p, d, e), x in self.live[name].items() if d == e == 0}
        for e in range(1, self.g.B):
            got, at = self.g.pb(whole, e), 0
            for p in sorted(own):
                rows = own[p].shape[0]
                self.live[name] = {**self.live[name], (p, 0, e): got[at : at + rows]}
                at += rows

    def fetch_a(self, *jobs):
        for d in range(1, self.g.A):
            got = permute_joined(
                lambda x, d=d: self.g.pa(x, d), [self.live[n][p, 0, 0] for n, p in jobs]
            )
            for (n, p), x in zip(jobs, got):
                self.live[n] = {**self.live[n], (p, d, 0): x}

    def fetch_b(self, *jobs):
        jobs = [
            (n, p, d) for n, p, rest in jobs for d in (range(1, self.g.A) if rest else (0,))
        ]
        for e in range(1, self.g.B):
            got = permute_joined(
                lambda x, e=e: self.g.pb(x, e), [self.live[n][p, d, 0] for n, p, d in jobs]
            )
            for (n, p, d), x in zip(jobs, got):
                self.live[n] = {**self.live[n], (p, d, e): x}

    def total(self, name, parts):
        g = self.g
        self.live[name] = {}
        for p, x in enumerate(parts):
            by_b = x.swapaxes(0, 1)
            sent = [pick(by_b, g.b ^ e).astype(BF16) for e in range(1, g.B)]
            self.live[name][p] = (pick(by_b, g.b), sent)

    def total_b(self, *jobs):
        g = self.g
        got = [
            permute_joined(lambda x, e=e: g.pb(x, e), [self.live[n][p][1][e - 1] for n, p in jobs])
            for e in range(1, g.B)
        ]
        for k, (n, p) in enumerate(jobs):
            self.live[n] = {**self.live[n], p: (self.live[n][p][0], [x[k] for x in got])}

    def prepare_a(self, *jobs):
        g = self.g
        for n, p in jobs:
            kept, got = self.live[n][p]
            rows = add_all([kept.astype(F32)] + got)
            sent = [pick(rows, g.a ^ d).astype(BF16) for d in range(1, g.A)]
            self.live[n] = {**self.live[n], p: (pick(rows, g.a), sent)}

    def total_a(self, *jobs):
        g = self.g
        got = [
            permute_joined(lambda x, d=d: g.pa(x, d), [self.live[n][p][1][d - 1] for n, p in jobs])
            for d in range(1, g.A)
        ]
        for k, (n, p) in enumerate(jobs):
            self.live[n] = {**self.live[n], p: (self.live[n][p][0], [x[k] for x in got])}

    def finish(self, *names):
        for n in names:
            self.live[n] = {
                p: add_all([kept] + got).astype(BF16) for p, (kept, got) in self.live[n].items()
            }

    def rows(self, name):
        g, state = self.g, self.live[name]
        parts = 1 + max(p for p, _, _ in state)
        height = [state[p, 0, 0].shape[0] for p in range(parts)]
        out = jnp.zeros((g.A, g.B, sum(height)) + state[0, 0, 0].shape[1:], BF16)
        for (p, d, e), x in state.items():
            starts = [g.a ^ d, g.b ^ e, sum(height[:p])] + [0] * (x.ndim - 1)
            out = lax.dynamic_update_slice(out, x[None, None], starts)
        return out

    def columns(self, name):
        g, state = self.g, self.live[name]
        pieces, rows = [], []
        for (p, d, e), x in state.items():
            pieces.append(x)
            for k in range(2):
                dt, du = ORDER[2 * p + k]
                rows.append(
                    (((g.a ^ d) * 2 + (g.t ^ dt)) * g.B + (g.b ^ e)) * 2 + (g.u ^ du)
                )
        return jnp.stack(rows).astype(jnp.int32), pieces

    def total_rows(self):
        g = self.g
        return jnp.stack(
            [
                (a * 2 + t) * g.B + (g.b ^ e)
                for t in range(2)
                for e in range(g.B)
                for a in range(g.A)
            ]
        ).astype(jnp.int32)

    def total_split(self, name, arrays):
        n = self.g.B
        self.live[name] = {p: (arrays[p * n], arrays[p * n + 1 : (p + 1) * n]) for p in range(2)}


def columns_pieces(g, state):
    both = jnp.stack([state[0], state[1]])
    return [pick(both, g.t ^ dt, g.u ^ du) for dt, du in ORDER]


def kernel_call(kernel, ins, outs, scratch, name):
    vmem = pl.BlockSpec(memory_space=pltpu.VMEM)
    smem = pl.BlockSpec(memory_space=pltpu.SMEM)
    return pl.pallas_call(
        kernel,
        in_specs=[smem if x.dtype == jnp.int32 else vmem for x in ins],
        out_specs=[vmem] * len(outs),
        out_shape=[jax.ShapeDtypeStruct(shape, dtype) for shape, dtype in outs],
        scratch_shapes=[pltpu.VMEM(shape, dtype) for shape, dtype in scratch],
        compiler_params=pltpu.CompilerParams(vmem_limit_bytes=16 << 20),
        cost_estimate=pl.CostEstimate(flops=1 << 20, bytes_accessed=1 << 16, transcendentals=0),
        name=name,
    )(*ins)


def join_rows(rows_ref, pieces, whole):
    height = pieces[0].shape[1]
    for j, piece in enumerate(pieces):
        for k in range(2):
            at = pl.multiple_of(rows_ref[2 * j + k] * height, height)
            whole[pl.ds(at, height), :] = piece[k]


def split_rows(rows_ref, whole, outs):
    j = 0
    for out in outs:
        count, height = out.shape[0], out.shape[1] * out.shape[2]
        for k in range(count):
            at = pl.multiple_of(rows_ref[j] * height, height)
            out[k] = whole[pl.ds(at, height), :].reshape(out.shape[1:])
            j += 1


BLOCK = 512


def over_rows(near, far, body):
    for part, ref in enumerate((near, far)):

        @pl.loop(0, ref.shape[0] // BLOCK)
        def _(j, part=part, ref=ref):
            at = pl.multiple_of(j * BLOCK, BLOCK)
            body(part, at, pl.multiple_of(part * ref.shape[0] + at, BLOCK), ref[pl.ds(at, BLOCK), :])


def grad_rows(near, far, right, whole):
    half = near.shape[0]

    @pl.loop(0, near.shape[1] // BLOCK)
    def _(j):
        at = pl.multiple_of(j * BLOCK, BLOCK)
        cols = pl.ds(at, BLOCK)
        whole[cols, :] = (
            dot_tn(near[:, cols], right[:half, :]) + dot_tn(far[:, cols], right[half:, :])
        ).astype(BF16)


def turn_half(x):
    return pltpu.roll(x, HD // 2, 1)


SCALE = 1.0 / math.sqrt(HD)


def attend(rows, pieces, near, far, cosines, sines, mask, g_q, g_k):
    many, span = 2 * near.shape[0], near.shape[0] // 4
    width = near.shape[1]

    def kernel(rows_ref, *refs):
        ws, refs = refs[: len(pieces)], refs[len(pieces) :]
        near, far, cos_ref, sin_ref, mask_ref, gq_ref, gk_ref = refs[:7]
        w_ref, raw_ref, q_ref, k_ref, v_ref, p_ref, att_ref, qkv_ref = refs[7:]
        join_rows(rows_ref, ws, w_ref)

        def project(part, at, row, x):
            qkv_ref[pl.ds(row, BLOCK), :] = dot(x, w_ref[...])

        over_rows(near, far, project)
        raw_ref[...] = qkv_ref[:, : 3 * HD]

        @pl.loop(0, 4)
        def _(k):
            own = pl.ds(pl.multiple_of(k * span, span), span)
            other = pl.ds(pl.multiple_of(4 * span + k * span, span), span)
            x = jnp.concatenate([qkv_ref[own, :], qkv_ref[other, :]])
            cos, sin = cos_ref[k], sin_ref[k]

            def head(u, gain):
                u = u * lax.rsqrt(jnp.mean(u * u, axis=-1, keepdims=True) + NORM_EPS) * gain
                return (u * cos + turn_half(u) * sin).astype(BF16)

            key = head(x[:, 2 * HD : 3 * HD], gk_ref[...])
            val = x[:, 3 * HD :].astype(BF16)
            k_ref[k] = key
            v_ref[k] = val
            for h in range(2):
                cols = slice(h * HD, (h + 1) * HD)
                query = head(x[:, cols], gq_ref[...])
                q_ref[k, :, cols] = query
                scores = jnp.where(mask_ref[k] > 0, dot_nt(query, key) * SCALE, NEG_FILL)
                expo = jnp.exp(scores - jnp.max(scores, axis=-1, keepdims=True))
                probs = expo / jnp.sum(expo, axis=-1, keepdims=True)
                p_ref[k, h] = probs
                att = dot(probs.astype(BF16), val).astype(BF16)
                att_ref[own, cols] = att[:span]
                att_ref[other, cols] = att[span:]

    seq = 2 * span
    outs = [
        ((width, 4 * HD), BF16), ((many, 3 * HD), F32), ((4, seq, 2 * HD), BF16),
        ((4, seq, HD), BF16), ((4, seq, HD), BF16), ((4, 2, seq, seq), F32), ((many, 2 * HD), BF16),
    ]
    ins = [rows, *pieces, near, far, cosines, sines, mask, g_q, g_k]
    return kernel_call(kernel, ins, outs, [((many, 4 * HD), F32)], "attend")


def attend_back(g, rows_out, near_d, far_d, w_o, att, saved, cosines, sines, g_q, g_k, near, far, rows_in):
    w_qkv, raw, q, k, v, probs = saved
    many, span = 2 * near.shape[0], near.shape[0] // 4
    width = near.shape[1]
    parts = 2 * g.B

    def kernel(rows_ref, *refs):
        near_d, far_d, wo_ref, att_ref, w_ref, raw_ref, q_ref, k_ref, v_ref, p_ref = refs[:10]
        cos_ref, sin_ref, gq_ref, gk_ref, near, far = refs[10:16]
        own_ref, sent_ref, go_ref, gain_ref, in_ref = refs[16:21]
        outs, (datt_ref, dqkv_ref, whole_ref) = refs[21 : 21 + parts], refs[21 + parts :]

        def project(part, at, row, x):
            datt_ref[pl.ds(row, BLOCK), :] = dot_nt(x, wo_ref[...]).astype(BF16)

        over_rows(near_d, far_d, project)
        gain_ref[...] = jnp.zeros_like(gain_ref)

        @pl.loop(0, 4)
        def _(s):
            own = pl.ds(pl.multiple_of(s * span, span), span)
            other = pl.ds(pl.multiple_of(4 * span + s * span, span), span)
            cos, sin = cos_ref[s], sin_ref[s]
            key, val = k_ref[s], v_ref[s]
            d_val = d_key = None

            def put_back(cols, x):
                x = x.astype(BF16)
                dqkv_ref[own, cols] = x[:span]
                dqkv_ref[other, cols] = x[span:]

            def head_back(cot, cols, gain, which):
                x = jnp.concatenate([raw_ref[own, cols], raw_ref[other, cols]])
                r = lax.rsqrt(jnp.mean(x * x, axis=-1, keepdims=True) + NORM_EPS)
                d_norm = cot * cos + turn_half(cot * sin)
                x = x * r
                gain_ref[which : which + 1, :] += jnp.sum(d_norm * x, axis=0, keepdims=True)
                d_norm = d_norm * gain
                put_back(cols, r * (d_norm - x * jnp.mean(d_norm * x, axis=-1, keepdims=True)))

            for h in range(2):
                cols = slice(h * HD, (h + 1) * HD)
                d_att = jnp.concatenate([datt_ref[own, cols], datt_ref[other, cols]])
                probs = p_ref[s, h]
                query = q_ref[s, :, cols]
                dv = dot_tn(probs.astype(BF16), d_att)
                dp = dot_nt(d_att, val)
                ds = probs * (dp - jnp.sum(probs * dp, axis=-1, keepdims=True)) * SCALE
                ds = ds.astype(BF16)
                dk = dot_tn(ds, query)
                d_val = dv if d_val is None else d_val + dv
                d_key = dk if d_key is None else d_key + dk
                head_back(dot(ds, key), cols, gq_ref[...], 0)
            head_back(d_key, slice(2 * HD, 3 * HD), gk_ref[...], 1)
            put_back(slice(3 * HD, 4 * HD), d_val)

        half = many // 2

        in_ref[...] = jnp.zeros_like(in_ref)

        def inward(part, at, row, x):
            d_xn = dot_nt(dqkv_ref[pl.ds(row, BLOCK), :], w_ref[...])
            in_ref[...] += jnp.sum(d_xn * x.astype(F32), axis=0, keepdims=True)
            out = sent_ref if part else own_ref
            out[pl.ds(at, BLOCK), :] = d_xn.astype(out.dtype)

        over_rows(near, far, inward)
        grad_rows(near, far, dqkv_ref, whole_ref)
        split_rows(rows_ref, whole_ref, outs)

        @pl.loop(0, width // BLOCK)
        def _(j):
            cols = pl.ds(pl.multiple_of(j * BLOCK, BLOCK), BLOCK)
            go_ref[:, cols] = (
                dot_tn(att_ref[:half, :], near_d[:, cols])
                + dot_tn(att_ref[half:, :], far_d[:, cols])
            ).astype(BF16)

    outs = [
        ((many // 2, width), F32), ((many // 2, width), BF16), ((2 * HD, width), BF16), ((2, HD), F32),
        ((1, width), F32),
    ]
    outs += [((g.A, 2, rows_in, 4 * HD), BF16)] * parts
    scratch = [((many, 2 * HD), BF16), ((many, 4 * HD), BF16), ((width, 4 * HD), BF16)]
    ins = [rows_out, near_d, far_d, w_o, att, w_qkv, raw, q, k, v, probs]
    ins += [cosines, sines, g_q, g_k, near, far]
    return kernel_call(kernel, ins, outs, scratch, "attend_back")


def feed(g, rows, rows_out, pieces, near, far, near_d, far_d, w_d, before, last):
    many, width = 2 * near.shape[0], near.shape[1]
    pw, rows_in = w_d.shape[0], pieces[0].shape[1]
    parts = 2 * g.B
    half = many // 2

    def kernel(rows_ref, rows_out_ref, *refs):
        ws, refs = refs[: len(pieces)], refs[len(pieces) :]
        near, far, near_d, far_d, wd_ref = refs[:5]
        given, refs = refs[5 : 5 + len(before)], refs[5 + len(before) :]
        hid_ref, gd_ref = refs[:2]
        outs, refs = refs[2 : 2 + parts], refs[2 + parts :]
        if len(before) == 0:
            (dgu_ref, w_ref), refs = refs[:2], refs[2:]
            dx = None
        else:
            dx, refs = refs[:2], refs[2:]
            (dgu_ref, w_ref), refs = refs[-2:], refs[:-2]
        (whole_ref,) = refs
        join_rows(rows_ref, ws, w_ref)

        def one(part, at, row, x):
            both = dot(x, w_ref[...])
            gate, up = both[:, :pw], both[:, pw:]
            d_ref = far_d if part else near_d
            dh = dot_nt(d_ref[pl.ds(at, BLOCK), :], wd_ref[...])
            sig = jax.nn.sigmoid(gate)
            lit = gate * sig
            rows = pl.ds(row, BLOCK)
            hid_ref[rows, :] = (lit * up).astype(BF16)
            dgu_ref[rows, pw:] = (dh * lit).astype(BF16)
            dgu_ref[rows, :pw] = (dh * up * sig * (1.0 + gate * (1.0 - sig))).astype(BF16)
            if dx is not None:
                total = dot_nt(dgu_ref[rows, :], w_ref[...])
                if last:
                    total = total + given[part][pl.ds(at, BLOCK), :]
                else:
                    total = total + dot_nt(given[0][rows, :], given[1][...])
                dx[part][pl.ds(at, BLOCK), :] = total.astype(dx[part].dtype)

        over_rows(near, far, one)
        grad_rows(near, far, dgu_ref, whole_ref)
        split_rows(rows_out_ref, whole_ref, outs)

        @pl.loop(0, width // BLOCK)
        def _(j):
            cols = pl.ds(pl.multiple_of(j * BLOCK, BLOCK), BLOCK)
            gd_ref[:, cols] = (
                dot_tn(hid_ref[:half, :], near_d[:, cols])
                + dot_tn(hid_ref[half:, :], far_d[:, cols])
            ).astype(BF16)

    outs = [((many, pw), BF16), ((pw, width), BF16)]
    outs += [((g.A, 2, rows_in, 2 * pw), BF16)] * parts
    local = [((many, 2 * pw), BF16), ((width, 2 * pw), BF16)]
    whole = [((width, 2 * pw), BF16)]
    if len(before) == 0:
        outs, scratch = outs + local, whole
    else:
        outs += [((half, width), F32), ((half, width), BF16 if last else F32)]
        scratch = whole + local
    ins = [rows, rows_out, *pieces, near, far, near_d, far_d, w_d, *before]
    got = kernel_call(kernel, ins, outs, scratch, "feed")
    return got[0], got[1], got[2 : 2 + parts], got[2 + parts :]


def project_out(x, w):
    half, width = x.shape[0] // 2, w.shape[1]

    def kernel(x_ref, w_ref, own_ref, sent_ref):
        @pl.loop(0, half // BLOCK)
        def _(j):
            at = pl.ds(pl.multiple_of(j * BLOCK, BLOCK), BLOCK)
            own_ref[at, :] = dot(x_ref[at, :], w_ref[...])
            low = pl.ds(pl.multiple_of(half + j * BLOCK, BLOCK), BLOCK)
            sent_ref[at, :] = dot(x_ref[low, :], w_ref[...]).astype(BF16)

    outs = [((half, width), F32), ((half, width), BF16)]
    return kernel_call(kernel, [x, w], outs, [], "project_out")


PARTS = 3


def per_device(
    g,
    tokens,
    segments,
    cotangent,
    w_query,
    w_key,
    w_value,
    w_output,
    w_gate,
    w_up,
    w_down,
    gain_in,
    gain_query,
    gain_key,
    gain_post,
):
    g.place()
    A, B, Q = g.A, g.B, g.Q
    _, span, width = tokens.shape
    seq_len = segments.shape[1]
    w_q, w_k, w_v, w_o, w_g, w_u, w_d = (
        w[0] for w in (w_query, w_key, w_value, w_output, w_gate, w_up, w_down)
    )
    rows_in, rows_o, rows_d = w_q.shape[0], w_o.shape[0], w_d.shape[0]
    q_width, kv_width, hidden_width = w_q.shape[1], w_k.shape[1], w_g.shape[1]
    g_in, g_q, g_k, g_post = gain_in[0], gain_query[0], gain_key[0], gain_post[0]
    many = 8 * span
    units = hidden_width // 8
    pw = units // PARTS
    hd2 = 2 * HD

    def hidden_cuts(t, u, c, part):
        out = []
        for j, i in enumerate(g.hidden_blocks(t, u, c)):
            lo, hi = max(j * rows_d, part * pw), min((j + 1) * rows_d, (part + 1) * pw)
            if lo < hi:
                out.append((i * rows_d + lo - j * rows_d, hi - lo))
        return out

    x_own = tokens[0].astype(F32)
    xn_own = rms_scale(x_own, g_in).astype(BF16)
    half_o = lax.dynamic_slice(w_o, (g.c * (rows_o // 2), 0), (rows_o // 2, width))
    half_d = lax.dynamic_slice(w_d, (g.c * (rows_d // 2), 0), (rows_d // 2, width))
    third = rows_d // 6
    seg_low = segments[0].astype(BF16)[None]
    seg_low = jnp.pad(seg_low, ((0, 15), (0, 0)))
    qkv_cuts, gu_cuts = [], []
    for dt, du in ORDER:
        t, u = g.t ^ dt, g.u ^ du
        kv = g.kv_head(t, u, g.c, rows_o)
        qkv_cuts.append([(2, kv * hd2, hd2), (3, kv * HD, HD), (4, kv * HD, HD)])
        gu_cuts.append(
            [
                (k, at, w)
                for part in range(PARTS)
                for k in (0, 1)
                for at, w in hidden_cuts(t, u, g.c, part)
            ]
        )
    cuts = [qkv_cuts[0], qkv_cuts[1], qkv_cuts[2] + gu_cuts[2], qkv_cuts[3]]
    cuts += [gu_cuts[0], gu_cuts[3] + gu_cuts[1]]
    cut = cut_columns([w_g, w_u, w_q, w_k, w_v], cuts, [seg_low] * 4 + [None] * 2)
    L = Live(qkv=cut[:4])
    S = Shards(g, L)
    S.fetch("o", [half_o])
    S.fetch("d", [half_d[k * third : (k + 1) * third] for k in range(3)], half_d)

    def done(*floating):
        new = lax.optimization_barrier({k: v for k, v in L.items() if k not in floating})
        L.update(new)

    def pairs(x):
        return [jnp.stack(x[:2]), jnp.stack(x[2:])]

    done()

    L.qkv = chips_swap(g, L.qkv)
    S.fetch_a(("o", 0))
    S.fetch_b(("o", 0, False))
    L.xn, L.cot = xn_own, cotangent[0]
    L.gu, L.gu_t, L.gu_f = cut[4], cut[5][:, : 2 * units], cut[5][:, 2 * units :]
    done()

    L.xn = gather_one(g, L.xn)
    L.gu_u = L.qkv[2][:rows_in, 4 * HD :]
    L.seg = [x[rows_in, :seq_len] for x in L.qkv]
    L.qkv = [x[:rows_in, : 4 * HD] for x in L.qkv]
    S.fetch("qkv", pairs(L.qkv))
    S.fetch_a(("qkv", 0))
    S.fetch_b(("qkv", 0, False), ("qkv", 1, False), ("o", 0, True))
    done()
    L.xn = gather_two(g, L.xn)
    S.fetch_a(("qkv", 1))
    S.fetch_b(("qkv", 0, True))
    L.gu_f = g.pt(L.gu_f, 1, 0)
    o_blocks = S.rows("o").reshape(2, 2, Q, rows_o // 2, width)
    L.o = (pick(o_blocks, g.u), pick(o_blocks, 1 - g.u))
    done()

    near = jnp.concatenate(L.xn)
    L.xn = (near, g.pc(near))
    L.gu_t = g.pt(L.gu_t, 1, 0)
    joined = rows_in == span
    if joined:
        L.gu_f = jnp.concatenate([L.cot, L.gu_f], axis=1)
    S.fetch_a(("d", 0))
    S.fetch_b(("qkv", 1, True))
    L.o = (L.o[0], g.px(L.o[1], g.umask))
    seg_all = jnp.stack(L.seg)
    index = lax.broadcasted_iota(jnp.int32, (4, seq_len), 1)
    earlier = seg_all[:, None, :] < seg_all[:, :, None]
    pos = index - jnp.sum(earlier.astype(jnp.int32), axis=-1)
    turn = lambda v: lax.dynamic_slice(
        jnp.concatenate([v, v], axis=1), (0, g.c * span), (4, seq_len)
    )
    index, pos, seg_own = turn(index), turn(pos).astype(F32), turn(seg_all)
    inv_freq = jnp.exp(jnp.arange(HD // 2, dtype=F32) * (-2.0 * math.log(ROPE_BASE) / HD))
    rotation = pos[:, :, None] * inv_freq
    cosines, sines = jnp.cos(rotation), jnp.sin(rotation)
    L.cosines = jnp.concatenate([cosines, cosines], axis=-1)
    L.sines = jnp.concatenate([-sines, sines], axis=-1)
    same_doc = (index[:, None, :] <= index[:, :, None]) & (
        seg_own[:, :, None] == seg_own[:, None, :]
    )
    L.mask = same_doc.astype(F32)
    done()

    def core_sum(own, sent):
        return own + g.pc(sent).astype(F32)

    def chip_blocks(x):
        return [x[k * span : (k + 1) * span] for k in range(4)]

    if joined:
        both = g.pt(L.gu_f, 0, 1)
        L.cot = (L.cot, both[:, :width], g.pt(L.cot, 1, 0))
        L.gu_f = both[:, width:]
    else:
        L.cot, L.gu_f = gather_one(g, L.cot), g.pt(L.gu_f, 0, 1)
    L.gu = [L.gu, L.gu_f, L.gu_u, L.gu_t]
    del L["gu_t"], L["gu_u"], L["gu_f"]
    S.fetch_a(("d", 1), ("d", 2))
    S.fetch_b_own("d")
    o_mine, o_next = L.o
    o_pair = jnp.where(g.u == 0, jnp.stack([o_mine, o_next]), jnp.stack([o_next, o_mine]))
    o_pair = o_pair.transpose(1, 2, 0, 3, 4)
    w_o_all = swap_halves(g, pick(o_pair, g.c), g.pc(pick(o_pair, 1 - g.c)))
    w_o_all = w_o_all.transpose(1, 2, 0, 3, 4).reshape(-1, width)
    rows, pieces = S.columns("qkv")
    *saved, att = attend(rows, pieces, *L.xn, L.cosines, L.sines, L.mask, gain_query, gain_key)
    L.part = project_out(att, w_o_all)
    done()

    L.part = core_sum(*L.part)
    for k in range(PARTS):
        pieces = [x[:, 2 * pw * k : 2 * pw * (k + 1)] for x in L.gu]
        S.fetch(f"gu{k + 1}", pairs(pieces), jnp.stack(pieces))
    del L["gu"]
    S.fetch_a(("gu1", 0))
    S.fetch_b(("d", 0, True), ("d", 1, True))
    done()

    L.part = scatter_one(g, chip_blocks(L.part))
    S.fetch_a(("gu1", 1))
    S.fetch_b(("d", 2, True))
    S.fetch_b_own("gu1")
    L.cot = gather_two_along_t(g, L.cot)
    done()
    L.part = scatter_two(g, L.part)
    S.fetch_a(("gu2", 0))
    S.fetch_b(("gu1", 0, True), ("gu1", 1, True))
    cot_near = jnp.concatenate(L.cot)
    L.cot = (cot_near, g.pc(cot_near))
    d_blocks = S.rows("d").reshape(A, 2, B // 2, rows_d // 2, width).transpose(1, 0, 2, 3, 4)
    L.d = (pick(d_blocks, g.c), pick(d_blocks, 1 - g.c))
    done()

    mid = x_own + add_all(L.part)
    xn2_own, post_back = jax.vjp(rms_scale, mid, g_post)
    L.xn2 = gather_one(g, xn2_own.astype(BF16))
    S.fetch_a(("gu2", 1))
    S.fetch_b_own("gu2")
    L.d = (L.d[0], g.pc(L.d[1]))
    done()
    L.xn2 = gather_two(g, L.xn2)
    S.fetch_a(("gu3", 0))
    S.fetch_b(("gu2", 0, True), ("gu2", 1, True))
    w_d_all = swap_halves(g, *L.d)
    L.w_d_all = w_d_all.transpose(1, 2, 0, 3, 4).reshape(-1, width)
    done()

    near = jnp.concatenate(L.xn2)
    L.xn2 = (near, g.pc(near))
    S.fetch_a(("gu3", 1))
    S.fetch_b_own("gu3")
    done()
    w_d_all = L.w_d_all

    rows_out = S.total_rows()

    def feed_part(part, before):
        name = f"gu{part + 1}"
        rows, pieces = S.columns(name)
        w_d_part = w_d_all[part * pw : (part + 1) * pw]
        hid, grad_d, grads, rest = feed(
            g, rows, rows_out, pieces, *L.xn2, *L.cot, w_d_part, before, part == PARTS - 1
        )
        S.total_split(name, grads)
        return (hid, grad_d), rest

    S.fetch_b(("gu3", 0, True), ("gu3", 1, True))
    L.one, L.rest = feed_part(0, ())
    done()

    S.total_b(("gu1", 0))
    S.prepare_a(("gu1", 0))
    L.two, L.rest = feed_part(1, L.rest)
    done()

    S.total_b(("gu1", 1))
    S.prepare_a(("gu1", 1))
    S.total_a(("gu1", 0))
    L.three, L.part = feed_part(2, L.rest)
    done()

    L.part = core_sum(*L.part)
    S.total_b(("gu2", 0))
    S.prepare_a(("gu2", 0))
    S.total_a(("gu1", 1))
    grad_d = jnp.concatenate([L.one[1], L.two[1], L.three[1]])
    grad_d = grad_d.reshape(A, B // 2, 2, rows_d // 2, width)
    grad_d = grad_d.transpose(2, 0, 1, 3, 4)
    L.d = (pick(grad_d, g.c), pick(grad_d, 1 - g.c))
    done()

    L.part = scatter_one(g, chip_blocks(L.part))
    S.total_b(("gu2", 1))
    S.prepare_a(("gu2", 1))
    S.total_a(("gu2", 0))
    S.finish("gu1")
    L.d = (L.d[0], g.pc(L.d[1]))
    L.hidden = jnp.concatenate([L.one[0], L.two[0], L.three[0]], axis=1)
    done()
    L.part = scatter_two(g, L.part)
    S.total_b(("gu3", 0))
    S.prepare_a(("gu3", 0))
    S.total_a(("gu2", 1))
    grad_d = swap_halves(g, *L.d).transpose(1, 0, 2, 3, 4).reshape(A, B, rows_d // 2, width)
    S.total("d", [grad_d[:, :, k * third : (k + 1) * third] for k in range(3)])
    L.out = project_out(L.hidden, w_d_all)
    done()

    d_post, grad_post = post_back(add_all(L.part))
    d_mid = cotangent[0].astype(F32) + d_post
    L.dmb = gather_one(g, d_mid.astype(BF16))
    S.total_b(("gu3", 1))
    S.prepare_a(("gu3", 1))
    S.total_a(("gu3", 0))
    S.finish("gu2")
    done()
    L.dmb = gather_two(g, L.dmb)
    S.total_b(("d", 0))
    S.prepare_a(("d", 0))
    S.total_a(("gu3", 1))
    L.out = core_sum(*L.out)
    done()

    near = jnp.concatenate(L.dmb)
    L.dmb = (near, g.pc(near))
    S.total_b(("d", 1))
    S.prepare_a(("d", 1))
    S.total_a(("d", 0))
    S.finish("gu3")
    out = chip_blocks(L.out)
    L.out = scatter_one(g, out)
    grads = [columns_pieces(g, L[f"gu{k + 1}"]) for k in range(PARTS)]
    L.gu = [jnp.concatenate(x, axis=1) for x in zip(*grads)]
    done()

    S.total_b(("d", 2))
    S.prepare_a(("d", 2))
    S.total_a(("d", 1))
    L.gu = chips_swap(g, L.gu)
    own, sent, grad_o, head_gains, grad_in, *grads = attend_back(
        g, rows_out, *L.dmb, w_o_all, att, saved, L.cosines, L.sines, gain_query, gain_key, *L.xn,
        rows_in,
    )
    L.part = (own, sent)
    L.gains = jnp.concatenate([grad_in[0] / g_in, grad_post, head_gains.reshape(-1)])
    grad_o = grad_o.reshape(Q, 2, rows_o, width).transpose(1, 0, 2, 3)
    L.o = (pick(grad_o, g.u), pick(grad_o, 1 - g.u))
    S.total_split("qkv", grads)
    done()

    L.part = core_sum(*L.part)
    S.total_b(("qkv", 0))
    S.prepare_a(("qkv", 0))
    S.total_a(("d", 2))
    L.o = (L.o[0], g.px(L.o[1], g.umask))
    own, to_u, to_t, relayed = L.out
    L.out = (own, to_u, g.pt((to_t + relayed.astype(F32)).astype(BF16), 1, 0))
    L.gains = L.gains + g.pc(L.gains)
    done()

    L.part = scatter_one(g, chip_blocks(L.part))
    S.total_b(("qkv", 1))
    S.total_a(("qkv", 0))
    S.finish("d")
    mine, other = L.o
    grad_o = jnp.where(g.u == 0, jnp.stack([mine, other]), jnp.stack([other, mine]))
    grad_o = grad_o.reshape(2, Q, 2, rows_o // 2, width).transpose(2, 0, 1, 3, 4)
    grad_o = swap_halves(g, pick(grad_o, g.c), g.pc(pick(grad_o, 1 - g.c)))
    grad_o = grad_o.transpose(1, 0, 2, 3, 4).reshape(A, B, rows_o // 2, width)
    S.total("o", [grad_o])
    S.prepare_a(("qkv", 1))
    bits = int(math.log2(g.n))
    for bit in range(bits // 2):
        L.gains = L.gains + g.px(L.gains, 1 << bit)
    done()
    L.part = scatter_two(g, L.part)
    for bit in range(bits // 2, bits - 1):
        L.gains = L.gains + g.px(L.gains, 1 << bit)
    S.total_b(("o", 0))
    S.total_a(("qkv", 1))
    S.prepare_a(("o", 0))
    S.finish("qkv")
    L.gu = (L.gu, g.pc(jnp.stack(L.gu)))
    d_sum = jnp.concatenate([L.d[k] for k in range(3)])
    L.d = d_sum
    done()

    def both_cores(pair):
        near, far = pair
        return list(near) + [far[k] for k in range(4)]

    pieces, places = both_cores(L.gu), []
    for part in range(PARTS):
        for j, piece in enumerate(pieces):
            dt, du = ORDER[j % 4]
            at = 2 * pw * part
            for to, w in hidden_cuts(g.t ^ dt, g.u ^ du, g.c ^ (j // 4), part):
                places += [
                    (j, at, w, 0, to),
                    (j, pw + at, w, 1, to),
                ]
                at += w
    L.gate, L.up = place_columns(pieces, [hidden_width, hidden_width], places)
    S.total_a(("o", 0))
    L.qkv = chips_swap(g, columns_pieces(g, L.qkv))
    own, to_u, from_t = L.out
    L.out = (own, g.pt(to_u.astype(BF16), 0, 1), from_t)
    _, in_back = jax.vjp(lambda x: rms_scale(x, g_in), x_own)
    L.d_tokens = (d_mid + in_back(add_all(L.part))[0]).astype(BF16)
    done("out")

    L.d = swap_halves(g, L.d, g.pc(L.d)).reshape(1, rows_d, width).astype(F32)
    gains = (L.gains + g.px(L.gains, 1 << (bits - 1)))[None]
    S.finish("o")
    L.qkv = (L.qkv, g.pc(jnp.stack(L.qkv)))
    grad_output = swap_halves(g, L.o[0], g.pc(L.o[0])).reshape(1, rows_o, width).astype(F32)
    activations = (mid + add_all(L.out)).astype(BF16)
    d_tokens = L.d_tokens

    pieces = both_cores(L.qkv)
    places = []
    for j, piece in enumerate(pieces):
        dt, du = ORDER[j % 4]
        kv = g.kv_head(g.t ^ dt, g.u ^ du, g.c ^ (j // 4), rows_o)
        places += [
            (j, 0, hd2, 0, kv * hd2),
            (j, hd2, HD, 1, kv * HD),
            (j, hd2 + HD, HD, 2, kv * HD),
        ]
    grad_query, grad_key, grad_value = place_columns(pieces, [q_width, kv_width, kv_width], places)

    return (
        activations[None],
        d_tokens[None],
        grad_query[None],
        grad_key[None],
        grad_value[None],
        grad_output,
        L.gate[None],
        L.up[None],
        L.d,
        gains[:, :width],
        gains[:, 2 * width : 2 * width + HD],
        gains[:, 2 * width + HD :],
        gains[:, width : 2 * width],
    )


def solution(mesh):
    rows = P("fsdp", "rep", None)
    cut_rows = P(None, "fsdp", None)
    return jax.shard_map(
        functools.partial(per_device, Grid(mesh)),
        mesh=mesh,
        in_specs=(rows, P("fsdp", None), rows) + (cut_rows,) * 7 + (P(),) * 4,
        out_specs=(rows, rows) + (cut_rows,) * 7 + (P(),) * 4,
        check_vma=False,
    )
```

```python
import functools
import math

import jax
import jax.numpy as jnp
from jax import lax
from jax.experimental import pallas as pl
from jax.experimental.pallas import tpu as pltpu
from jax.sharding import PartitionSpec as P

HD = 128
NORM_EPS = 1e-06
NEG_FILL = -1e30
ROPE_BASE = 1000000.0
BF16 = jnp.bfloat16
F32 = jnp.float32


def dot(x, y):
    return jnp.dot(x, y, preferred_element_type=F32)


def dot_tn(x, y):
    return lax.dot_general(x, y, (((0,), (0,)), ((), ())), preferred_element_type=F32)


def dot_nt(x, y):
    return lax.dot_general(x, y, (((1,), (1,)), ((), ())), preferred_element_type=F32)


def rms_scale(v, gain):
    return v * lax.rsqrt(jnp.mean(v * v, axis=-1, keepdims=True) + NORM_EPS) * gain


class Grid:
    def __init__(self, mesh):
        n = mesh.shape["fsdp"]
        assert mesh.shape["rep"] == 2 and n % 16 == 0 and n & (n - 1) == 0
        self.n = n
        self.F = n // 4
        self.B = 2 ** (int(math.log2(self.F)) // 2)
        self.A = self.F // self.B
        self.Q = self.F // 4
        self.tmask, self.umask = 2 * self.B, 1

    def place(self):
        i = lax.axis_index("fsdp")
        self.u = i % 2
        self.b = (i // 2) % self.B
        self.t = (i // (2 * self.B)) % 2
        self.a = i // (4 * self.B)
        self.c = lax.axis_index("rep")

    def px(self, x, mask):
        return lax.ppermute(x, "fsdp", [(i, i ^ mask) for i in range(self.n)])

    def pc(self, x):
        return lax.ppermute(x, "rep", [(0, 1), (1, 0)])

    def pa(self, x, delta):
        return self.px(x, 4 * self.B * delta)

    def pb(self, x, delta):
        return self.px(x, 2 * delta)

    def pt(self, x, dt, du):
        return self.px(x, dt * self.tmask + du * self.umask)

    def kv_head(self, t, u, c, rows):
        first = (u * 2 + c) * self.Q
        block = ((first // self.B * 2 + t) * self.B + first % self.B) * 2
        return block * rows // (2 * HD)

    def hidden_blocks(self, t, u, c):
        half = self.B // 2
        return [
            ((a * 2 + t) * self.B + c * half + b) * 2 + u
            for a in range(self.A)
            for b in range(half)
        ]


SHIFTS = ((1, 1), (0, 1), (1, 0))


def pick(x, *index):
    lead = len(index)
    starts = list(index) + [0] * (x.ndim - lead)
    sizes = [1] * lead + list(x.shape[lead:])
    return lax.dynamic_slice(x, starts, sizes).reshape(x.shape[lead:])


def put(x, piece, *index):
    lead = len(index)
    starts = list(index) + [0] * (x.ndim - lead)
    return lax.dynamic_update_slice(x, piece.reshape((1,) * lead + x.shape[lead:]), starts)


def swap_halves(g, own, other):
    return jnp.where(g.c == 0, jnp.stack([own, other]), jnp.stack([other, own]))


class Live(dict):
    __getattr__ = dict.__getitem__
    __setattr__ = dict.__setitem__


ORDER = ((0, 0),) + SHIFTS
LANES = 128


def cut_columns(sources, pieces, tail):
    rows = sources[0].shape[0]
    cuts = [cut for piece in pieces for cut in piece]
    widths = [sum(w for _, _, w in piece) for piece in pieces]
    heights = [rows if rest is None else rows + rest.shape[0] for rest in tail]
    if any(c[2] % LANES for c in cuts) or rows % 16:
        out = [
            jnp.concatenate(
                [lax.dynamic_slice(sources[k], (0, at), (rows, w)) for k, at, w in piece], axis=1
            )
            for piece in pieces
        ]
        return [
            x if rest is None else jnp.concatenate([x, jnp.pad(rest, ((0, 0), (0, w - rest.shape[1])))])
            for x, rest, w in zip(out, tail, widths)
        ]
    (rest,) = {id(x): x for x in tail if x is not None}.values()

    def kernel(at_ref, *refs):
        ins, rest_ref, outs = refs[: len(sources)], refs[len(sources)], refs[len(sources) + 1 :]
        j = 0
        for out, piece, height in zip(outs, pieces, heights):
            to = 0
            for k, _, w in piece:
                start = pl.multiple_of(at_ref[j] * LANES, LANES)
                out[:rows, to : to + w] = ins[k][:, pl.ds(start, w)]
                to += w
                j += 1
            if height > rows:
                out[rows:, :] = jnp.zeros((height - rows, to), out.dtype)
                out[rows:, : rest.shape[1]] = rest_ref[...]

    vmem = pl.BlockSpec(memory_space=pltpu.VMEM)
    return pl.pallas_call(
        kernel,
        in_specs=[pl.BlockSpec(memory_space=pltpu.SMEM)] + [vmem] * (len(sources) + 1),
        out_specs=[vmem] * len(pieces),
        out_shape=[
            jax.ShapeDtypeStruct(shape, sources[0].dtype) for shape in zip(heights, widths)
        ],
        compiler_params=pltpu.CompilerParams(vmem_limit_bytes=10 << 20),
        name="cut_columns",
    )(jnp.stack([jnp.asarray(at // LANES, jnp.int32) for _, at, _ in cuts]), *sources, rest)


def place_columns(pieces, widths, places):
    rows = pieces[0].shape[0]
    if any(p[2] % LANES or p[1] % LANES for p in places) or rows % 16:
        outs = [jnp.zeros((rows, w), F32) for w in widths]
        for k, at, w, o, to in places:
            part = pieces[k][:, at : at + w].astype(F32)
            outs[o] = lax.dynamic_update_slice(outs[o], part, (0, to))
        return outs

    def kernel(to_ref, *refs):
        ins, outs = refs[: len(pieces)], refs[len(pieces) :]
        for j, (k, at, w, o, _) in enumerate(places):
            start = pl.multiple_of(to_ref[j] * LANES, LANES)
            outs[o][:, pl.ds(start, w)] = ins[k][:, at : at + w].astype(F32)

    vmem = pl.BlockSpec(memory_space=pltpu.VMEM)
    return pl.pallas_call(
        kernel,
        in_specs=[pl.BlockSpec(memory_space=pltpu.SMEM)] + [vmem] * len(pieces),
        out_specs=[vmem] * len(widths),
        out_shape=[jax.ShapeDtypeStruct((rows, w), F32) for w in widths],
        compiler_params=pltpu.CompilerParams(vmem_limit_bytes=10 << 20),
        name="place_columns",
    )(jnp.stack([jnp.asarray(to // LANES, jnp.int32) for *_, to in places]), *pieces)


def chips_swap(g, pieces):
    return [pieces[0]] + [g.pt(x, dt, du) for x, (dt, du) in zip(pieces[1:], SHIFTS)]


def gather_one(g, x):
    return x, g.pt(x, 0, 1), g.pt(x, 1, 0)


def gather_two(g, near):
    own, along_u, along_t = near
    return [own, g.pt(along_t, 0, 1), along_u, along_t]


def gather_two_along_t(g, near):
    own, along_u, along_t = near
    return [own, g.pt(along_u, 1, 0), along_u, along_t]


def scatter_one(g, blocks):
    own, far, to_u, to_t = blocks
    return own, to_u, to_t, g.pt(far.astype(BF16), 0, 1)


def scatter_two(g, state):
    own, to_u, to_t, relayed = state
    return (
        own,
        g.pt(to_u.astype(BF16), 0, 1),
        g.pt((to_t + relayed.astype(F32)).astype(BF16), 1, 0),
    )


def add_all(pieces):
    total = pieces[0]
    for x in pieces[1:]:
        total = total + x.astype(F32)
    return total


def permute_joined(permute, arrays):
    out = [None] * len(arrays)
    for n in sorted({x.shape[-1] for x in arrays}):
        which = [k for k, x in enumerate(arrays) if x.shape[-1] == n]
        flat = [arrays[k].reshape(-1, n) for k in which]
        got = permute(jnp.concatenate(flat) if len(flat) > 1 else flat[0])
        at = 0
        for k, x in zip(which, flat):
            out[k] = got[at : at + x.shape[0]].reshape(arrays[k].shape)
            at += x.shape[0]
    return out


class Shards:
    def __init__(self, g, live):
        self.g, self.live = g, live

    def fetch(self, name, parts, whole=None):
        self.live[name] = {(p, 0, 0): x for p, x in enumerate(parts)}
        if whole is not None:
            self.live[name + "_whole"] = whole

    def fetch_b_own(self, name):
        whole = self.live.pop(name + "_whole")
        own = {p: x for (p, d, e), x in self.live[name].items() if d == e == 0}
        for e in range(1, self.g.B):
            got, at = self.g.pb(whole, e), 0
            for p in sorted(own):
                rows = own[p].shape[0]
                self.live[name] = {**self.live[name], (p, 0, e): got[at : at + rows]}
                at += rows

    def fetch_a(self, *jobs):
        for d in range(1, self.g.A):
            got = permute_joined(
                lambda x, d=d: self.g.pa(x, d), [self.live[n][p, 0, 0] for n, p in jobs]
            )
            for (n, p), x in zip(jobs, got):
                self.live[n] = {**self.live[n], (p, d, 0): x}

    def fetch_b(self, *jobs):
        jobs = [
            (n, p, d) for n, p, rest in jobs for d in (range(1, self.g.A) if rest else (0,))
        ]
        for e in range(1, self.g.B):
            got = permute_joined(
                lambda x, e=e: self.g.pb(x, e), [self.live[n][p, d, 0] for n, p, d in jobs]
            )
            for (n, p, d), x in zip(jobs, got):
                self.live[n] = {**self.live[n], (p, d, e): x}

    def total(self, name, parts):
        g = self.g
        self.live[name] = {}
        for p, x in enumerate(parts):
            by_b = x.swapaxes(0, 1)
            sent = [pick(by_b, g.b ^ e).astype(BF16) for e in range(1, g.B)]
            self.live[name][p] = (pick(by_b, g.b), sent)

    def total_b(self, *jobs):
        g = self.g
        got = [
            permute_joined(lambda x, e=e: g.pb(x, e), [self.live[n][p][1][e - 1] for n, p in jobs])
            for e in range(1, g.B)
        ]
        for k, (n, p) in enumerate(jobs):
            self.live[n] = {**self.live[n], p: (self.live[n][p][0], [x[k] for x in got])}

    def prepare_a(self, *jobs):
        g = self.g
        for n, p in jobs:
            kept, got = self.live[n][p]
            rows = add_all([kept.astype(F32)] + got)
            sent = [pick(rows, g.a ^ d).astype(BF16) for d in range(1, g.A)]
            self.live[n] = {**self.live[n], p: (pick(rows, g.a), sent)}

    def total_a(self, *jobs):
        g = self.g
        got = [
            permute_joined(lambda x, d=d: g.pa(x, d), [self.live[n][p][1][d - 1] for n, p in jobs])
            for d in range(1, g.A)
        ]
        for k, (n, p) in enumerate(jobs):
            self.live[n] = {**self.live[n], p: (self.live[n][p][0], [x[k] for x in got])}

    def finish(self, *names):
        for n in names:
            self.live[n] = {
                p: add_all([kept] + got).astype(BF16) for p, (kept, got) in self.live[n].items()
            }

    def rows(self, name):
        g, state = self.g, self.live[name]
        parts = 1 + max(p for p, _, _ in state)
        height = [state[p, 0, 0].shape[0] for p in range(parts)]
        out = jnp.zeros((g.A, g.B, sum(height)) + state[0, 0, 0].shape[1:], BF16)
        for (p, d, e), x in state.items():
            starts = [g.a ^ d, g.b ^ e, sum(height[:p])] + [0] * (x.ndim - 1)
            out = lax.dynamic_update_slice(out, x[None, None], starts)
        return out

    def columns(self, name):
        g, state = self.g, self.live[name]
        pieces, rows = [], []
        for (p, d, e), x in state.items():
            pieces.append(x)
            for k in range(2):
                dt, du = ORDER[2 * p + k]
                rows.append(
                    (((g.a ^ d) * 2 + (g.t ^ dt)) * g.B + (g.b ^ e)) * 2 + (g.u ^ du)
                )
        return jnp.stack(rows).astype(jnp.int32), pieces

    def total_rows(self):
        g = self.g
        return jnp.stack(
            [
                (a * 2 + t) * g.B + (g.b ^ e)
                for t in range(2)
                for e in range(g.B)
                for a in range(g.A)
            ]
        ).astype(jnp.int32)

    def total_split(self, name, arrays):
        n = self.g.B
        self.live[name] = {p: (arrays[p * n], arrays[p * n + 1 : (p + 1) * n]) for p in range(2)}


def columns_pieces(g, state):
    both = jnp.stack([state[0], state[1]])
    return [pick(both, g.t ^ dt, g.u ^ du) for dt, du in ORDER]


def kernel_call(kernel, ins, outs, scratch, name):
    vmem = pl.BlockSpec(memory_space=pltpu.VMEM)
    smem = pl.BlockSpec(memory_space=pltpu.SMEM)
    return pl.pallas_call(
        kernel,
        in_specs=[smem if x.dtype == jnp.int32 else vmem for x in ins],
        out_specs=[vmem] * len(outs),
        out_shape=[jax.ShapeDtypeStruct(shape, dtype) for shape, dtype in outs],
        scratch_shapes=[pltpu.VMEM(shape, dtype) for shape, dtype in scratch],
        compiler_params=pltpu.CompilerParams(vmem_limit_bytes=16 << 20),
        cost_estimate=pl.CostEstimate(flops=1 << 20, bytes_accessed=1 << 16, transcendentals=0),
        name=name,
    )(*ins)


def join_rows(rows_ref, pieces, whole):
    height = pieces[0].shape[1]
    for j, piece in enumerate(pieces):
        for k in range(2):
            at = pl.multiple_of(rows_ref[2 * j + k] * height, height)
            whole[pl.ds(at, height), :] = piece[k]


def split_rows(rows_ref, whole, outs):
    j = 0
    for out in outs:
        count, height = out.shape[0], out.shape[1] * out.shape[2]
        for k in range(count):
            at = pl.multiple_of(rows_ref[j] * height, height)
            out[k] = whole[pl.ds(at, height), :].reshape(out.shape[1:])
            j += 1


BLOCK = 512


def over_rows(near, far, body):
    for part, ref in enumerate((near, far)):

        @pl.loop(0, ref.shape[0] // BLOCK)
        def _(j, part=part, ref=ref):
            at = pl.multiple_of(j * BLOCK, BLOCK)
            body(part, at, pl.multiple_of(part * ref.shape[0] + at, BLOCK), ref[pl.ds(at, BLOCK), :])


def grad_rows(near, far, right, whole):
    half = near.shape[0]

    @pl.loop(0, near.shape[1] // BLOCK)
    def _(j):
        at = pl.multiple_of(j * BLOCK, BLOCK)
        cols = pl.ds(at, BLOCK)
        whole[cols, :] = (
            dot_tn(near[:, cols], right[:half, :]) + dot_tn(far[:, cols], right[half:, :])
        ).astype(BF16)


def turn_half(x):
    return pltpu.roll(x, HD // 2, 1)


SCALE = 1.0 / math.sqrt(HD)


def attend(rows, pieces, near, far, cosines, sines, mask, g_q, g_k):
    many, span = 2 * near.shape[0], near.shape[0] // 4
    width = near.shape[1]

    def kernel(rows_ref, *refs):
        ws, refs = refs[: len(pieces)], refs[len(pieces) :]
        near, far, cos_ref, sin_ref, mask_ref, gq_ref, gk_ref = refs[:7]
        w_ref, raw_ref, q_ref, k_ref, v_ref, p_ref, att_ref, qkv_ref = refs[7:]
        join_rows(rows_ref, ws, w_ref)

        def project(part, at, row, x):
            qkv_ref[pl.ds(row, BLOCK), :] = dot(x, w_ref[...])

        over_rows(near, far, project)
        raw_ref[...] = qkv_ref[:, : 3 * HD]

        @pl.loop(0, 4)
        def _(k):
            own = pl.ds(pl.multiple_of(k * span, span), span)
            other = pl.ds(pl.multiple_of(4 * span + k * span, span), span)
            x = jnp.concatenate([qkv_ref[own, :], qkv_ref[other, :]])
            cos, sin = cos_ref[k], sin_ref[k]

            def head(u, gain):
                u = u * lax.rsqrt(jnp.mean(u * u, axis=-1, keepdims=True) + NORM_EPS) * gain
                return (u * cos + turn_half(u) * sin).astype(BF16)

            key = head(x[:, 2 * HD : 3 * HD], gk_ref[...])
            val = x[:, 3 * HD :].astype(BF16)
            k_ref[k] = key
            v_ref[k] = val
            for h in range(2):
                cols = slice(h * HD, (h + 1) * HD)
                query = head(x[:, cols], gq_ref[...])
                q_ref[k, :, cols] = query
                scores = jnp.where(mask_ref[k] > 0, dot_nt(query, key) * SCALE, NEG_FILL)
                expo = jnp.exp(scores - jnp.max(scores, axis=-1, keepdims=True))
                probs = expo / jnp.sum(expo, axis=-1, keepdims=True)
                p_ref[k, h] = probs
                att = dot(probs.astype(BF16), val).astype(BF16)
                att_ref[own, cols] = att[:span]
                att_ref[other, cols] = att[span:]

    seq = 2 * span
    outs = [
        ((width, 4 * HD), BF16), ((many, 3 * HD), F32), ((4, seq, 2 * HD), BF16),
        ((4, seq, HD), BF16), ((4, seq, HD), BF16), ((4, 2, seq, seq), F32), ((many, 2 * HD), BF16),
    ]
    ins = [rows, *pieces, near, far, cosines, sines, mask, g_q, g_k]
    return kernel_call(kernel, ins, outs, [((many, 4 * HD), F32)], "attend")


def attend_back(g, rows_out, near_d, far_d, w_o, att, saved, cosines, sines, g_q, g_k, near, far, rows_in):
    w_qkv, raw, q, k, v, probs = saved
    many, span = 2 * near.shape[0], near.shape[0] // 4
    width = near.shape[1]
    parts = 2 * g.B

    def kernel(rows_ref, *refs):
        near_d, far_d, wo_ref, att_ref, w_ref, raw_ref, q_ref, k_ref, v_ref, p_ref = refs[:10]
        cos_ref, sin_ref, gq_ref, gk_ref, near, far = refs[10:16]
        own_ref, sent_ref, go_ref, gain_ref, in_ref = refs[16:21]
        outs, (datt_ref, dqkv_ref, whole_ref) = refs[21 : 21 + parts], refs[21 + parts :]

        def project(part, at, row, x):
            datt_ref[pl.ds(row, BLOCK), :] = dot_nt(x, wo_ref[...]).astype(BF16)

        over_rows(near_d, far_d, project)
        gain_ref[...] = jnp.zeros_like(gain_ref)

        @pl.loop(0, 4)
        def _(s):
            own = pl.ds(pl.multiple_of(s * span, span), span)
            other = pl.ds(pl.multiple_of(4 * span + s * span, span), span)
            cos, sin = cos_ref[s], sin_ref[s]
            key, val = k_ref[s], v_ref[s]
            d_val = d_key = None

            def put_back(cols, x):
                x = x.astype(BF16)
                dqkv_ref[own, cols] = x[:span]
                dqkv_ref[other, cols] = x[span:]

            def head_back(cot, cols, gain, which):
                x = jnp.concatenate([raw_ref[own, cols], raw_ref[other, cols]])
                r = lax.rsqrt(jnp.mean(x * x, axis=-1, keepdims=True) + NORM_EPS)
                d_norm = cot * cos + turn_half(cot * sin)
                x = x * r
                gain_ref[which : which + 1, :] += jnp.sum(d_norm * x, axis=0, keepdims=True)
                d_norm = d_norm * gain
                put_back(cols, r * (d_norm - x * jnp.mean(d_norm * x, axis=-1, keepdims=True)))

            for h in range(2):
                cols = slice(h * HD, (h + 1) * HD)
                d_att = jnp.concatenate([datt_ref[own, cols], datt_ref[other, cols]])
                probs = p_ref[s, h]
                query = q_ref[s, :, cols]
                dv = dot_tn(probs.astype(BF16), d_att)
                dp = dot_nt(d_att, val)
                ds = probs * (dp - jnp.sum(probs * dp, axis=-1, keepdims=True)) * SCALE
                ds = ds.astype(BF16)
                dk = dot_tn(ds, query)
                d_val = dv if d_val is None else d_val + dv
                d_key = dk if d_key is None else d_key + dk
                head_back(dot(ds, key), cols, gq_ref[...], 0)
            head_back(d_key, slice(2 * HD, 3 * HD), gk_ref[...], 1)
            put_back(slice(3 * HD, 4 * HD), d_val)

        half = many // 2

        in_ref[...] = jnp.zeros_like(in_ref)

        def inward(part, at, row, x):
            d_xn = dot_nt(dqkv_ref[pl.ds(row, BLOCK), :], w_ref[...])
            in_ref[...] += jnp.sum(d_xn * x.astype(F32), axis=0, keepdims=True)
            out = sent_ref if part else own_ref
            out[pl.ds(at, BLOCK), :] = d_xn.astype(out.dtype)

        over_rows(near, far, inward)
        grad_rows(near, far, dqkv_ref, whole_ref)
        split_rows(rows_ref, whole_ref, outs)

        @pl.loop(0, width // BLOCK)
        def _(j):
            cols = pl.ds(pl.multiple_of(j * BLOCK, BLOCK), BLOCK)
            go_ref[:, cols] = (
                dot_tn(att_ref[:half, :], near_d[:, cols])
                + dot_tn(att_ref[half:, :], far_d[:, cols])
            ).astype(BF16)

    outs = [
        ((many // 2, width), F32), ((many // 2, width), BF16), ((2 * HD, width), BF16), ((2, HD), F32),
        ((1, width), F32),
    ]
    outs += [((g.A, 2, rows_in, 4 * HD), BF16)] * parts
    scratch = [((many, 2 * HD), BF16), ((many, 4 * HD), BF16), ((width, 4 * HD), BF16)]
    ins = [rows_out, near_d, far_d, w_o, att, w_qkv, raw, q, k, v, probs]
    ins += [cosines, sines, g_q, g_k, near, far]
    return kernel_call(kernel, ins, outs, scratch, "attend_back")


def feed(g, rows, rows_out, pieces, near, far, near_d, far_d, w_d, before, last):
    many, width = 2 * near.shape[0], near.shape[1]
    pw, rows_in = w_d.shape[0], pieces[0].shape[1]
    parts = 2 * g.B
    half = many // 2

    def kernel(rows_ref, rows_out_ref, *refs):
        ws, refs = refs[: len(pieces)], refs[len(pieces) :]
        near, far, near_d, far_d, wd_ref = refs[:5]
        given, refs = refs[5 : 5 + len(before)], refs[5 + len(before) :]
        hid_ref, gd_ref = refs[:2]
        outs, refs = refs[2 : 2 + parts], refs[2 + parts :]
        if len(before) == 0:
            (dgu_ref, w_ref), refs = refs[:2], refs[2:]
            dx = None
        else:
            dx, refs = refs[:2], refs[2:]
            (dgu_ref, w_ref), refs = refs[-2:], refs[:-2]
        (whole_ref,) = refs
        join_rows(rows_ref, ws, w_ref)

        def one(part, at, row, x):
            both = dot(x, w_ref[...])
            gate, up = both[:, :pw], both[:, pw:]
            d_ref = far_d if part else near_d
            dh = dot_nt(d_ref[pl.ds(at, BLOCK), :], wd_ref[...])
            sig = jax.nn.sigmoid(gate)
            lit = gate * sig
            rows = pl.ds(row, BLOCK)
            hid_ref[rows, :] = (lit * up).astype(BF16)
            dgu_ref[rows, pw:] = (dh * lit).astype(BF16)
            dgu_ref[rows, :pw] = (dh * up * sig * (1.0 + gate * (1.0 - sig))).astype(BF16)
            if dx is not None:
                total = dot_nt(dgu_ref[rows, :], w_ref[...])
                if last:
                    total = total + given[part][pl.ds(at, BLOCK), :]
                else:
                    total = total + dot_nt(given[0][rows, :], given[1][...])
                dx[part][pl.ds(at, BLOCK), :] = total.astype(dx[part].dtype)

        over_rows(near, far, one)
        grad_rows(near, far, dgu_ref, whole_ref)
        split_rows(rows_out_ref, whole_ref, outs)

        @pl.loop(0, width // BLOCK)
        def _(j):
            cols = pl.ds(pl.multiple_of(j * BLOCK, BLOCK), BLOCK)
            gd_ref[:, cols] = (
                dot_tn(hid_ref[:half, :], near_d[:, cols])
                + dot_tn(hid_ref[half:, :], far_d[:, cols])
            ).astype(BF16)

    outs = [((many, pw), BF16), ((pw, width), BF16)]
    outs += [((g.A, 2, rows_in, 2 * pw), BF16)] * parts
    local = [((many, 2 * pw), BF16), ((width, 2 * pw), BF16)]
    whole = [((width, 2 * pw), BF16)]
    if len(before) == 0:
        outs, scratch = outs + local, whole
    else:
        outs += [((half, width), F32), ((half, width), BF16 if last else F32)]
        scratch = whole + local
    ins = [rows, rows_out, *pieces, near, far, near_d, far_d, w_d, *before]
    got = kernel_call(kernel, ins, outs, scratch, "feed")
    return got[0], got[1], got[2 : 2 + parts], got[2 + parts :]


def project_out(x, w):
    half, width = x.shape[0] // 2, w.shape[1]

    def kernel(x_ref, w_ref, own_ref, sent_ref):
        @pl.loop(0, half // BLOCK)
        def _(j):
            at = pl.ds(pl.multiple_of(j * BLOCK, BLOCK), BLOCK)
            own_ref[at, :] = dot(x_ref[at, :], w_ref[...])
            low = pl.ds(pl.multiple_of(half + j * BLOCK, BLOCK), BLOCK)
            sent_ref[at, :] = dot(x_ref[low, :], w_ref[...]).astype(BF16)

    outs = [((half, width), F32), ((half, width), BF16)]
    return kernel_call(kernel, [x, w], outs, [], "project_out")


PARTS = 3


def per_device(
    g,
    tokens,
    segments,
    cotangent,
    w_query,
    w_key,
    w_value,
    w_output,
    w_gate,
    w_up,
    w_down,
    gain_in,
    gain_query,
    gain_key,
    gain_post,
):
    g.place()
    A, B, Q = g.A, g.B, g.Q
    _, span, width = tokens.shape
    seq_len = segments.shape[1]
    w_q, w_k, w_v, w_o, w_g, w_u, w_d = (
        w[0] for w in (w_query, w_key, w_value, w_output, w_gate, w_up, w_down)
    )
    rows_in, rows_o, rows_d = w_q.shape[0], w_o.shape[0], w_d.shape[0]
    q_width, kv_width, hidden_width = w_q.shape[1], w_k.shape[1], w_g.shape[1]
    g_in, g_q, g_k, g_post = gain_in[0], gain_query[0], gain_key[0], gain_post[0]
    many = 8 * span
    units = hidden_width // 8
    pw = units // PARTS
    hd2 = 2 * HD

    def hidden_cuts(t, u, c, part):
        out = []
        for j, i in enumerate(g.hidden_blocks(t, u, c)):
            lo, hi = max(j * rows_d, part * pw), min((j + 1) * rows_d, (part + 1) * pw)
            if lo < hi:
                out.append((i * rows_d + lo - j * rows_d, hi - lo))
        return out

    x_own = tokens[0].astype(F32)
    xn_own = rms_scale(x_own, g_in).astype(BF16)
    half_o = lax.dynamic_slice(w_o, (g.c * (rows_o // 2), 0), (rows_o // 2, width))
    half_d = lax.dynamic_slice(w_d, (g.c * (rows_d // 2), 0), (rows_d // 2, width))
    third = rows_d // 6
    seg_low = segments[0].astype(BF16)[None]
    seg_low = jnp.pad(seg_low, ((0, 15), (0, 0)))
    qkv_cuts, gu_cuts = [], []
    for dt, du in ORDER:
        t, u = g.t ^ dt, g.u ^ du
        kv = g.kv_head(t, u, g.c, rows_o)
        qkv_cuts.append([(2, kv * hd2, hd2), (3, kv * HD, HD), (4, kv * HD, HD)])
        gu_cuts.append(
            [
                (k, at, w)
                for part in range(PARTS)
                for k in (0, 1)
                for at, w in hidden_cuts(t, u, g.c, part)
            ]
        )
    cuts = [qkv_cuts[0], qkv_cuts[1], qkv_cuts[2] + gu_cuts[2], qkv_cuts[3]]
    cuts += [gu_cuts[0], gu_cuts[3] + gu_cuts[1]]
    cut = cut_columns([w_g, w_u, w_q, w_k, w_v], cuts, [seg_low] * 4 + [None] * 2)
    L = Live(qkv=cut[:4])
    S = Shards(g, L)
    S.fetch("o", [half_o])
    S.fetch("d", [half_d[k * third : (k + 1) * third] for k in range(3)], half_d)

    def done(*floating):
        new = lax.optimization_barrier({k: v for k, v in L.items() if k not in floating})
        L.update(new)

    def pairs(x):
        return [jnp.stack(x[:2]), jnp.stack(x[2:])]

    done()

    L.qkv = chips_swap(g, L.qkv)
    S.fetch_a(("o", 0))
    S.fetch_b(("o", 0, False))
    L.xn, L.cot = xn_own, cotangent[0]
    L.gu, L.gu_t, L.gu_f = cut[4], cut[5][:, : 2 * units], cut[5][:, 2 * units :]
    done()

    L.xn = gather_one(g, L.xn)
    L.gu_u = L.qkv[2][:rows_in, 4 * HD :]
    L.seg = [x[rows_in, :seq_len] for x in L.qkv]
    L.qkv = [x[:rows_in, : 4 * HD] for x in L.qkv]
    S.fetch("qkv", pairs(L.qkv))
    S.fetch_a(("qkv", 0))
    S.fetch_b(("qkv", 0, False), ("qkv", 1, False), ("o", 0, True))
    done()
    L.xn = gather_two(g, L.xn)
    S.fetch_a(("qkv", 1))
    S.fetch_b(("qkv", 0, True))
    L.gu_f = g.pt(L.gu_f, 1, 0)
    o_blocks = S.rows("o").reshape(2, 2, Q, rows_o // 2, width)
    L.o = (pick(o_blocks, g.u), pick(o_blocks, 1 - g.u))
    done()

    near = jnp.concatenate(L.xn)
    L.xn = (near, g.pc(near))
    L.gu_t = g.pt(L.gu_t, 1, 0)
    joined = rows_in == span
    if joined:
        L.gu_f = jnp.concatenate([L.cot, L.gu_f], axis=1)
    S.fetch_a(("d", 0))
    S.fetch_b(("qkv", 1, True))
    L.o = (L.o[0], g.px(L.o[1], g.umask))
    seg_all = jnp.stack(L.seg)
    index = lax.broadcasted_iota(jnp.int32, (4, seq_len), 1)
    earlier = seg_all[:, None, :] < seg_all[:, :, None]
    pos = index - jnp.sum(earlier.astype(jnp.int32), axis=-1)
    turn = lambda v: lax.dynamic_slice(
        jnp.concatenate([v, v], axis=1), (0, g.c * span), (4, seq_len)
    )
    index, pos, seg_own = turn(index), turn(pos).astype(F32), turn(seg_all)
    inv_freq = jnp.exp(jnp.arange(HD // 2, dtype=F32) * (-2.0 * math.log(ROPE_BASE) / HD))
    rotation = pos[:, :, None] * inv_freq
    cosines, sines = jnp.cos(rotation), jnp.sin(rotation)
    L.cosines = jnp.concatenate([cosines, cosines], axis=-1)
    L.sines = jnp.concatenate([-sines, sines], axis=-1)
    same_doc = (index[:, None, :] <= index[:, :, None]) & (
        seg_own[:, :, None] == seg_own[:, None, :]
    )
    L.mask = same_doc.astype(F32)
    done()

    def core_sum(own, sent):
        return own + g.pc(sent).astype(F32)

    def chip_blocks(x):
        return [x[k * span : (k + 1) * span] for k in range(4)]

    if joined:
        both = g.pt(L.gu_f, 0, 1)
        L.cot = (L.cot, both[:, :width], g.pt(L.cot, 1, 0))
        L.gu_f = both[:, width:]
    else:
        L.cot, L.gu_f = gather_one(g, L.cot), g.pt(L.gu_f, 0, 1)
    L.gu = [L.gu, L.gu_f, L.gu_u, L.gu_t]
    del L["gu_t"], L["gu_u"], L["gu_f"]
    S.fetch_a(("d", 1), ("d", 2))
    S.fetch_b_own("d")
    o_mine, o_next = L.o
    o_pair = jnp.where(g.u == 0, jnp.stack([o_mine, o_next]), jnp.stack([o_next, o_mine]))
    o_pair = o_pair.transpose(1, 2, 0, 3, 4)
    w_o_all = swap_halves(g, pick(o_pair, g.c), g.pc(pick(o_pair, 1 - g.c)))
    w_o_all = w_o_all.transpose(1, 2, 0, 3, 4).reshape(-1, width)
    rows, pieces = S.columns("qkv")
    *saved, att = attend(rows, pieces, *L.xn, L.cosines, L.sines, L.mask, gain_query, gain_key)
    L.part = project_out(att, w_o_all)
    done()

    L.part = core_sum(*L.part)
    for k in range(PARTS):
        pieces = [x[:, 2 * pw * k : 2 * pw * (k + 1)] for x in L.gu]
        S.fetch(f"gu{k + 1}", pairs(pieces), jnp.stack(pieces))
    del L["gu"]
    S.fetch_a(("gu1", 0))
    S.fetch_b(("d", 0, True), ("d", 1, True))
    done()

    L.part = scatter_one(g, chip_blocks(L.part))
    S.fetch_a(("gu1", 1))
    S.fetch_b(("d", 2, True))
    S.fetch_b_own("gu1")
    L.cot = gather_two_along_t(g, L.cot)
    done()
    L.part = scatter_two(g, L.part)
    S.fetch_a(("gu2", 0))
    S.fetch_b(("gu1", 0, True), ("gu1", 1, True))
    cot_near = jnp.concatenate(L.cot)
    L.cot = (cot_near, g.pc(cot_near))
    d_blocks = S.rows("d").reshape(A, 2, B // 2, rows_d // 2, width).transpose(1, 0, 2, 3, 4)
    L.d = (pick(d_blocks, g.c), pick(d_blocks, 1 - g.c))
    done()

    mid = x_own + add_all(L.part)
    xn2_own, post_back = jax.vjp(rms_scale, mid, g_post)
    L.xn2 = gather_one(g, xn2_own.astype(BF16))
    S.fetch_a(("gu2", 1))
    S.fetch_b_own("gu2")
    L.d = (L.d[0], g.pc(L.d[1]))
    done()
    L.xn2 = gather_two(g, L.xn2)
    S.fetch_a(("gu3", 0))
    S.fetch_b(("gu2", 0, True), ("gu2", 1, True))
    w_d_all = swap_halves(g, *L.d)
    L.w_d_all = w_d_all.transpose(1, 2, 0, 3, 4).reshape(-1, width)
    done()

    near = jnp.concatenate(L.xn2)
    L.xn2 = (near, g.pc(near))
    S.fetch_a(("gu3", 1))
    S.fetch_b_own("gu3")
    done()
    w_d_all = L.w_d_all

    rows_out = S.total_rows()

    def feed_part(part, before):
        name = f"gu{part + 1}"
        rows, pieces = S.columns(name)
        w_d_part = w_d_all[part * pw : (part + 1) * pw]
        hid, grad_d, grads, rest = feed(
            g, rows, rows_out, pieces, *L.xn2, *L.cot, w_d_part, before, part == PARTS - 1
        )
        S.total_split(name, grads)
        return (hid, grad_d), rest

    S.fetch_b(("gu3", 0, True), ("gu3", 1, True))
    L.one, L.rest = feed_part(0, ())
    done()

    S.total_b(("gu1", 0))
    S.prepare_a(("gu1", 0))
    L.two, L.rest = feed_part(1, L.rest)
    done()

    S.total_b(("gu1", 1))
    S.prepare_a(("gu1", 1))
    S.total_a(("gu1", 0))
    L.three, L.part = feed_part(2, L.rest)
    done()

    L.part = core_sum(*L.part)
    S.total_b(("gu2", 0))
    S.prepare_a(("gu2", 0))
    S.total_a(("gu1", 1))
    grad_d = jnp.concatenate([L.one[1], L.two[1], L.three[1]])
    grad_d = grad_d.reshape(A, B // 2, 2, rows_d // 2, width)
    grad_d = grad_d.transpose(2, 0, 1, 3, 4)
    L.d = (pick(grad_d, g.c), pick(grad_d, 1 - g.c))
    done()

    L.part = scatter_one(g, chip_blocks(L.part))
    S.total_b(("gu2", 1))
    S.prepare_a(("gu2", 1))
    S.total_a(("gu2", 0))
    S.finish("gu1")
    L.d = (L.d[0], g.pc(L.d[1]))
    L.hidden = jnp.concatenate([L.one[0], L.two[0], L.three[0]], axis=1)
    done()
    L.part = scatter_two(g, L.part)
    S.total_b(("gu3", 0))
    S.prepare_a(("gu3", 0))
    S.total_a(("gu2", 1))
    grad_d = swap_halves(g, *L.d).transpose(1, 0, 2, 3, 4).reshape(A, B, rows_d // 2, width)
    S.total("d", [grad_d[:, :, k * third : (k + 1) * third] for k in range(3)])
    L.out = project_out(L.hidden, w_d_all)
    done()

    d_post, grad_post = post_back(add_all(L.part))
    d_mid = cotangent[0].astype(F32) + d_post
    L.dmb = gather_one(g, d_mid.astype(BF16))
    S.total_b(("gu3", 1))
    S.prepare_a(("gu3", 1))
    S.total_a(("gu3", 0))
    S.finish("gu2")
    done()
    L.dmb = gather_two(g, L.dmb)
    S.total_b(("d", 0))
    S.prepare_a(("d", 0))
    S.total_a(("gu3", 1))
    L.out = core_sum(*L.out)
    done()

    near = jnp.concatenate(L.dmb)
    L.dmb = (near, g.pc(near))
    S.total_b(("d", 1))
    S.prepare_a(("d", 1))
    S.total_a(("d", 0))
    S.finish("gu3")
    out = chip_blocks(L.out)
    L.out = scatter_one(g, out)
    grads = [columns_pieces(g, L[f"gu{k + 1}"]) for k in range(PARTS)]
    L.gu = [jnp.concatenate(x, axis=1) for x in zip(*grads)]
    done()

    S.total_b(("d", 2))
    S.prepare_a(("d", 2))
    S.total_a(("d", 1))
    L.gu = chips_swap(g, L.gu)
    own, sent, grad_o, head_gains, grad_in, *grads = attend_back(
        g, rows_out, *L.dmb, w_o_all, att, saved, L.cosines, L.sines, gain_query, gain_key, *L.xn,
        rows_in,
    )
    L.part = (own, sent)
    L.gains = jnp.concatenate([grad_in[0] / g_in, grad_post, head_gains.reshape(-1)])
    grad_o = grad_o.reshape(Q, 2, rows_o, width).transpose(1, 0, 2, 3)
    L.o = (pick(grad_o, g.u), pick(grad_o, 1 - g.u))
    S.total_split("qkv", grads)
    done()

    L.part = core_sum(*L.part)
    S.total_b(("qkv", 0))
    S.prepare_a(("qkv", 0))
    S.total_a(("d", 2))
    L.o = (L.o[0], g.px(L.o[1], g.umask))
    own, to_u, to_t, relayed = L.out
    L.out = (own, to_u, g.pt((to_t + relayed.astype(F32)).astype(BF16), 1, 0))
    L.gains = L.gains + g.pc(L.gains)
    done()

    L.part = scatter_one(g, chip_blocks(L.part))
    S.total_b(("qkv", 1))
    S.total_a(("qkv", 0))
    S.finish("d")
    mine, other = L.o
    grad_o = jnp.where(g.u == 0, jnp.stack([mine, other]), jnp.stack([other, mine]))
    grad_o = grad_o.reshape(2, Q, 2, rows_o // 2, width).transpose(2, 0, 1, 3, 4)
    grad_o = swap_halves(g, pick(grad_o, g.c), g.pc(pick(grad_o, 1 - g.c)))
    grad_o = grad_o.transpose(1, 0, 2, 3, 4).reshape(A, B, rows_o // 2, width)
    S.total("o", [grad_o])
    S.prepare_a(("qkv", 1))
    bits = int(math.log2(g.n))
    for bit in range(bits // 2):
        L.gains = L.gains + g.px(L.gains, 1 << bit)
    done()
    L.part = scatter_two(g, L.part)
    for bit in range(bits // 2, bits - 1):
        L.gains = L.gains + g.px(L.gains, 1 << bit)
    S.total_b(("o", 0))
    S.total_a(("qkv", 1))
    S.prepare_a(("o", 0))
    S.finish("qkv")
    L.gu = (L.gu, g.pc(jnp.stack(L.gu)))
    d_sum = jnp.concatenate([L.d[k] for k in range(3)])
    L.d = d_sum
    done()

    def both_cores(pair):
        near, far = pair
        return list(near) + [far[k] for k in range(4)]

    pieces, places = both_cores(L.gu), []
    for part in range(PARTS):
        for j, piece in enumerate(pieces):
            dt, du = ORDER[j % 4]
            at = 2 * pw * part
            for to, w in hidden_cuts(g.t ^ dt, g.u ^ du, g.c ^ (j // 4), part):
                places += [
                    (j, at, w, 0, to),
                    (j, pw + at, w, 1, to),
                ]
                at += w
    L.gate, L.up = place_columns(pieces, [hidden_width, hidden_width], places)
    S.total_a(("o", 0))
    L.qkv = chips_swap(g, columns_pieces(g, L.qkv))
    own, to_u, from_t = L.out
    L.out = (own, g.pt(to_u.astype(BF16), 0, 1), from_t)
    _, in_back = jax.vjp(lambda x: rms_scale(x, g_in), x_own)
    L.d_tokens = (d_mid + in_back(add_all(L.part))[0]).astype(BF16)
    done("out")

    L.d = swap_halves(g, L.d, g.pc(L.d)).reshape(1, rows_d, width).astype(F32)
    gains = (L.gains + g.px(L.gains, 1 << (bits - 1)))[None]
    S.finish("o")
    L.qkv = (L.qkv, g.pc(jnp.stack(L.qkv)))
    grad_output = swap_halves(g, L.o[0], g.pc(L.o[0])).reshape(1, rows_o, width).astype(F32)
    activations = (mid + add_all(L.out)).astype(BF16)
    d_tokens = L.d_tokens

    pieces = both_cores(L.qkv)
    places = []
    for j, piece in enumerate(pieces):
        dt, du = ORDER[j % 4]
        kv = g.kv_head(g.t ^ dt, g.u ^ du, g.c ^ (j // 4), rows_o)
        places += [
            (j, 0, hd2, 0, kv * hd2),
            (j, hd2, HD, 1, kv * HD),
            (j, hd2 + HD, HD, 2, kv * HD),
        ]
    grad_query, grad_key, grad_value = place_columns(pieces, [q_width, kv_width, kv_width], places)

    return (
        activations[None],
        d_tokens[None],
        grad_query[None],
        grad_key[None],
        grad_value[None],
        grad_output,
        L.gate[None],
        L.up[None],
        L.d,
        gains[:, :width],
        gains[:, 2 * width : 2 * width + HD],
        gains[:, 2 * width + HD :],
        gains[:, width : 2 * width],
    )


def solution(mesh):
    rows = P("fsdp", "rep", None)
    cut_rows = P(None, "fsdp", None)
    return jax.shard_map(
        functools.partial(per_device, Grid(mesh)),
        mesh=mesh,
        in_specs=(rows, P("fsdp", None), rows) + (cut_rows,) * 7 + (P(),) * 4,
        out_specs=(rows, rows) + (cut_rows,) * 7 + (P(),) * 4,
        check_vma=False,
    )
```
